32 devices in a mesh: dp: 8 (over y, x, core), seq: 4 (over z).
Axes of the slice: x: 2, y: 2, z: 4, core: 2. Of those that a mesh axis runs over, the one named last changes fastest.
Arguments:
- tokens: bfloat16 [8, 512, 1024], P('dp', 'seq'), may hold values from -6 to 6
- positions: int32 [8, 512], P('dp', 'seq'), may hold values from 0 to 4095
- counts: int32 [8, 4], P('dp'), may hold values from 1 to 128, 384 in all within a row
- ln_gain: float32 [1024], replicated, may hold values from 0.1 to 1.9
- w_qkv: bfloat16 [3, 1024, 1024], replicated
- w_out: bfloat16 [1024, 1024], replicated, may hold values from -0.1875 to 0.1875
- d_out: bfloat16 [8, 512, 1024], P('dp', 'seq'), may hold values from -6 to 6
Outputs:
- d_tokens: bfloat16 [8, 512, 1024], P('dp', 'seq')
- grad_qkv: float32 [3, 1024, 1024], P(None, 'seq', 'dp')
- grad_out: float32 [1024, 1024], P('dp', 'seq')
The draws below stay inside these ranges and needn't reach their ends.
Inputs may be any that keep to these rules, and one draw needn't show every extreme that they name: Each record's counts sum to 384, and the largest of them is 128.
All inputs are finite; a program needn't handle non-finite values.
Results may differ from the reference program's by a relative error of at most 0.0075.
Values may be sent and summed in bfloat16 or wider, within the bound.
No kernel may reach another device: no remote copies, remote signals or barrier semaphores. Data moves between devices by JAX's collectives and lax.ppermute only.
A program may use at most 128 MiB of HBM per device.

```python
import math
import jax
import jax.numpy as jnp
import numpy as np
from jax import lax

D = 1024
HEADS = 16
HEAD_DIM = 64
CAP = 128
NPOS = 4096
SLOTS = 512
VIS = 384
BATCH = 8
N_SEQ = 4


def draw_w_qkv(key, part):
    base = jax.random.normal(jax.random.fold_in(key, 11), (3, D, D), jnp.float32) * D ** (-0.5)
    return base.astype(jnp.bfloat16)


def with_ends(values, own_key, low, high):
    extent = values.shape
    spot = [jax.random.randint(jax.random.fold_in(own_key, axis), (), 0, extent[axis]) for axis in range(len(extent))]
    values = values.at[tuple(spot)].set(low)
    longest = extent.index(max(extent))
    spot[longest] = (spot[longest] + 1) % extent[longest]
    return values.at[tuple(spot)].set(high)


def shard_levels(stream_key, extent, split, least, largest):
    loudness = 1.0
    for dim, shards_of in split:
        heights = jax.random.uniform(jax.random.fold_in(jax.random.fold_in(stream_key, 6), dim), (shards_of,), jnp.float32, least / len(split), largest / len(split))
        loudness = loudness * jnp.repeat(jnp.exp(heights), extent[dim] // shards_of).reshape((-1,) + (1,) * (len(extent) - 1 - dim))
    return loudness


def profile(number_of, total, bound, skew):
    loads = [(1 << 20) // math.isqrt(rank ** skew) + 1 for rank in range(2, number_of + 1)]
    spare, holding = total - bound - (number_of - 1), [1] * (number_of - 1)
    while spare > 0:
        candidates = [i for i in range(number_of - 1) if holding[i] < bound]
        whole, budget = sum([loads[i] for i in candidates]), spare
        for i in candidates:
            more = min(bound - holding[i], max(1, budget * loads[i] // whole), spare)
            holding[i] = holding[i] + more
            spare = spare - more
    return np.array([bound] + holding)


def ragged_sizes(rng, amount, total, most, lean):
    if amount == 2:
        one = jax.random.randint(rng, (), max(1, total - most), min(most, total - 1) + 1)
        return jnp.stack([one, total - one])
    sizes = jnp.asarray(profile(amount, total, most, lean), jnp.int32)
    twos = (amount - 1) // 2
    donor, receiver = sizes[1:1 + 2 * twos:2], sizes[2:2 + 2 * twos:2]
    room = jnp.minimum(donor - 1, most - receiver)
    moved = jax.random.randint(jax.random.fold_in(rng, 1), (twos,), 0, 1 << 20) % (room + 1)
    sizes = sizes.at[1:1 + 2 * twos:2].set(donor - moved).at[2:2 + 2 * twos:2].set(receiver + moved)
    return sizes[jax.random.permutation(jax.random.fold_in(rng, 2), amount)]


def noise(own_key, dims, width, most, split=(), held_as=jnp.bfloat16):
    gain = shard_levels(own_key, dims, split, -0.22, 0.18) if split else 1.0
    entries = jax.random.normal(own_key, dims, jnp.float32) * width * gain
    return jnp.minimum(jnp.maximum(entries, -most), most).astype(held_as)


def setup_inputs(seed: int = 0) -> dict:
    arg_keys = jax.random.split(jax.random.key(seed), 8)
    tokens = noise(arg_keys[0], (BATCH, SLOTS, D), 1.0, 6.0, ((0, 8), (1, 4)))
    positions = with_ends(jax.random.randint(arg_keys[1], (BATCH, SLOTS), 0, NPOS), jax.random.fold_in(arg_keys[1], 1), 0, NPOS - 1).astype(jnp.int32)
    counts = jax.vmap(lambda own: ragged_sizes(own, N_SEQ, VIS, CAP, 2))(jax.random.split(arg_keys[2], BATCH)).reshape((BATCH, N_SEQ)).astype(jnp.int32)
    ln_gain = jnp.clip(1.0 + 0.18 * jax.random.normal(arg_keys[3], (D,), jnp.float32), 0.1, 1.9)
    w_qkv = draw_w_qkv(jax.random.fold_in(arg_keys[7], 71), 0)
    w_out = noise(arg_keys[5], (D, D), D ** -0.5, 0.1875)
    d_out = noise(arg_keys[6], (BATCH, SLOTS, D), 1.0, 6.0, ((0, 8), (1, 4)))
    return {"tokens": tokens, "positions": positions, "counts": counts, "ln_gain": ln_gain, "w_qkv": w_qkv, "w_out": w_out, "d_out": d_out}


EPSILON = 1e-06
MASKED = -1e+30

def position_code(places, feature_width):
    half = feature_width // 2
    freqs = jnp.exp(jnp.arange(half, dtype=jnp.float32) * (-math.log(10000.0) / half))
    angle = places.astype(jnp.float32)[:, None] * freqs[None, :]
    return jnp.concatenate([jnp.sin(angle), jnp.cos(angle)], axis=1)

def layer_norm(inputs, places, ln_gain):
    shifted = inputs.astype(jnp.float32) + position_code(places, inputs.shape[1])
    centred = shifted - lax.optimization_barrier(jnp.mean(shifted, axis=1, keepdims=True))
    inv_std = lax.rsqrt(lax.optimization_barrier(jnp.mean(centred * centred, axis=1, keepdims=True)) + EPSILON)
    standard = centred * inv_std
    normed = (standard * ln_gain.astype(jnp.float32)).astype(jnp.bfloat16)
    return (normed, standard, inv_std)

def input_grad(query_grad, key_grad, value_grad, masked_grad, w_qkv, standard, inv_std, ln_gain):
    normed_grad = jnp.dot(query_grad, w_qkv[0], preferred_element_type=jnp.float32)
    normed_grad = normed_grad + jnp.dot(key_grad, w_qkv[1], preferred_element_type=jnp.float32)
    normed_grad = normed_grad + jnp.dot(value_grad, w_qkv[2], preferred_element_type=jnp.float32)
    unit_grad = normed_grad * ln_gain.astype(jnp.float32)
    inner = unit_grad - lax.optimization_barrier(jnp.mean(unit_grad, axis=1, keepdims=True))
    inner = inner - standard * lax.optimization_barrier(jnp.mean(unit_grad * standard, axis=1, keepdims=True))
    return (masked_grad.astype(jnp.float32) + inv_std * inner).astype(jnp.bfloat16)

def head_attention(queries, key_rows, value_rows, attn_grad, key_valid, score_scale):
    scores = jnp.dot(queries, key_rows.T, preferred_element_type=jnp.float32) * score_scale
    scores = jnp.where(key_valid[None, :], scores, MASKED)
    peak = lax.optimization_barrier(jnp.max(scores, axis=1, keepdims=True))
    expo = jnp.exp(scores - peak)
    probs = expo / lax.optimization_barrier(jnp.sum(expo, axis=1, keepdims=True))
    probs_low = probs.astype(jnp.bfloat16)
    attended = jnp.dot(probs_low, value_rows, preferred_element_type=jnp.float32)
    delta = lax.optimization_barrier(jnp.sum(attn_grad.astype(jnp.float32) * attended, axis=1))
    prob_grad = jnp.dot(attn_grad, value_rows.T, preferred_element_type=jnp.float32)
    score_grad = (probs * (prob_grad - delta[:, None])).astype(jnp.bfloat16)
    query_grad = (jnp.dot(score_grad, key_rows, preferred_element_type=jnp.float32) * score_scale).astype(jnp.bfloat16)
    key_grad = (jnp.dot(score_grad.T, queries, preferred_element_type=jnp.float32) * score_scale).astype(jnp.bfloat16)
    value_grad = jnp.dot(probs_low.T, attn_grad, preferred_element_type=jnp.float32).astype(jnp.bfloat16)
    return (attended.astype(jnp.bfloat16), query_grad, key_grad, value_grad)

def reference(tokens, positions, counts, ln_gain, w_qkv, w_out, d_out):
    score_scale = HEAD_DIM ** (-0.5)
    slot_index = jnp.arange(SLOTS, dtype=jnp.int32)

    def split_heads(array):
        return array.reshape(SLOTS, HEADS, HEAD_DIM).transpose(1, 0, 2)

    def join_heads(array):
        return array.transpose(1, 0, 2).reshape(SLOTS, D)

    def project(normed, weight):
        return jnp.dot(normed, weight.T, preferred_element_type=jnp.float32).astype(jnp.bfloat16)

    def one_record(carry, item):
        inputs, places, shard_counts, upstream = item
        valid = slot_index % CAP < jnp.repeat(shard_counts, CAP)
        normed, standard, inv_std = layer_norm(inputs, places, ln_gain)
        masked_grad = jnp.where(valid[:, None], upstream, jnp.zeros_like(upstream))
        queries = project(normed, w_qkv[0])
        key_rows = project(normed, w_qkv[1])
        value_rows = project(normed, w_qkv[2])
        attn_grad = jnp.dot(masked_grad, w_out, preferred_element_type=jnp.float32).astype(jnp.bfloat16)

        def per_head(parts):
            return head_attention(parts[0], parts[1], parts[2], parts[3], valid, score_scale)
        results = lax.map(per_head, (split_heads(queries), split_heads(key_rows), split_heads(value_rows), split_heads(attn_grad)))
        attended = join_heads(results[0])
        query_grad = join_heads(results[1])
        key_grad = join_heads(results[2])
        value_grad = join_heads(results[3])
        d_inputs = input_grad(query_grad, key_grad, value_grad, masked_grad, w_qkv, standard, inv_std, ln_gain)
        term_qkv = jnp.stack([jnp.dot(query_grad.T, normed, preferred_element_type=jnp.float32), jnp.dot(key_grad.T, normed, preferred_element_type=jnp.float32), jnp.dot(value_grad.T, normed, preferred_element_type=jnp.float32)])
        term_out = jnp.dot(masked_grad.T, attended, preferred_element_type=jnp.float32)
        return ((carry[0] + term_qkv, carry[1] + term_out), d_inputs)
    start = (jnp.zeros((3, D, D), jnp.float32), jnp.zeros((D, D), jnp.float32))
    sums, d_tokens = lax.scan(one_record, start, (tokens, positions, counts, d_out))
    factor = 1.0 / math.sqrt(BATCH * VIS)
    return (d_tokens, sums[0] * factor, sums[1] * factor)
```

```python
import math

import jax
import jax.numpy as jnp
from jax import lax
from jax.experimental import pallas as pl
from jax.experimental.pallas import tpu as pltpu
from jax.sharding import PartitionSpec as P

HEAD_DIM = 64


EPSILON = 1e-06
MASKED = -1e30


def position_code(places, feature_width):
    half = feature_width // 2
    freqs = jnp.exp(jnp.arange(half, dtype=jnp.float32) * (-math.log(10000.0) / half))
    angle = places.astype(jnp.float32)[:, None] * freqs[None, :]
    return jnp.concatenate([jnp.sin(angle), jnp.cos(angle)], axis=1)


def layer_norm(inputs, places, ln_gain):
    shifted = inputs.astype(jnp.float32) + position_code(places, inputs.shape[1])
    centred = shifted - jnp.mean(shifted, axis=1, keepdims=True)
    inv_std = lax.rsqrt(jnp.mean(centred * centred, axis=1, keepdims=True) + EPSILON)
    standard = centred * inv_std
    normed = (standard * ln_gain).astype(jnp.bfloat16)
    return (normed, standard, inv_std)


def input_grad(query_grad, key_grad, value_grad, masked_grad, w_qkv, standard, inv_std, ln_gain):
    normed_grad = jnp.dot(query_grad, w_qkv[0], preferred_element_type=jnp.float32)
    normed_grad = normed_grad + jnp.dot(key_grad, w_qkv[1], preferred_element_type=jnp.float32)
    normed_grad = normed_grad + jnp.dot(value_grad, w_qkv[2], preferred_element_type=jnp.float32)
    unit_grad = normed_grad * ln_gain
    inner = unit_grad - jnp.mean(unit_grad, axis=1, keepdims=True)
    inner = inner - standard * jnp.mean(unit_grad * standard, axis=1, keepdims=True)
    return (masked_grad.astype(jnp.float32) + inv_std * inner).astype(jnp.bfloat16)


def project(normed, weight):
    return jnp.einsum("td,od->to", normed, weight, preferred_element_type=jnp.float32).astype(
        jnp.bfloat16
    )


def token_sum(left, right):
    return lax.dot_general(
        left, right, (((0,), (0,)), ((), ())), preferred_element_type=jnp.float32
    )


def attention_grads(queries, key_rows, value_rows, attn_grad, key_valid, score_scale):
    total, span = queries.shape
    heads_here = span // HEAD_DIM
    block = math.gcd(512, total)
    blocks = total // block
    key_three = key_rows.reshape(total, heads_here, HEAD_DIM)
    value_three = value_rows.reshape(total, heads_here, HEAD_DIM)
    query_four = queries.reshape(blocks, block, heads_here, HEAD_DIM)
    grad_four = attn_grad.reshape(blocks, block, heads_here, HEAD_DIM)

    def step(carry, item):
        key_acc, value_acc = carry
        query_block, grad_block = item
        scores = (
            jnp.einsum("qhd,khd->hqk", query_block, key_three, preferred_element_type=jnp.float32)
            * score_scale
        )
        scores = jnp.where(key_valid[None, None, :], scores, MASKED)
        peak = jnp.max(scores, axis=2, keepdims=True)
        expo = jnp.exp(scores - peak)
        probs = expo / jnp.sum(expo, axis=2, keepdims=True)
        probs_low = probs.astype(jnp.bfloat16)
        attended = jnp.einsum(
            "hqk,khd->qhd", probs_low, value_three, preferred_element_type=jnp.float32
        )
        delta = jnp.sum(grad_block.astype(jnp.float32) * attended, axis=2)
        prob_grad = jnp.einsum(
            "qhd,khd->hqk", grad_block, value_three, preferred_element_type=jnp.float32
        )
        score_grad = (probs * (prob_grad - jnp.transpose(delta)[:, :, None])).astype(jnp.bfloat16)
        query_grad = jnp.einsum(
            "hqk,khd->qhd", score_grad, key_three, preferred_element_type=jnp.float32
        )
        query_grad = (query_grad * score_scale).astype(jnp.bfloat16)
        key_acc = key_acc + jnp.einsum(
            "hqk,qhd->khd", score_grad, query_block, preferred_element_type=jnp.float32
        )
        value_acc = value_acc + jnp.einsum(
            "hqk,qhd->khd", probs_low, grad_block, preferred_element_type=jnp.float32
        )
        return ((key_acc, value_acc), (attended.astype(jnp.bfloat16), query_grad))

    zeros_acc = jnp.zeros((total, heads_here, HEAD_DIM), jnp.float32)
    sums, outputs = lax.scan(step, (zeros_acc, zeros_acc), (query_four, grad_four))
    attended = outputs[0].reshape(total, span)
    query_grad = outputs[1].reshape(total, span)
    key_grad = (sums[0] * score_scale).astype(jnp.bfloat16).reshape(total, span)
    value_grad = sums[1].astype(jnp.bfloat16).reshape(total, span)
    return (attended, query_grad, key_grad, value_grad)


def shards(tokens, positions, counts, ln_gain, w_qkv, w_out, d_out):
    inputs = tokens[0]
    places = positions[0]
    upstream = d_out[0]
    capacity, feature_width = inputs.shape
    shard_total = lax.axis_size("seq")
    shard_index = lax.axis_index("seq")
    slot_count = capacity * shard_total
    key_valid = jnp.arange(slot_count, dtype=jnp.int32) % capacity < jnp.repeat(counts[0], capacity)
    own_valid = lax.dynamic_slice_in_dim(key_valid, shard_index * capacity, capacity)
    normed, standard, inv_std = layer_norm(inputs, places, ln_gain)
    masked_grad = jnp.where(own_valid[:, None], upstream, jnp.zeros_like(upstream))
    score_scale = HEAD_DIM ** (-0.5)
    factor = 1.0 / math.sqrt(lax.axis_size("dp") * (3 * slot_count // 4))
    head_width = feature_width // shard_total
    normed_all, grad_all = (
        lax.all_gather(normed, "seq", axis=0, tiled=True),
        lax.all_gather(masked_grad, "seq", axis=0, tiled=True),
    )
    local_qkv = lax.dynamic_slice_in_dim(w_qkv, shard_index * head_width, head_width, 1)
    local_out = lax.dynamic_slice_in_dim(w_out, shard_index * head_width, head_width, 1)
    queries = project(normed_all, local_qkv[0])
    key_rows = project(normed_all, local_qkv[1])
    value_rows = project(normed_all, local_qkv[2])
    attn_grad = jnp.dot(grad_all, local_out, preferred_element_type=jnp.float32).astype(
        jnp.bfloat16
    )
    attended, query_grad, key_grad, value_grad = attention_grads(
        queries, key_rows, value_rows, attn_grad, key_valid, score_scale
    )
    term_qkv = jnp.stack(
        [
            token_sum(query_grad, normed_all),
            token_sum(key_grad, normed_all),
            token_sum(value_grad, normed_all),
        ]
    )
    term_out = token_sum(grad_all, attended)
    grad_qkv, grad_out = (
        lax.psum_scatter(term_qkv, "dp", scatter_dimension=2, tiled=True),
        lax.psum_scatter(term_out, "dp", scatter_dimension=0, tiled=True),
    )
    query_rows, key_back, value_back = (
        lax.all_to_all(query_grad, "seq", split_axis=0, concat_axis=1, tiled=True),
        lax.all_to_all(key_grad, "seq", split_axis=0, concat_axis=1, tiled=True),
        lax.all_to_all(value_grad, "seq", split_axis=0, concat_axis=1, tiled=True),
    )
    d_inputs = input_grad(
        query_rows, key_back, value_back, masked_grad, w_qkv, standard, inv_std, ln_gain
    )
    return (d_inputs[None], grad_qkv * factor, grad_out * factor)


FIRST_MOVES = (
    ((0, 0), (2, 0)),
    ((1, 0), (0, 0)),
    ((2, 0), (0, 1)),
    ((3, 0), (2, 1)),
    ((0, 1), (1, 0)),
    ((1, 1), (3, 1)),
    ((2, 1), (3, 0)),
    ((3, 1), (1, 1)),
)
SECOND_MOVES = (
    ((0, 1), (3, 0)),
    ((3, 0), (0, 1)),
    ((1, 0), (2, 1)),
    ((2, 1), (1, 0)),
)
SWAP_MOVES = (
    ((0, 1), (1, 0)),
    ((1, 0), (0, 1)),
    ((2, 1), (3, 0)),
    ((3, 0), (2, 1)),
)


def column_pairs(moves, chips, seqs, back=False):
    pairs = []
    for chip in range(chips):
        for source, target in moves:
            if back:
                source, target = target, source
            pairs.append(
                ((chip * 2 + source[1]) * seqs + source[0], (chip * 2 + target[1]) * seqs + target[0])
            )
    return pairs


def block_table():
    table = [[0, 0] for _ in range(8)]
    for (source, _), (target, core) in FIRST_MOVES:
        table[target * 2 + core][0] = source
        table[target * 2 + core][1] = target
    for (source, _), (target, core) in SECOND_MOVES:
        table[target * 2 + core][1] = source
    return table


def nt(left, right):
    return lax.dot_general(left, right, (((1,), (1,)), ((), ())), preferred_element_type=jnp.float32)


def nn(left, right):
    return lax.dot_general(left, right, (((1,), (0,)), ((), ())), preferred_element_type=jnp.float32)


def tn(left, right):
    return lax.dot_general(left, right, (((0,), (0,)), ((), ())), preferred_element_type=jnp.float32)


def attention_kernel(
    sizes, here_t, there_t, here_g, there_g, w_qkv, w_out,
    grads, attended, normed_keep, normed_send,
    query, key, value, lifted, query_sum, key_sum, value_sum, attended_sum,
):
    half, _ = here_t.shape
    total = 2 * half
    width = w_out.shape[1]
    capacity = half // 2
    low = jnp.bfloat16
    scale = HEAD_DIM ** (-0.5)

    def row_ok(part):
        row = lax.broadcasted_iota(jnp.int32, (half, 1), 0)
        first, second = sizes[2 * part], sizes[2 * part + 1]
        return row < jnp.where(row < capacity, first, second + capacity)

    for part, (rows_t, rows_g) in enumerate(((here_t, here_g), (there_t, there_g))):
        span = pl.ds(part * half, half)
        rows = rows_t[...]
        query[span, :] = (nt(rows, w_qkv[0:width, :]).astype(low) * scale).astype(low)
        key[span, :] = nt(rows, w_qkv[width : 2 * width, :]).astype(low)
        value[span, :] = nt(rows, w_qkv[2 * width : 3 * width, :]).astype(low)
        up = nn(rows_g[...], w_out[...])
        lifted[span, :] = jnp.where(row_ok(part), up, 0.0).astype(low)

    column = lax.broadcasted_iota(jnp.int32, (1, total), 1)
    block = column // capacity
    limit = jnp.where(
        block == 0, sizes[0], jnp.where(block == 1, sizes[1], jnp.where(block == 2, sizes[2], sizes[3]))
    )
    bias = jnp.where(column - block * capacity < limit, 0.0, MASKED)
    lane = lax.broadcasted_iota(jnp.int32, (1, width), 1) // HEAD_DIM

    key_sum[...] = jnp.zeros_like(key_sum)
    value_sum[...] = jnp.zeros_like(value_sum)
    query_sum[...] = jnp.zeros_like(query_sum)
    attended_sum[...] = jnp.zeros_like(attended_sum)

    def head_step(head, carry):
        mine = lane == head
        zero = jnp.zeros((), low)
        key_h = jnp.where(mine, key[...], zero)
        value_h = jnp.where(mine, value[...], zero)
        for part in range(2):
            span = pl.ds(part * half, half)
            query_h = jnp.where(mine, query[span, :], zero)
            lifted_h = jnp.where(mine, lifted[span, :], zero)
            scores = nt(query_h, key[...]) + bias
            expo = jnp.exp(scores - jnp.max(scores, axis=1, keepdims=True))
            probs = expo * (1.0 / jnp.sum(expo, axis=1, keepdims=True))
            probs_low = probs.astype(low)
            attended_h = nn(probs_low, value_h)
            attended_sum[span, :] += attended_h
            delta = jnp.sum(lifted_h.astype(jnp.float32) * attended_h, axis=1, keepdims=True)
            score_grad = (probs * (nt(lifted_h, value[...]) - delta)).astype(low)
            query_sum[span, :] += nn(score_grad, key_h)
            key_sum[...] += tn(score_grad, query_h)
            value_sum[...] += tn(probs_low, lifted_h)
        return carry

    lax.fori_loop(0, width // HEAD_DIM, head_step, 0)

    grads[:, 0:width] = (query_sum[...] * scale).astype(low)
    grads[:, width : 2 * width] = key_sum[...].astype(low)
    grads[:, 2 * width : 3 * width] = value_sum[...].astype(low)
    for part in range(2):
        span = pl.ds(part * half, half)
        attended[span, :] = jnp.where(row_ok(part), attended_sum[span, :], 0.0).astype(low)
    normed_keep[...] = nn(grads[0:half, :], w_qkv[...])
    normed_send[...] = nn(grads[half:total, :], w_qkv[...]).astype(low)


def weight_kernel(
    place, here_t, there_t, here_g, there_g, grads, attended, x_keep, x_send, y_keep, y_send
):
    half, _ = here_t.shape
    total = 2 * half
    width = attended.shape[1]
    lanes = width // 2
    for slot_y in range(2):
        for slot_x in range(2):
            block = (place[0] ^ slot_y) * 2 + (place[1] ^ slot_x)
            cols = pl.ds(pl.multiple_of(block * width, width), width)
            for rows, target, index in (
                (0, x_keep if slot_x == 0 else x_send, slot_y),
                (1, y_keep if slot_y == 0 else y_send, slot_x),
            ):
                low, high = rows * 2 * width, (rows + 1) * 2 * width if rows == 0 else 3 * width
                term = tn(grads[0:half, low:high], here_t[:, cols])
                term = term + tn(grads[half:total, low:high], there_t[:, cols])
                term = term.astype(target.dtype)
                for core in range(2):
                    target[index, core, 0 : high - low, :] = term[:, core * lanes : (core + 1) * lanes]
                if rows == 1:
                    term = tn(here_g[:, cols], attended[0:half, :])
                    term = term + tn(there_g[:, cols], attended[half:total, :])
                    term = term.astype(target.dtype)
                    for core in range(2):
                        for side in range(2):
                            target[index, core, pl.ds(width + side * lanes, lanes), :] = term[
                                core * lanes : (core + 1) * lanes, side * lanes : (side + 1) * lanes
                            ]


def vmem(count):
    return [pl.BlockSpec(memory_space=pltpu.VMEM)] * count


def column_shards(tokens, positions, counts, ln_gain, w_qkv, w_out, d_out):
    low, wide = jnp.bfloat16, jnp.float32
    inputs = tokens[0]
    upstream = d_out[0]
    capacity, features = inputs.shape
    seqs = lax.axis_size("seq")
    chips = lax.axis_size("dp") // 2
    seat = lax.axis_index("seq")
    dp = lax.axis_index("dp")
    core, place_x, place_y = dp % 2, (dp // 2) % 2, dp // 4
    half, total = 2 * capacity, 4 * capacity
    width = features // seqs
    lanes = width // 2
    factor = 1.0 / math.sqrt(lax.axis_size("dp") * (3 * total // 4))
    resident = core == seat % 2

    axes = ("dp", "seq")
    first = column_pairs(FIRST_MOVES, chips, seqs)
    second = column_pairs(SECOND_MOVES, chips, seqs)
    first_back = column_pairs(FIRST_MOVES, chips, seqs, True)
    swap = column_pairs(SWAP_MOVES, chips, seqs)

    def across(array, bit):
        return lax.ppermute(array, "dp", [(i, i ^ bit) for i in range(2 * chips)])

    def share(array):
        from_first = lax.ppermute(array, axes, first)
        from_second = lax.ppermute(array, axes, second)
        here = jnp.concatenate([from_first, jnp.where(resident, array, from_second)], axis=0)
        return here, across(here, 1)

    here_g, there_g = share(upstream)
    normed, standard, inv_std = layer_norm(inputs, positions[0], ln_gain)
    here_t, there_t = share(normed)

    other_counts = across(counts[0], 1)
    sizes = jnp.where(resident, counts[0], other_counts)
    table = jnp.array(block_table(), jnp.int32)
    order = jnp.concatenate([table[seat * 2 + core], table[seat * 2 + 1 - core]])
    sizes = sizes[order]

    group = (seat // 2) * 2 + core
    own_qkv = lax.dynamic_slice_in_dim(w_qkv, group * width, width, 1).reshape(3 * width, features)
    own_out = lax.dynamic_slice_in_dim(w_out, group * width, width, 1)

    smem = pl.BlockSpec(memory_space=pltpu.SMEM)
    grads, attended, normed_keep, normed_send = pl.pallas_call(
        attention_kernel,
        out_shape=(
            jax.ShapeDtypeStruct((total, 3 * width), low),
            jax.ShapeDtypeStruct((total, width), low),
            jax.ShapeDtypeStruct((half, features), wide),
            jax.ShapeDtypeStruct((half, features), low),
        ),
        in_specs=[smem] + vmem(6),
        out_specs=vmem(4),
        scratch_shapes=[pltpu.VMEM((total, width), low)] * 4 + [pltpu.VMEM((total, width), wide)] * 4,
        compiler_params=pltpu.CompilerParams(vmem_limit_bytes=48 * 1024 * 1024),
        cost_estimate=pl.CostEstimate(
            flops=2 * total * features * width * 7 + 12 * 4 * total * total * width,
            bytes_accessed=8 * 1024 * 1024,
            transcendentals=4 * total * total,
        ),
    )(sizes, here_t, there_t, here_g, there_g, own_qkv, own_out)

    place = jnp.stack([place_y, place_x]).astype(jnp.int32)
    x_keep, x_send, y_keep, y_send = pl.pallas_call(
        weight_kernel,
        out_shape=(
            jax.ShapeDtypeStruct((2, 2, 2 * width, lanes), wide),
            jax.ShapeDtypeStruct((2, 2, 2 * width, lanes), low),
            jax.ShapeDtypeStruct((2, 2, 2 * width, lanes), wide),
            jax.ShapeDtypeStruct((2, 2, 2 * width, lanes), low),
        ),
        in_specs=[smem] + vmem(6),
        out_specs=vmem(4),
        compiler_params=pltpu.CompilerParams(vmem_limit_bytes=48 * 1024 * 1024),
        cost_estimate=pl.CostEstimate(
            flops=2 * total * features * width * 4, bytes_accessed=10 * 1024 * 1024, transcendentals=0
        ),
    )(place, here_t, there_t, here_g, there_g, grads, attended)

    x_part = x_keep + across(x_send, 2).astype(wide)
    y_part = y_keep + across(y_send, 4).astype(wide)
    x_part = x_part[0] + across(x_part[1].astype(low), 4).astype(wide)
    y_part = y_part[0] + across(y_part[1].astype(low), 2).astype(wide)
    sums = jnp.concatenate([x_part, y_part], axis=1)
    swapped = lax.ppermute(sums.astype(low), axes, swap)
    sums = jnp.where(resident, sums, swapped.astype(wide))
    kept = lax.dynamic_index_in_dim(sums, core, 0, False)
    given = lax.dynamic_index_in_dim(sums, 1 - core, 0, False)
    final = (kept + across(given, 1)) * factor
    grad_qkv = final[: 3 * width].reshape(3, width, lanes)
    grad_out = jnp.concatenate([final[3 * width : 3 * width + lanes], final[3 * width + lanes :]], axis=1)

    back = normed_keep + across(normed_send, 1).astype(wide)
    from_first = lax.ppermute(back[:capacity].astype(low), axes, first_back)
    from_second = lax.ppermute(back[capacity:].astype(low), axes, second)
    normed_grad = from_first.astype(wide) + jnp.where(
        resident, back[capacity:], from_second.astype(wide)
    )
    own_valid = jnp.arange(capacity, dtype=jnp.int32) < lax.dynamic_index_in_dim(counts[0], seat, 0, False)
    masked_grad = jnp.where(own_valid[:, None], upstream, jnp.zeros_like(upstream))
    unit_grad = normed_grad * ln_gain
    inner = unit_grad - jnp.mean(unit_grad, axis=1, keepdims=True)
    inner = inner - standard * jnp.mean(unit_grad * standard, axis=1, keepdims=True)
    d_inputs = (masked_grad.astype(wide) + inv_std * inner).astype(low)
    return (d_inputs[None], grad_qkv, grad_out)


def solution(mesh):
    fits = mesh.shape["dp"] == 8 and mesh.shape["seq"] == 4
    placed = (
        P("dp", "seq", None),
        P("dp", "seq"),
        P("dp", None),
        P(),
        P(),
        P(),
        P("dp", "seq", None),
    )
    return jax.shard_map(
        column_shards if fits else shards,
        mesh=mesh,
        in_specs=placed,
        out_specs=(P("dp", "seq", None), P(None, "seq", "dp"), P("dp", "seq")),
        check_vma=False,
    )
```

```python
import math

import jax
import jax.numpy as jnp
from jax import lax
from jax.experimental import pallas as pl
from jax.experimental.pallas import tpu as pltpu
from jax.sharding import PartitionSpec as P

HEAD_DIM = 64


EPSILON = 1e-06
MASKED = -1e30


def position_code(places, feature_width):
    half = feature_width // 2
    freqs = jnp.exp(jnp.arange(half, dtype=jnp.float32) * (-math.log(10000.0) / half))
    angle = places.astype(jnp.float32)[:, None] * freqs[None, :]
    return jnp.concatenate([jnp.sin(angle), jnp.cos(angle)], axis=1)


def layer_norm(inputs, places, ln_gain):
    shifted = inputs.astype(jnp.float32) + position_code(places, inputs.shape[1])
    centred = shifted - jnp.mean(shifted, axis=1, keepdims=True)
    inv_std = lax.rsqrt(jnp.mean(centred * centred, axis=1, keepdims=True) + EPSILON)
    standard = centred * inv_std
    normed = (standard * ln_gain).astype(jnp.bfloat16)
    return (normed, standard, inv_std)


def input_grad(query_grad, key_grad, value_grad, masked_grad, w_qkv, standard, inv_std, ln_gain):
    normed_grad = jnp.dot(query_grad, w_qkv[0], preferred_element_type=jnp.float32)
    normed_grad = normed_grad + jnp.dot(key_grad, w_qkv[1], preferred_element_type=jnp.float32)
    normed_grad = normed_grad + jnp.dot(value_grad, w_qkv[2], preferred_element_type=jnp.float32)
    unit_grad = normed_grad * ln_gain
    inner = unit_grad - jnp.mean(unit_grad, axis=1, keepdims=True)
    inner = inner - standard * jnp.mean(unit_grad * standard, axis=1, keepdims=True)
    return (masked_grad.astype(jnp.float32) + inv_std * inner).astype(jnp.bfloat16)


def project(normed, weight):
    return jnp.einsum("td,od->to", normed, weight, preferred_element_type=jnp.float32).astype(
        jnp.bfloat16
    )


def token_sum(left, right):
    return lax.dot_general(
        left, right, (((0,), (0,)), ((), ())), preferred_element_type=jnp.float32
    )


def attention_grads(queries, key_rows, value_rows, attn_grad, key_valid, score_scale):
    total, span = queries.shape
    heads_here = span // HEAD_DIM
    block = math.gcd(512, total)
    blocks = total // block
    key_three = key_rows.reshape(total, heads_here, HEAD_DIM)
    value_three = value_rows.reshape(total, heads_here, HEAD_DIM)
    query_four = queries.reshape(blocks, block, heads_here, HEAD_DIM)
    grad_four = attn_grad.reshape(blocks, block, heads_here, HEAD_DIM)

    def step(carry, item):
        key_acc, value_acc = carry
        query_block, grad_block = item
        scores = (
            jnp.einsum("qhd,khd->hqk", query_block, key_three, preferred_element_type=jnp.float32)
            * score_scale
        )
        scores = jnp.where(key_valid[None, None, :], scores, MASKED)
        peak = jnp.max(scores, axis=2, keepdims=True)
        expo = jnp.exp(scores - peak)
        probs = expo / jnp.sum(expo, axis=2, keepdims=True)
        probs_low = probs.astype(jnp.bfloat16)
        attended = jnp.einsum(
            "hqk,khd->qhd", probs_low, value_three, preferred_element_type=jnp.float32
        )
        delta = jnp.sum(grad_block.astype(jnp.float32) * attended, axis=2)
        prob_grad = jnp.einsum(
            "qhd,khd->hqk", grad_block, value_three, preferred_element_type=jnp.float32
        )
        score_grad = (probs * (prob_grad - jnp.transpose(delta)[:, :, None])).astype(jnp.bfloat16)
        query_grad = jnp.einsum(
            "hqk,khd->qhd", score_grad, key_three, preferred_element_type=jnp.float32
        )
        query_grad = (query_grad * score_scale).astype(jnp.bfloat16)
        key_acc = key_acc + jnp.einsum(
            "hqk,qhd->khd", score_grad, query_block, preferred_element_type=jnp.float32
        )
        value_acc = value_acc + jnp.einsum(
            "hqk,qhd->khd", probs_low, grad_block, preferred_element_type=jnp.float32
        )
        return ((key_acc, value_acc), (attended.astype(jnp.bfloat16), query_grad))

    zeros_acc = jnp.zeros((total, heads_here, HEAD_DIM), jnp.float32)
    sums, outputs = lax.scan(step, (zeros_acc, zeros_acc), (query_four, grad_four))
    attended = outputs[0].reshape(total, span)
    query_grad = outputs[1].reshape(total, span)
    key_grad = (sums[0] * score_scale).astype(jnp.bfloat16).reshape(total, span)
    value_grad = sums[1].astype(jnp.bfloat16).reshape(total, span)
    return (attended, query_grad, key_grad, value_grad)


def shards(tokens, positions, counts, ln_gain, w_qkv, w_out, d_out):
    inputs = tokens[0]
    places = positions[0]
    upstream = d_out[0]
    capacity, feature_width = inputs.shape
    shard_total = lax.axis_size("seq")
    shard_index = lax.axis_index("seq")
    slot_count = capacity * shard_total
    key_valid = jnp.arange(slot_count, dtype=jnp.int32) % capacity < jnp.repeat(counts[0], capacity)
    own_valid = lax.dynamic_slice_in_dim(key_valid, shard_index * capacity, capacity)
    normed, standard, inv_std = layer_norm(inputs, places, ln_gain)
    masked_grad = jnp.where(own_valid[:, None], upstream, jnp.zeros_like(upstream))
    score_scale = HEAD_DIM ** (-0.5)
    factor = 1.0 / math.sqrt(lax.axis_size("dp") * (3 * slot_count // 4))
    head_width = feature_width // shard_total
    normed_all, grad_all = (
        lax.all_gather(normed, "seq", axis=0, tiled=True),
        lax.all_gather(masked_grad, "seq", axis=0, tiled=True),
    )
    local_qkv = lax.dynamic_slice_in_dim(w_qkv, shard_index * head_width, head_width, 1)
    local_out = lax.dynamic_slice_in_dim(w_out, shard_index * head_width, head_width, 1)
    queries = project(normed_all, local_qkv[0])
    key_rows = project(normed_all, local_qkv[1])
    value_rows = project(normed_all, local_qkv[2])
    attn_grad = jnp.dot(grad_all, local_out, preferred_element_type=jnp.float32).astype(
        jnp.bfloat16
    )
    attended, query_grad, key_grad, value_grad = attention_grads(
        queries, key_rows, value_rows, attn_grad, key_valid, score_scale
    )
    term_qkv = jnp.stack(
        [
            token_sum(query_grad, normed_all),
            token_sum(key_grad, normed_all),
            token_sum(value_grad, normed_all),
        ]
    )
    term_out = token_sum(grad_all, attended)
    grad_qkv, grad_out = (
        lax.psum_scatter(term_qkv, "dp", scatter_dimension=2, tiled=True),
        lax.psum_scatter(term_out, "dp", scatter_dimension=0, tiled=True),
    )
    query_rows, key_back, value_back = (
        lax.all_to_all(query_grad, "seq", split_axis=0, concat_axis=1, tiled=True),
        lax.all_to_all(key_grad, "seq", split_axis=0, concat_axis=1, tiled=True),
        lax.all_to_all(value_grad, "seq", split_axis=0, concat_axis=1, tiled=True),
    )
    d_inputs = input_grad(
        query_rows, key_back, value_back, masked_grad, w_qkv, standard, inv_std, ln_gain
    )
    return (d_inputs[None], grad_qkv * factor, grad_out * factor)


FIRST_MOVES = (
    ((0, 0), (2, 0)),
    ((1, 0), (0, 0)),
    ((2, 0), (0, 1)),
    ((3, 0), (2, 1)),
    ((0, 1), (1, 0)),
    ((1, 1), (3, 1)),
    ((2, 1), (3, 0)),
    ((3, 1), (1, 1)),
)
SECOND_MOVES = (
    ((0, 1), (3, 0)),
    ((3, 0), (0, 1)),
    ((1, 0), (2, 1)),
    ((2, 1), (1, 0)),
    ((0, 0), (0, 0)),
    ((1, 1), (1, 1)),
    ((2, 0), (2, 0)),
    ((3, 1), (3, 1)),
)
HOME_MOVES = (
    ((0, 0), (0, 1)),
    ((1, 1), (1, 0)),
    ((1, 0), (0, 0)),
    ((0, 1), (1, 1)),
    ((2, 0), (2, 1)),
    ((3, 1), (3, 0)),
    ((3, 0), (2, 0)),
    ((2, 1), (3, 1)),
)
GUEST_MOVES = (
    ((1, 0), (0, 1)),
    ((0, 1), (1, 0)),
    ((3, 0), (2, 1)),
    ((2, 1), (3, 0)),
)


def column_pairs(moves, chips, seqs, back=False):
    pairs = []
    for chip in range(chips):
        for source, target in moves:
            if back:
                source, target = target, source
            pairs.append(
                ((chip * 2 + source[1]) * seqs + source[0], (chip * 2 + target[1]) * seqs + target[0])
            )
    return pairs


def block_table():
    table = [[0, 0] for _ in range(8)]
    for place, moves in enumerate((FIRST_MOVES, SECOND_MOVES)):
        for (source, _), (target, core) in moves:
            table[target * 2 + core][place] = source
    return table


def nt(left, right):
    return lax.dot_general(left, right, (((1,), (1,)), ((), ())), preferred_element_type=jnp.float32)


def nn(left, right):
    return lax.dot_general(left, right, (((1,), (0,)), ((), ())), preferred_element_type=jnp.float32)


def tn(left, right):
    return lax.dot_general(left, right, (((0,), (0,)), ((), ())), preferred_element_type=jnp.float32)


def valid_slots(info, capacity, axis, total):
    shape = (total, 1) if axis == 0 else (1, total)
    slot = lax.broadcasted_iota(jnp.int32, shape, axis)
    limit = info[0] + jnp.zeros(shape, jnp.int32)
    for block in range(1, total // capacity):
        limit = jnp.where(slot >= block * capacity, block * capacity + info[block], limit)
    return slot < limit


def lift_kernel(info, g0, g1, g2, g3, w_out, lifted, rows, weight, sems):
    capacity = g0.shape[0]
    width = lifted.shape[0]
    total = lifted.shape[1]
    copies = [
        pltpu.make_async_copy(
            w_out.at[:, pl.ds(pl.multiple_of(info[4] * width, width), width)], weight, sems.at[4]
        )
    ]
    for block, source in enumerate((g0, g1, g2, g3)):
        copies.append(
            pltpu.make_async_copy(source, rows.at[pl.ds(block * capacity, capacity), :], sems.at[block])
        )
    for copy in copies:
        copy.start()
    for copy in copies:
        copy.wait()
    up = nn(rows[...], weight[...])
    up = jnp.where(valid_slots(info, capacity, 0, total), up, 0.0)
    lifted[...] = up.T.astype(lifted.dtype)


def main_kernel(
    info, t0, t1, t2, t3, g0, g1, g2, g3, lifted_in, w_qkv,
    x_send, x_keep, y_send, y_keep, grads,
    rows_t, rows_g, weight, lifted, query, key, value, stack,
    x_send_buf, x_keep_buf, y_send_buf, y_keep_buf, in_sems, out_sems,
):
    capacity = t0.shape[0]
    total = rows_t.shape[0]
    width = lifted.shape[0]
    lanes = width // 2
    low = jnp.bfloat16
    scale = HEAD_DIM ** (-0.5)

    loads = []
    for block, source in enumerate((t0, t1, t2, t3)):
        loads.append(
            pltpu.make_async_copy(
                source, rows_t.at[pl.ds(block * capacity, capacity), :], in_sems.at[block]
            )
        )
    group = pl.multiple_of(info[4] * width, width)
    for part in range(3):
        loads.append(
            pltpu.make_async_copy(
                w_qkv.at[part, pl.ds(group, width), :],
                weight.at[pl.ds(part * width, width), :],
                in_sems.at[4 + part],
            )
        )
    loads.append(pltpu.make_async_copy(lifted_in, lifted, in_sems.at[7]))
    for block, source in enumerate((g0, g1, g2, g3)):
        loads.append(
            pltpu.make_async_copy(
                source, rows_g.at[pl.ds(block * capacity, capacity), :], in_sems.at[8 + block]
            )
        )
    for copy in loads:
        copy.start()
    for copy in loads[:5]:
        copy.wait()
    query[...] = (nt(weight[0:width, :], rows_t[...]).astype(low) * scale).astype(low)
    loads[5].wait()
    key[...] = nt(weight[width : 2 * width, :], rows_t[...]).astype(low)
    loads[6].wait()
    value[...] = nt(weight[2 * width : 3 * width, :], rows_t[...]).astype(low)
    loads[7].wait()

    bias = jnp.where(valid_slots(info, capacity, 0, total), 0.0, MASKED)
    row_ok = valid_slots(info, capacity, 1, total)
    for head in range(width // HEAD_DIM):
        span = pl.ds(head * HEAD_DIM, HEAD_DIM)
        query_h, key_h, value_h, lifted_h = query[span, :], key[span, :], value[span, :], lifted[span, :]
        scores = tn(key_h, query_h) + bias
        expo = jnp.exp(scores - jnp.max(scores, axis=0, keepdims=True))
        probs = expo * (1.0 / jnp.sum(expo, axis=0, keepdims=True))
        probs_low = probs.astype(low)
        attended = nn(value_h, probs_low)
        delta = jnp.sum(lifted_h.astype(jnp.float32) * attended, axis=0, keepdims=True)
        score_grad = (probs * (tn(value_h, lifted_h) - delta)).astype(low)
        stack[pl.ds(head * HEAD_DIM, HEAD_DIM), :] = (nn(key_h, score_grad) * scale).astype(low)
        stack[pl.ds(width + head * HEAD_DIM, HEAD_DIM), :] = nt(query_h, score_grad).astype(low)
        stack[pl.ds(2 * width + head * HEAD_DIM, HEAD_DIM), :] = nt(lifted_h, probs_low).astype(low)
        stack[pl.ds(3 * width + head * HEAD_DIM, HEAD_DIM), :] = jnp.where(
            row_ok, attended, 0.0
        ).astype(low)

    stores = [
        pltpu.make_async_copy(stack.at[pl.ds(0, 3 * width), :], grads, out_sems.at[0]),
        pltpu.make_async_copy(x_send_buf, x_send, out_sems.at[1]),
        pltpu.make_async_copy(y_send_buf, y_send, out_sems.at[2]),
        pltpu.make_async_copy(x_keep_buf, x_keep, out_sems.at[3]),
        pltpu.make_async_copy(y_keep_buf, y_keep, out_sems.at[4]),
    ]
    stores[0].start()
    for copy in loads[8:]:
        copy.wait()
    for slot_y, slot_x in ((1, 1), (0, 1), (1, 0), (0, 0)):
        block = (info[5] ^ slot_y) * 2 + (info[6] ^ slot_x)
        cols = pl.ds(pl.multiple_of(block * width, width), width)
        term_t = nn(stack[0 : 3 * width, :], rows_t[:, cols])
        term_g = nn(stack[3 * width : 4 * width, :], rows_g[:, cols])
        x_target = x_send_buf if slot_x else x_keep_buf
        y_target = y_send_buf if slot_y else y_keep_buf
        for side in range(2):
            across = slice(side * lanes, (side + 1) * lanes)
            spot = info[7] ^ side
            x_target[slot_y, spot, :, :] = term_t[0 : 2 * width, across].astype(x_target.dtype)
            y_target[slot_x, spot, 0:width, :] = term_t[2 * width : 3 * width, across].astype(y_target.dtype)
            y_target[slot_x, spot, width : 2 * width, :] = term_g[:, across].astype(y_target.dtype)
        if (slot_y, slot_x) == (0, 1):
            stores[1].start()
        if (slot_y, slot_x) == (1, 0):
            stores[2].start()
    stores[3].start()
    stores[4].start()
    for copy in stores:
        copy.wait()


def normed_kernel(info, grads_in, w_qkv, keep, send, grads, weight, sems):
    features = w_qkv.shape[2]
    total = grads.shape[1]
    width = grads.shape[0] // 3
    group = pl.multiple_of(info[4] * width, width)
    loads = [pltpu.make_async_copy(grads_in, grads, sems.at[3])]
    for part in range(3):
        loads.append(
            pltpu.make_async_copy(
                w_qkv.at[part, pl.ds(group, width), :],
                weight.at[pl.ds(part * width, width), :],
                sems.at[part],
            )
        )
    for copy in loads:
        copy.start()
    for copy in loads:
        copy.wait()
    send[...] = tn(grads[:, total // 2 : total], weight[...]).astype(send.dtype)
    keep[...] = tn(grads[:, 0 : total // 2], weight[...])


def specs(space, count):
    return [pl.BlockSpec(memory_space=space)] * count


VMEM_BYTES = 56 * 1024 * 1024


def column_shards(tokens, positions, counts, ln_gain, w_qkv, w_out, d_out):
    low, wide = jnp.bfloat16, jnp.float32
    inputs = tokens[0]
    upstream = d_out[0]
    capacity, features = inputs.shape
    seqs = lax.axis_size("seq")
    chips = lax.axis_size("dp") // 2
    seat = lax.axis_index("seq")
    dp = lax.axis_index("dp")
    core, place_x, place_y = dp & 1, (dp >> 1) & 1, dp >> 2
    total = seqs * capacity
    half = total // 2
    width = features // seqs
    lanes = width // 2
    factor = 1.0 / math.sqrt(lax.axis_size("dp") * (3 * total // 4))
    guest = core ^ (seat & 1)
    resident = guest == 0

    axes = ("dp", "seq")
    first = column_pairs(FIRST_MOVES, chips, seqs)
    second = column_pairs(SECOND_MOVES, chips, seqs)
    first_back = column_pairs(FIRST_MOVES, chips, seqs, True)
    home = column_pairs(HOME_MOVES, chips, seqs)
    guests = column_pairs(GUEST_MOVES, chips, seqs)

    def across(array, bit):
        return lax.ppermute(array, "dp", [(i, i ^ bit) for i in range(2 * chips)])

    def share(array):
        one = lax.ppermute(array, axes, first)
        two = lax.ppermute(array, axes, second)
        return one, two, across(one, 1), across(two, 1)

    blocks_g = share(upstream)
    other_counts = across(counts[0], 1)
    normed, standard, inv_std = layer_norm(inputs, positions[0], ln_gain)
    blocks_t = share(normed)

    sizes = jnp.where(resident, counts[0], other_counts)
    table = jnp.array(block_table(), jnp.int32)
    order = jnp.concatenate([table[seat * 2 + core], table[seat * 2 + 1 - core]])
    group = (seat >> 1) * 2 + core
    info = jnp.concatenate(
        [sizes[order], jnp.stack([group, place_y, place_x, core ^ 1 ^ guest]).astype(jnp.int32)]
    )

    params = pltpu.CompilerParams(vmem_limit_bytes=VMEM_BYTES)
    smem = specs(pltpu.SMEM, 1)
    lifted = pl.pallas_call(
        lift_kernel,
        out_shape=jax.ShapeDtypeStruct((width, total), low),
        in_specs=smem + specs(pltpu.HBM, 5),
        out_specs=pl.BlockSpec(memory_space=pltpu.VMEM),
        scratch_shapes=[
            pltpu.VMEM((total, features), low),
            pltpu.VMEM((features, width), low),
            pltpu.SemaphoreType.DMA((5,)),
        ],
        compiler_params=params,
        cost_estimate=pl.CostEstimate(
            flops=2 * total * features * width, bytes_accessed=2 * 1024 * 1024, transcendentals=0
        ),
    )(info, *blocks_g, w_out)

    send_shape = jax.ShapeDtypeStruct((2, 2, 2 * width, lanes), low)
    keep_shape = jax.ShapeDtypeStruct((2, 2, 2 * width, lanes), wide)
    x_send, x_keep, y_send, y_keep, grads = pl.pallas_call(
        main_kernel,
        out_shape=(
            send_shape, keep_shape, send_shape, keep_shape, jax.ShapeDtypeStruct((3 * width, total), low)
        ),
        in_specs=smem + specs(pltpu.HBM, 10),
        out_specs=specs(pltpu.HBM, 5),
        scratch_shapes=[
            pltpu.VMEM((total, features), low),
            pltpu.VMEM((total, features), low),
            pltpu.VMEM((3 * width, features), low),
            pltpu.VMEM((width, total), low),
            pltpu.VMEM((width, total), low),
            pltpu.VMEM((width, total), low),
            pltpu.VMEM((width, total), low),
            pltpu.VMEM((4 * width, total), low),
            pltpu.VMEM(send_shape.shape, low),
            pltpu.VMEM(send_shape.shape, wide),
            pltpu.VMEM(send_shape.shape, low),
            pltpu.VMEM(send_shape.shape, wide),
            pltpu.SemaphoreType.DMA((12,)),
            pltpu.SemaphoreType.DMA((5,)),
        ],
        compiler_params=params,
        cost_estimate=pl.CostEstimate(
            flops=2 * total * features * width * 7 + 12 * 4 * total * total * HEAD_DIM,
            bytes_accessed=8 * 1024 * 1024,
            transcendentals=4 * total * total,
        ),
    )(info, *blocks_t, *blocks_g, lifted, w_qkv)

    normed_keep, normed_send = pl.pallas_call(
        normed_kernel,
        out_shape=(
            jax.ShapeDtypeStruct((half, features), wide),
            jax.ShapeDtypeStruct((half, features), low),
        ),
        in_specs=smem + specs(pltpu.HBM, 2),
        out_specs=specs(pltpu.VMEM, 2),
        scratch_shapes=[
            pltpu.VMEM((3 * width, total), low),
            pltpu.VMEM((3 * width, features), low),
            pltpu.SemaphoreType.DMA((4,)),
        ],
        compiler_params=params,
        cost_estimate=pl.CostEstimate(
            flops=2 * total * features * width * 3, bytes_accessed=4 * 1024 * 1024, transcendentals=0
        ),
    )(info, grads, w_qkv)

    x_first, y_first = across(x_send, 2), across(y_send, 4)
    shared = across(normed_send, 1)
    back_one = (normed_keep[:capacity] + shared[:capacity].astype(wide)).astype(low)
    back_two = (normed_keep[capacity:] + shared[capacity:].astype(wide)).astype(low)
    normed_grad = lax.ppermute(back_one, axes, first_back).astype(wide)
    normed_grad = normed_grad + lax.ppermute(back_two, axes, second).astype(wide)

    x_second = across((x_keep[1] + x_first[1].astype(wide)).astype(low), 4)
    y_second = across((y_keep[1] + y_first[1].astype(wide)).astype(low), 2)
    x_part = x_keep[0] + x_first[0].astype(wide) + x_second.astype(wide)
    y_part = y_keep[0] + y_first[0].astype(wide) + y_second.astype(wide)
    sums = jnp.concatenate([x_part, y_part], axis=1)
    from_home = lax.ppermute(sums[0].astype(low), axes, home)
    from_guest = lax.ppermute(sums[1].astype(low), axes, guests)
    final = from_home.astype(wide) + jnp.where(resident, sums[1], from_guest.astype(wide))
    final = final * factor
    grad_qkv = final[: 3 * width].reshape(3, width, lanes)
    grad_out = final[3 * width :].T

    own_valid = jnp.arange(capacity, dtype=jnp.int32) < lax.dynamic_index_in_dim(counts[0], seat, 0, False)
    masked_grad = jnp.where(own_valid[:, None], upstream, jnp.zeros_like(upstream))
    unit_grad = normed_grad * ln_gain
    inner = unit_grad - jnp.mean(unit_grad, axis=1, keepdims=True)
    inner = inner - standard * jnp.mean(unit_grad * standard, axis=1, keepdims=True)
    d_inputs = (masked_grad.astype(wide) + inv_std * inner).astype(low)
    return (d_inputs[None], grad_qkv, grad_out)


def solution(mesh):
    fits = mesh.shape["dp"] == 8 and mesh.shape["seq"] == 4
    placed = (
        P("dp", "seq", None),
        P("dp", "seq"),
        P("dp", None),
        P(),
        P(),
        P(),
        P("dp", "seq", None),
    )
    return jax.shard_map(
        column_shards if fits else shards,
        mesh=mesh,
        in_specs=placed,
        out_specs=(P("dp", "seq", None), P(None, "seq", "dp"), P("dp", "seq")),
        check_vma=False,
    )
```

```python
import math

import jax
import jax.numpy as jnp
from jax import lax
from jax.experimental import pallas as pl
from jax.experimental.pallas import tpu as pltpu
from jax.sharding import PartitionSpec as P

HEAD_DIM = 64


EPSILON = 1e-06
MASKED = -1e30


def position_code(places, feature_width):
    half = feature_width // 2
    freqs = jnp.exp(jnp.arange(half, dtype=jnp.float32) * (-math.log(10000.0) / half))
    angle = places.astype(jnp.float32)[:, None] * freqs[None, :]
    return jnp.concatenate([jnp.sin(angle), jnp.cos(angle)], axis=1)


def layer_norm(inputs, places, ln_gain):
    shifted = inputs.astype(jnp.float32) + position_code(places, inputs.shape[1])
    centred = shifted - jnp.mean(shifted, axis=1, keepdims=True)
    inv_std = lax.rsqrt(jnp.mean(centred * centred, axis=1, keepdims=True) + EPSILON)
    standard = centred * inv_std
    normed = (standard * ln_gain).astype(jnp.bfloat16)
    return (normed, standard, inv_std)


def input_grad(query_grad, key_grad, value_grad, masked_grad, w_qkv, standard, inv_std, ln_gain):
    normed_grad = jnp.dot(query_grad, w_qkv[0], preferred_element_type=jnp.float32)
    normed_grad = normed_grad + jnp.dot(key_grad, w_qkv[1], preferred_element_type=jnp.float32)
    normed_grad = normed_grad + jnp.dot(value_grad, w_qkv[2], preferred_element_type=jnp.float32)
    unit_grad = normed_grad * ln_gain
    inner = unit_grad - jnp.mean(unit_grad, axis=1, keepdims=True)
    inner = inner - standard * jnp.mean(unit_grad * standard, axis=1, keepdims=True)
    return (masked_grad.astype(jnp.float32) + inv_std * inner).astype(jnp.bfloat16)


def project(normed, weight):
    return jnp.einsum("td,od->to", normed, weight, preferred_element_type=jnp.float32).astype(
        jnp.bfloat16
    )


def token_sum(left, right):
    return lax.dot_general(
        left, right, (((0,), (0,)), ((), ())), preferred_element_type=jnp.float32
    )


def attention_grads(queries, key_rows, value_rows, attn_grad, key_valid, score_scale):
    total, span = queries.shape
    heads_here = span // HEAD_DIM
    block = math.gcd(512, total)
    blocks = total // block
    key_three = key_rows.reshape(total, heads_here, HEAD_DIM)
    value_three = value_rows.reshape(total, heads_here, HEAD_DIM)
    query_four = queries.reshape(blocks, block, heads_here, HEAD_DIM)
    grad_four = attn_grad.reshape(blocks, block, heads_here, HEAD_DIM)

    def step(carry, item):
        key_acc, value_acc = carry
        query_block, grad_block = item
        scores = (
            jnp.einsum("qhd,khd->hqk", query_block, key_three, preferred_element_type=jnp.float32)
            * score_scale
        )
        scores = jnp.where(key_valid[None, None, :], scores, MASKED)
        peak = jnp.max(scores, axis=2, keepdims=True)
        expo = jnp.exp(scores - peak)
        probs = expo / jnp.sum(expo, axis=2, keepdims=True)
        probs_low = probs.astype(jnp.bfloat16)
        attended = jnp.einsum(
            "hqk,khd->qhd", probs_low, value_three, preferred_element_type=jnp.float32
        )
        delta = jnp.sum(grad_block.astype(jnp.float32) * attended, axis=2)
        prob_grad = jnp.einsum(
            "qhd,khd->hqk", grad_block, value_three, preferred_element_type=jnp.float32
        )
        score_grad = (probs * (prob_grad - jnp.transpose(delta)[:, :, None])).astype(jnp.bfloat16)
        query_grad = jnp.einsum(
            "hqk,khd->qhd", score_grad, key_three, preferred_element_type=jnp.float32
        )
        query_grad = (query_grad * score_scale).astype(jnp.bfloat16)
        key_acc = key_acc + jnp.einsum(
            "hqk,qhd->khd", score_grad, query_block, preferred_element_type=jnp.float32
        )
        value_acc = value_acc + jnp.einsum(
            "hqk,qhd->khd", probs_low, grad_block, preferred_element_type=jnp.float32
        )
        return ((key_acc, value_acc), (attended.astype(jnp.bfloat16), query_grad))

    zeros_acc = jnp.zeros((total, heads_here, HEAD_DIM), jnp.float32)
    sums, outputs = lax.scan(step, (zeros_acc, zeros_acc), (query_four, grad_four))
    attended = outputs[0].reshape(total, span)
    query_grad = outputs[1].reshape(total, span)
    key_grad = (sums[0] * score_scale).astype(jnp.bfloat16).reshape(total, span)
    value_grad = sums[1].astype(jnp.bfloat16).reshape(total, span)
    return (attended, query_grad, key_grad, value_grad)


def shards(tokens, positions, counts, ln_gain, w_qkv, w_out, d_out):
    inputs = tokens[0]
    places = positions[0]
    upstream = d_out[0]
    capacity, feature_width = inputs.shape
    shard_total = lax.axis_size("seq")
    shard_index = lax.axis_index("seq")
    slot_count = capacity * shard_total
    key_valid = jnp.arange(slot_count, dtype=jnp.int32) % capacity < jnp.repeat(counts[0], capacity)
    own_valid = lax.dynamic_slice_in_dim(key_valid, shard_index * capacity, capacity)
    normed, standard, inv_std = layer_norm(inputs, places, ln_gain)
    masked_grad = jnp.where(own_valid[:, None], upstream, jnp.zeros_like(upstream))
    score_scale = HEAD_DIM ** (-0.5)
    factor = 1.0 / math.sqrt(lax.axis_size("dp") * (3 * slot_count // 4))
    head_width = feature_width // shard_total
    normed_all, grad_all = (
        lax.all_gather(normed, "seq", axis=0, tiled=True),
        lax.all_gather(masked_grad, "seq", axis=0, tiled=True),
    )
    local_qkv = lax.dynamic_slice_in_dim(w_qkv, shard_index * head_width, head_width, 1)
    local_out = lax.dynamic_slice_in_dim(w_out, shard_index * head_width, head_width, 1)
    queries = project(normed_all, local_qkv[0])
    key_rows = project(normed_all, local_qkv[1])
    value_rows = project(normed_all, local_qkv[2])
    attn_grad = jnp.dot(grad_all, local_out, preferred_element_type=jnp.float32).astype(
        jnp.bfloat16
    )
    attended, query_grad, key_grad, value_grad = attention_grads(
        queries, key_rows, value_rows, attn_grad, key_valid, score_scale
    )
    term_qkv = jnp.stack(
        [
            token_sum(query_grad, normed_all),
            token_sum(key_grad, normed_all),
            token_sum(value_grad, normed_all),
        ]
    )
    term_out = token_sum(grad_all, attended)
    grad_qkv, grad_out = (
        lax.psum_scatter(term_qkv, "dp", scatter_dimension=2, tiled=True),
        lax.psum_scatter(term_out, "dp", scatter_dimension=0, tiled=True),
    )
    query_rows, key_back, value_back = (
        lax.all_to_all(query_grad, "seq", split_axis=0, concat_axis=1, tiled=True),
        lax.all_to_all(key_grad, "seq", split_axis=0, concat_axis=1, tiled=True),
        lax.all_to_all(value_grad, "seq", split_axis=0, concat_axis=1, tiled=True),
    )
    d_inputs = input_grad(
        query_rows, key_back, value_back, masked_grad, w_qkv, standard, inv_std, ln_gain
    )
    return (d_inputs[None], grad_qkv * factor, grad_out * factor)


FIRST_MOVES = (
    ((0, 0), (2, 0)),
    ((1, 0), (0, 0)),
    ((2, 0), (0, 1)),
    ((3, 0), (2, 1)),
    ((0, 1), (1, 0)),
    ((1, 1), (3, 1)),
    ((2, 1), (3, 0)),
    ((3, 1), (1, 1)),
)
SECOND_MOVES = (
    ((0, 1), (3, 0)),
    ((3, 0), (0, 1)),
    ((1, 0), (2, 1)),
    ((2, 1), (1, 0)),
    ((0, 0), (0, 0)),
    ((1, 1), (1, 1)),
    ((2, 0), (2, 0)),
    ((3, 1), (3, 1)),
)
HOME_MOVES = (
    ((0, 0), (0, 1)),
    ((1, 1), (1, 0)),
    ((1, 0), (0, 0)),
    ((0, 1), (1, 1)),
    ((2, 0), (2, 1)),
    ((3, 1), (3, 0)),
    ((3, 0), (2, 0)),
    ((2, 1), (3, 1)),
)
GUEST_MOVES = (
    ((1, 0), (0, 1)),
    ((0, 1), (1, 0)),
    ((3, 0), (2, 1)),
    ((2, 1), (3, 0)),
)


def column_pairs(moves, chips, seqs, back=False):
    pairs = []
    for chip in range(chips):
        for source, target in moves:
            if back:
                source, target = target, source
            pairs.append(
                ((chip * 2 + source[1]) * seqs + source[0], (chip * 2 + target[1]) * seqs + target[0])
            )
    return pairs


def block_table():
    table = [[0, 0] for _ in range(8)]
    for place, moves in enumerate((FIRST_MOVES, SECOND_MOVES)):
        for (source, _), (target, core) in moves:
            table[target * 2 + core][place] = source
    return table


def nt(left, right):
    return lax.dot_general(left, right, (((1,), (1,)), ((), ())), preferred_element_type=jnp.float32)


def nn(left, right):
    return lax.dot_general(left, right, (((1,), (0,)), ((), ())), preferred_element_type=jnp.float32)


def tn(left, right):
    return lax.dot_general(left, right, (((0,), (0,)), ((), ())), preferred_element_type=jnp.float32)


def valid_slots(info, capacity, axis, total):
    shape = (total, 1) if axis == 0 else (1, total)
    slot = lax.broadcasted_iota(jnp.int32, shape, axis)
    limit = info[0] + jnp.zeros(shape, jnp.int32)
    for block in range(1, total // capacity):
        limit = jnp.where(slot >= block * capacity, block * capacity + info[block], limit)
    return slot < limit


def weight_kernel(info, w_out, w_qkv, own_out, own_qkv, sems):
    width = own_out.shape[1]
    group = pl.multiple_of(info[4] * width, width)
    copies = [pltpu.make_async_copy(w_out.at[:, pl.ds(group, width)], own_out, sems.at[3])]
    for part in range(3):
        copies.append(
            pltpu.make_async_copy(
                w_qkv.at[part, pl.ds(group, width), :],
                own_qkv.at[pl.ds(part * width, width), :],
                sems.at[part],
            )
        )
    for copy in copies:
        copy.start()
    for copy in copies:
        copy.wait()


def main_kernel(
    info, t0, t1, t2, t3, g0, g1, g2, g3, weight_out, weight,
    x_send, x_keep, y_send, y_keep, grads_here, grads_there,
    rows_t, rows_g, lifted, query, key, value, stack,
    x_send_buf, x_keep_buf, y_send_buf, y_keep_buf, in_sems, out_sems,
):
    capacity = t0.shape[0]
    total = rows_t.shape[0]
    width = lifted.shape[0]
    lanes = width // 2
    low = jnp.bfloat16
    scale = HEAD_DIM ** (-0.5)

    loads = []
    for block, source in enumerate((t0, t1, t2, t3)):
        loads.append(
            pltpu.make_async_copy(
                source, rows_t.at[pl.ds(block * capacity, capacity), :], in_sems.at[block]
            )
        )
    for block, source in enumerate((g0, g1, g2, g3)):
        loads.append(
            pltpu.make_async_copy(
                source, rows_g.at[pl.ds(block * capacity, capacity), :], in_sems.at[4 + block]
            )
        )
    for copy in loads:
        copy.start()
    for copy in loads[:4]:
        copy.wait()
    query[...] = (nt(weight[0:width, :], rows_t[...]).astype(low) * scale).astype(low)
    key[...] = nt(weight[width : 2 * width, :], rows_t[...]).astype(low)
    value[...] = nt(weight[2 * width : 3 * width, :], rows_t[...]).astype(low)
    for copy in loads[4:]:
        copy.wait()
    up = nn(rows_g[...], weight_out[...])
    up = jnp.where(valid_slots(info, capacity, 0, total), up, 0.0)
    lifted[...] = up.T.astype(low)

    bias = jnp.where(valid_slots(info, capacity, 0, total), 0.0, MASKED)
    row_ok = valid_slots(info, capacity, 1, total)
    for head in range(width // HEAD_DIM):
        span = pl.ds(head * HEAD_DIM, HEAD_DIM)
        query_h, key_h, value_h, lifted_h = query[span, :], key[span, :], value[span, :], lifted[span, :]
        scores = tn(key_h, query_h) + bias
        expo = jnp.exp(scores - jnp.max(scores, axis=0, keepdims=True))
        probs = expo * (1.0 / jnp.sum(expo, axis=0, keepdims=True))
        probs_low = probs.astype(low)
        attended = nn(value_h, probs_low)
        delta = jnp.sum(lifted_h.astype(jnp.float32) * attended, axis=0, keepdims=True)
        score_grad = (probs * (tn(value_h, lifted_h) - delta)).astype(low)
        stack[pl.ds(head * HEAD_DIM, HEAD_DIM), :] = (nn(key_h, score_grad) * scale).astype(low)
        stack[pl.ds(width + head * HEAD_DIM, HEAD_DIM), :] = nt(query_h, score_grad).astype(low)
        stack[pl.ds(2 * width + head * HEAD_DIM, HEAD_DIM), :] = nt(lifted_h, probs_low).astype(low)
        stack[pl.ds(3 * width + head * HEAD_DIM, HEAD_DIM), :] = jnp.where(
            row_ok, attended, 0.0
        ).astype(low)

    stores = [
        pltpu.make_async_copy(
            stack.at[pl.ds(0, 3 * width), pl.ds(part * (total // 2), total // 2)],
            (grads_here, grads_there)[part],
            out_sems.at[part],
        )
        for part in range(2)
    ]
    for copy in stores:
        copy.start()
    for step, (slot_y, slot_x) in enumerate(((0, 0), (1, 0), (0, 1), (1, 1))):
        block = (info[5] ^ slot_y) * 2 + (info[6] ^ slot_x)
        cols = pl.ds(pl.multiple_of(block * width, width), width)
        term_t = nn(stack[0 : 3 * width, :], rows_t[:, cols])
        term_g = nn(stack[3 * width : 4 * width, :], rows_g[:, cols]).T
        x_target, x_out = (x_send_buf, x_send) if slot_x else (x_keep_buf, x_keep)
        y_target, y_out = (y_send_buf, y_send) if slot_y else (y_keep_buf, y_keep)
        for side in range(2):
            across = slice(side * lanes, (side + 1) * lanes)
            spot = info[7] ^ side
            x_target[slot_y, spot, :, :] = term_t[0 : 2 * width, across].astype(x_target.dtype)
            y_target[slot_x, spot, 0:width, :] = term_t[2 * width : 3 * width, across].astype(y_target.dtype)
            for part in range(2):
                y_target[slot_x, spot, width + part * lanes : width + (part + 1) * lanes, :] = term_g[
                    across, part * lanes : (part + 1) * lanes
                ].astype(y_target.dtype)
        for part, (target, out, index) in enumerate(((x_target, x_out, slot_y), (y_target, y_out, slot_x))):
            copy = pltpu.make_async_copy(target.at[index], out.at[index], out_sems.at[2 + 2 * step + part])
            copy.start()
            stores.append(copy)
    for copy in stores:
        copy.wait()


def normed_kernel(info, here, there, w_qkv, back_one, back_two, grads, weight, sems):
    width = here.shape[0] // 3
    capacity = back_one.shape[0]
    first = pl.multiple_of((info[4] >> 1) * 2 * width, 2 * width)
    core = info[4] & 1
    loads = []
    for part in range(3):
        loads.append(
            pltpu.make_async_copy(
                w_qkv.at[part, pl.ds(first, 2 * width), :],
                weight.at[pl.ds(part * 2 * width, 2 * width), :],
                sems.at[part],
            )
        )
        for place, source, spot in ((0, here, core), (1, there, 1 - core)):
            loads.append(
                pltpu.make_async_copy(
                    source.at[pl.ds(part * width, width), :],
                    grads.at[pl.ds(pl.multiple_of((part * 2 + spot) * width, width), width), :],
                    sems.at[3 + part * 2 + place],
                )
            )
    for copy in loads:
        copy.start()
    for copy in loads:
        copy.wait()
    back_one[...] = tn(grads[:, 0:capacity], weight[...]).astype(back_one.dtype)
    back_two[...] = tn(grads[:, capacity : 2 * capacity], weight[...]).astype(back_two.dtype)


def sum_kernel(x_part, y_part, x_second, y_second, home_send, guest_send, own):
    half = x_part.shape[1]
    for rows, part, second in ((0, x_part, x_second), (half, y_part, y_second)):
        span = pl.ds(rows, half)
        home_send[span, :] = (part[0] + second[0].astype(part.dtype)).astype(home_send.dtype)
        total = part[1] + second[1].astype(part.dtype)
        guest_send[span, :] = total.astype(guest_send.dtype)
        own[span, :] = total


def specs(space, count):
    return [pl.BlockSpec(memory_space=space)] * count


VMEM_BYTES = 50 * 1024 * 1024
MAIN_BYTES = 50 * 1024 * 1024


def column_shards(tokens, positions, counts, ln_gain, w_qkv, w_out, d_out):
    low, wide = jnp.bfloat16, jnp.float32
    inputs = tokens[0]
    upstream = d_out[0]
    capacity, features = inputs.shape
    seqs = lax.axis_size("seq")
    chips = lax.axis_size("dp") // 2
    seat = lax.axis_index("seq")
    dp = lax.axis_index("dp")
    core, place_x, place_y = dp & 1, (dp >> 1) & 1, dp >> 2
    total = seqs * capacity
    half = total // 2
    width = features // seqs
    lanes = width // 2
    factor = 1.0 / math.sqrt(lax.axis_size("dp") * (3 * total // 4))
    guest = core ^ (seat & 1)
    resident = guest == 0

    axes = ("dp", "seq")
    first = column_pairs(FIRST_MOVES, chips, seqs)
    second = column_pairs(SECOND_MOVES, chips, seqs)
    first_back = column_pairs(FIRST_MOVES, chips, seqs, True)
    home = column_pairs(HOME_MOVES, chips, seqs)
    guests = column_pairs(GUEST_MOVES, chips, seqs)

    def across(array, bit):
        return lax.ppermute(array, "dp", [(i, i ^ bit) for i in range(2 * chips)])

    def fetch(array):
        return lax.ppermute(array, axes, first), lax.ppermute(array, axes, second)

    def share(pair):
        return pair + (across(pair[0], 1), across(pair[1], 1))

    other_counts = across(counts[0], 1)
    blocks_g = share(fetch(upstream))
    normed, standard, inv_std = layer_norm(inputs, positions[0], ln_gain)
    fetched_t = fetch(normed)

    sizes = jnp.where(resident, counts[0], other_counts)
    table = jnp.array(block_table(), jnp.int32)
    order = jnp.concatenate([table[seat * 2 + core], table[seat * 2 + 1 - core]])
    group = (seat >> 1) * 2 + core
    info = jnp.concatenate(
        [sizes[order], jnp.stack([group, place_y, place_x, core ^ 1 ^ guest]).astype(jnp.int32)]
    )

    params = pltpu.CompilerParams(vmem_limit_bytes=VMEM_BYTES)
    smem = specs(pltpu.SMEM, 1)
    own_out, own_qkv = pl.pallas_call(
        weight_kernel,
        out_shape=(
            jax.ShapeDtypeStruct((features, width), low),
            jax.ShapeDtypeStruct((3 * width, features), low),
        ),
        in_specs=smem + specs(pl.ANY, 2),
        out_specs=specs(pltpu.VMEM, 2),
        scratch_shapes=[pltpu.SemaphoreType.DMA((4,))],
        compiler_params=params,
        cost_estimate=pl.CostEstimate(flops=0, bytes_accessed=4 * 1024 * 1024, transcendentals=0),
    )(info, w_out, w_qkv)
    fetched_t, blocks_g, own_out, own_qkv = lax.optimization_barrier((fetched_t, blocks_g, own_out, own_qkv))
    blocks_t = share(fetched_t)

    send_shape = jax.ShapeDtypeStruct((2, 2, 2 * width, lanes), low)
    keep_shape = jax.ShapeDtypeStruct((2, 2, 2 * width, lanes), wide)
    grads_shape = jax.ShapeDtypeStruct((3 * width, half), low)
    x_send, x_keep, y_send, y_keep, grads_here, grads_there = pl.pallas_call(
        main_kernel,
        out_shape=(
            send_shape, keep_shape, send_shape, keep_shape, grads_shape, grads_shape
        ),
        in_specs=smem + specs(pl.ANY, 8) + specs(pltpu.VMEM, 2),
        out_specs=specs(pltpu.HBM, 6),
        scratch_shapes=[
            pltpu.VMEM((total, features), low),
            pltpu.VMEM((total, features), low),
            pltpu.VMEM((width, total), low),
            pltpu.VMEM((width, total), low),
            pltpu.VMEM((width, total), low),
            pltpu.VMEM((width, total), low),
            pltpu.VMEM((4 * width, total), low),
            pltpu.VMEM(send_shape.shape, low),
            pltpu.VMEM(send_shape.shape, wide),
            pltpu.VMEM(send_shape.shape, low),
            pltpu.VMEM(send_shape.shape, wide),
            pltpu.SemaphoreType.DMA((8,)),
            pltpu.SemaphoreType.DMA((10,)),
        ],
        compiler_params=pltpu.CompilerParams(vmem_limit_bytes=MAIN_BYTES),
        cost_estimate=pl.CostEstimate(
            flops=2 * total * features * width * 7 + 12 * 4 * total * total * HEAD_DIM,
            bytes_accessed=8 * 1024 * 1024,
            transcendentals=4 * total * total,
        ),
    )(info, *blocks_t, *blocks_g, own_out, own_qkv)

    x_first, y_first = across(x_send, 2), across(y_send, 4)
    from_core = across(grads_there, 1)
    block_shape = jax.ShapeDtypeStruct((capacity, features), low)
    back_one, back_two = pl.pallas_call(
        normed_kernel,
        out_shape=(block_shape, block_shape),
        in_specs=smem + specs(pl.ANY, 2) + specs(pltpu.HBM, 1),
        out_specs=specs(pltpu.VMEM, 2),
        scratch_shapes=[
            pltpu.VMEM((6 * width, half), low),
            pltpu.VMEM((6 * width, features), low),
            pltpu.SemaphoreType.DMA((9,)),
        ],
        compiler_params=params,
        cost_estimate=pl.CostEstimate(
            flops=2 * total * features * width * 3, bytes_accessed=4 * 1024 * 1024, transcendentals=0
        ),
    )(info, grads_here, from_core, w_qkv)
    home_one = lax.ppermute(back_one, axes, first_back)
    home_two = lax.ppermute(back_two, axes, second)
    x_second = across((x_keep[1] + x_first[1].astype(wide)).astype(low), 4)
    y_second = across((y_keep[1] + y_first[1].astype(wide)).astype(low), 2)
    x_part = x_keep[0] + x_first[0].astype(wide)
    y_part = y_keep[0] + y_first[0].astype(wide)
    x_part, y_part = lax.optimization_barrier((x_part, y_part))
    home_send, guest_send, own = pl.pallas_call(
        sum_kernel,
        out_shape=(
            jax.ShapeDtypeStruct((4 * width, lanes), low),
            jax.ShapeDtypeStruct((4 * width, lanes), low),
            jax.ShapeDtypeStruct((4 * width, lanes), wide),
        ),
        in_specs=specs(pltpu.VMEM, 4),
        out_specs=specs(pltpu.VMEM, 3),
        compiler_params=pltpu.CompilerParams(vmem_limit_bytes=16 * 1024 * 1024),
        cost_estimate=pl.CostEstimate(flops=4 * width * 2 * lanes, bytes_accessed=2 * 1024 * 1024, transcendentals=0),
    )(x_part, y_part, x_second, y_second)
    from_home = lax.ppermute(home_send, axes, home)
    from_guest = lax.ppermute(guest_send, axes, guests)

    def finish(low_row, high_row):
        rest = jnp.where(resident, own[low_row:high_row], from_guest[low_row:high_row].astype(wide))
        return (from_home[low_row:high_row].astype(wide) + rest) * factor

    grad_qkv = finish(0, 3 * width).reshape(3, width, lanes)
    grad_out = jnp.concatenate(
        [finish(3 * width, 3 * width + lanes), finish(3 * width + lanes, 4 * width)], axis=1
    )

    normed_grad = home_one.astype(wide) + home_two.astype(wide)
    own_valid = jnp.arange(capacity, dtype=jnp.int32) < lax.dynamic_index_in_dim(counts[0], seat, 0, False)
    masked_grad = jnp.where(own_valid[:, None], upstream, jnp.zeros_like(upstream))
    unit_grad = normed_grad * ln_gain
    inner = unit_grad - jnp.mean(unit_grad, axis=1, keepdims=True)
    inner = inner - standard * jnp.mean(unit_grad * standard, axis=1, keepdims=True)
    d_inputs = (masked_grad.astype(wide) + inv_std * inner).astype(low)
    return (d_inputs[None], grad_qkv, grad_out)


def solution(mesh):
    fits = mesh.shape["dp"] == 8 and mesh.shape["seq"] == 4
    placed = (
        P("dp", "seq", None),
        P("dp", "seq"),
        P("dp", None),
        P(),
        P(),
        P(),
        P("dp", "seq", None),
    )
    return jax.shard_map(
        column_shards if fits else shards,
        mesh=mesh,
        in_specs=placed,
        out_specs=(P("dp", "seq", None), P(None, "seq", "dp"), P("dp", "seq")),
        check_vma=False,
    )
```

```python
import math

import jax
import jax.numpy as jnp
import numpy as np
from jax import lax
from jax.experimental import pallas as pl
from jax.experimental.pallas import tpu as pltpu
from jax.sharding import PartitionSpec as P

HEAD_DIM = 64


EPSILON = 1e-06
MASKED = -1e30


def position_code(places, feature_width):
    half = feature_width // 2
    freqs = jnp.exp(jnp.arange(half, dtype=jnp.float32) * (-math.log(10000.0) / half))
    angle = places.astype(jnp.float32)[:, None] * freqs[None, :]
    return jnp.concatenate([jnp.sin(angle), jnp.cos(angle)], axis=1)


def layer_norm(inputs, places, ln_gain):
    shifted = inputs.astype(jnp.float32) + position_code(places, inputs.shape[1])
    centred = shifted - jnp.mean(shifted, axis=1, keepdims=True)
    inv_std = lax.rsqrt(jnp.mean(centred * centred, axis=1, keepdims=True) + EPSILON)
    standard = centred * inv_std
    normed = (standard * ln_gain).astype(jnp.bfloat16)
    return (normed, standard, inv_std)


def input_grad(query_grad, key_grad, value_grad, masked_grad, w_qkv, standard, inv_std, ln_gain):
    normed_grad = jnp.dot(query_grad, w_qkv[0], preferred_element_type=jnp.float32)
    normed_grad = normed_grad + jnp.dot(key_grad, w_qkv[1], preferred_element_type=jnp.float32)
    normed_grad = normed_grad + jnp.dot(value_grad, w_qkv[2], preferred_element_type=jnp.float32)
    unit_grad = normed_grad * ln_gain
    inner = unit_grad - jnp.mean(unit_grad, axis=1, keepdims=True)
    inner = inner - standard * jnp.mean(unit_grad * standard, axis=1, keepdims=True)
    return (masked_grad.astype(jnp.float32) + inv_std * inner).astype(jnp.bfloat16)


def project(normed, weight):
    return jnp.einsum("td,od->to", normed, weight, preferred_element_type=jnp.float32).astype(
        jnp.bfloat16
    )


def token_sum(left, right):
    return lax.dot_general(
        left, right, (((0,), (0,)), ((), ())), preferred_element_type=jnp.float32
    )


def attention_grads(queries, key_rows, value_rows, attn_grad, key_valid, score_scale):
    total, span = queries.shape
    heads_here = span // HEAD_DIM
    block = math.gcd(512, total)
    blocks = total // block
    key_three = key_rows.reshape(total, heads_here, HEAD_DIM)
    value_three = value_rows.reshape(total, heads_here, HEAD_DIM)
    query_four = queries.reshape(blocks, block, heads_here, HEAD_DIM)
    grad_four = attn_grad.reshape(blocks, block, heads_here, HEAD_DIM)

    def step(carry, item):
        key_acc, value_acc = carry
        query_block, grad_block = item
        scores = (
            jnp.einsum("qhd,khd->hqk", query_block, key_three, preferred_element_type=jnp.float32)
            * score_scale
        )
        scores = jnp.where(key_valid[None, None, :], scores, MASKED)
        peak = jnp.max(scores, axis=2, keepdims=True)
        expo = jnp.exp(scores - peak)
        probs = expo / jnp.sum(expo, axis=2, keepdims=True)
        probs_low = probs.astype(jnp.bfloat16)
        attended = jnp.einsum(
            "hqk,khd->qhd", probs_low, value_three, preferred_element_type=jnp.float32
        )
        delta = jnp.sum(grad_block.astype(jnp.float32) * attended, axis=2)
        prob_grad = jnp.einsum(
            "qhd,khd->hqk", grad_block, value_three, preferred_element_type=jnp.float32
        )
        score_grad = (probs * (prob_grad - jnp.transpose(delta)[:, :, None])).astype(jnp.bfloat16)
        query_grad = jnp.einsum(
            "hqk,khd->qhd", score_grad, key_three, preferred_element_type=jnp.float32
        )
        query_grad = (query_grad * score_scale).astype(jnp.bfloat16)
        key_acc = key_acc + jnp.einsum(
            "hqk,qhd->khd", score_grad, query_block, preferred_element_type=jnp.float32
        )
        value_acc = value_acc + jnp.einsum(
            "hqk,qhd->khd", probs_low, grad_block, preferred_element_type=jnp.float32
        )
        return ((key_acc, value_acc), (attended.astype(jnp.bfloat16), query_grad))

    zeros_acc = jnp.zeros((total, heads_here, HEAD_DIM), jnp.float32)
    sums, outputs = lax.scan(step, (zeros_acc, zeros_acc), (query_four, grad_four))
    attended = outputs[0].reshape(total, span)
    query_grad = outputs[1].reshape(total, span)
    key_grad = (sums[0] * score_scale).astype(jnp.bfloat16).reshape(total, span)
    value_grad = sums[1].astype(jnp.bfloat16).reshape(total, span)
    return (attended, query_grad, key_grad, value_grad)


def shards(tokens, positions, counts, ln_gain, w_qkv, w_out, d_out):
    inputs = tokens[0]
    places = positions[0]
    upstream = d_out[0]
    capacity, feature_width = inputs.shape
    shard_total = lax.axis_size("seq")
    shard_index = lax.axis_index("seq")
    slot_count = capacity * shard_total
    key_valid = jnp.arange(slot_count, dtype=jnp.int32) % capacity < jnp.repeat(counts[0], capacity)
    own_valid = lax.dynamic_slice_in_dim(key_valid, shard_index * capacity, capacity)
    normed, standard, inv_std = layer_norm(inputs, places, ln_gain)
    masked_grad = jnp.where(own_valid[:, None], upstream, jnp.zeros_like(upstream))
    score_scale = HEAD_DIM ** (-0.5)
    factor = 1.0 / math.sqrt(lax.axis_size("dp") * (3 * slot_count // 4))
    head_width = feature_width // shard_total
    normed_all, grad_all = (
        lax.all_gather(normed, "seq", axis=0, tiled=True),
        lax.all_gather(masked_grad, "seq", axis=0, tiled=True),
    )
    local_qkv = lax.dynamic_slice_in_dim(w_qkv, shard_index * head_width, head_width, 1)
    local_out = lax.dynamic_slice_in_dim(w_out, shard_index * head_width, head_width, 1)
    queries = project(normed_all, local_qkv[0])
    key_rows = project(normed_all, local_qkv[1])
    value_rows = project(normed_all, local_qkv[2])
    attn_grad = jnp.dot(grad_all, local_out, preferred_element_type=jnp.float32).astype(
        jnp.bfloat16
    )
    attended, query_grad, key_grad, value_grad = attention_grads(
        queries, key_rows, value_rows, attn_grad, key_valid, score_scale
    )
    term_qkv = jnp.stack(
        [
            token_sum(query_grad, normed_all),
            token_sum(key_grad, normed_all),
            token_sum(value_grad, normed_all),
        ]
    )
    term_out = token_sum(grad_all, attended)
    grad_qkv, grad_out = (
        lax.psum_scatter(term_qkv, "dp", scatter_dimension=2, tiled=True),
        lax.psum_scatter(term_out, "dp", scatter_dimension=0, tiled=True),
    )
    query_rows, key_back, value_back = (
        lax.all_to_all(query_grad, "seq", split_axis=0, concat_axis=1, tiled=True),
        lax.all_to_all(key_grad, "seq", split_axis=0, concat_axis=1, tiled=True),
        lax.all_to_all(value_grad, "seq", split_axis=0, concat_axis=1, tiled=True),
    )
    d_inputs = input_grad(
        query_rows, key_back, value_back, masked_grad, w_qkv, standard, inv_std, ln_gain
    )
    return (d_inputs[None], grad_qkv * factor, grad_out * factor)


FIRST_MOVES = (
    ((0, 0), (2, 0)),
    ((1, 0), (0, 0)),
    ((2, 0), (0, 1)),
    ((3, 0), (2, 1)),
    ((0, 1), (1, 0)),
    ((1, 1), (3, 1)),
    ((2, 1), (3, 0)),
    ((3, 1), (1, 1)),
)
SECOND_MOVES = (
    ((0, 1), (3, 0)),
    ((3, 0), (0, 1)),
    ((1, 0), (2, 1)),
    ((2, 1), (1, 0)),
    ((0, 0), (0, 0)),
    ((1, 1), (1, 1)),
    ((2, 0), (2, 0)),
    ((3, 1), (3, 1)),
)
HOME_MOVES = (
    ((0, 0), (0, 1)),
    ((1, 1), (1, 0)),
    ((1, 0), (0, 0)),
    ((0, 1), (1, 1)),
    ((2, 0), (2, 1)),
    ((3, 1), (3, 0)),
    ((3, 0), (2, 0)),
    ((2, 1), (3, 1)),
)
GUEST_MOVES = (
    ((1, 0), (0, 1)),
    ((0, 1), (1, 0)),
    ((3, 0), (2, 1)),
    ((2, 1), (3, 0)),
)


def column_pairs(moves, chips, seqs, back=False):
    pairs = []
    for chip in range(chips):
        for source, target in moves:
            if back:
                source, target = target, source
            pairs.append(
                ((chip * 2 + source[1]) * seqs + source[0], (chip * 2 + target[1]) * seqs + target[0])
            )
    return pairs


def block_table():
    table = [[0, 0] for _ in range(8)]
    for place, moves in enumerate((FIRST_MOVES, SECOND_MOVES)):
        for (source, _), (target, core) in moves:
            table[target * 2 + core][place] = source
    return table


def nt(left, right):
    return lax.dot_general(left, right, (((1,), (1,)), ((), ())), preferred_element_type=jnp.float32)


def nn(left, right):
    return lax.dot_general(left, right, (((1,), (0,)), ((), ())), preferred_element_type=jnp.float32)


def tn(left, right):
    return lax.dot_general(left, right, (((0,), (0,)), ((), ())), preferred_element_type=jnp.float32)


def gather_matrix(sizes, capacity, rows):
    total = len(sizes) * capacity
    slot = lax.broadcasted_iota(jnp.int32, (1, total), 1)
    limit = jnp.zeros((1, total), jnp.int32)
    shift = jnp.zeros((1, total), jnp.int32)
    start = 0
    for block, size in enumerate(sizes):
        later = slot >= block * capacity
        limit = jnp.where(later, block * capacity + size, limit)
        shift = jnp.where(later, start - block * capacity, shift)
        start = start + size
    rank = jnp.where(slot < limit, slot + shift, -1)
    row = lax.broadcasted_iota(jnp.int32, (rows, total), 0)
    return jnp.where(row == rank, 1.0, 0.0).astype(jnp.bfloat16)


def layer_norm_kernel(places, inputs, ln_gain, freqs, normed):
    rows, features = inputs.shape
    place = jnp.broadcast_to(places[...].astype(jnp.float32), (rows, rows)).T
    angle = jnp.concatenate([place] * (features // 2 // rows), axis=1) * freqs[...]
    shifted = inputs[...].astype(jnp.float32) + jnp.concatenate([jnp.sin(angle), jnp.cos(angle)], axis=1)
    centred = shifted - jnp.mean(shifted, axis=1, keepdims=True)
    inv_std = lax.rsqrt(jnp.mean(centred * centred, axis=1, keepdims=True) + EPSILON)
    normed[...] = (centred * inv_std * ln_gain[...]).astype(normed.dtype)


def lift_kernel(info, g0, g1, g2, g3, weight_out, gathered, lifted, rows_g, sems):
    capacity = g0.shape[0]
    copies = [
        pltpu.make_async_copy(source, rows_g.at[pl.ds(block * capacity, capacity), :], sems.at[block])
        for block, source in enumerate((g0, g1, g2, g3))
    ]
    for copy in copies:
        copy.start()
    matrix = gather_matrix([info[block] for block in range(4)], capacity, gathered.shape[0])
    for copy in copies:
        copy.wait()
    gathered[...] = nn(matrix, rows_g[...]).astype(gathered.dtype)
    lifted[...] = nn(gathered[...], weight_out[...]).T.astype(lifted.dtype)


def weight_kernel(place, w_out, w_qkv, own_out, own_qkv, sems):
    width = own_out.shape[1]
    group = pl.multiple_of(place[0] * width, width)
    copies = [pltpu.make_async_copy(w_out.at[:, pl.ds(group, width)], own_out, sems.at[3])]
    for part in range(3):
        copies.append(
            pltpu.make_async_copy(
                w_qkv.at[part, pl.ds(group, width), :],
                own_qkv.at[pl.ds(part * width, width), :],
                sems.at[part],
            )
        )
    for copy in copies:
        copy.start()
    for copy in copies:
        copy.wait()


def main_kernel(
    info, t0, t1, t2, t3, gathered_g, lifted, weight,
    x_send, x_keep, y_send, y_keep, grads,
    rows_t, gathered_t, query, key, value, stack,
):
    capacity = t0.shape[0]
    width = lifted.shape[0]
    lanes = width // 2
    low = jnp.bfloat16
    scale = HEAD_DIM ** (-0.5)

    matrix = gather_matrix([info[block] for block in range(4)], capacity, gathered_t.shape[0])
    for block, source in enumerate((t0, t1, t2, t3)):
        rows_t[pl.ds(block * capacity, capacity), :] = source[...]
    gathered_t[...] = nn(matrix, rows_t[...]).astype(low)
    query[...] = (nt(weight[0:width, :], gathered_t[...]).astype(low) * scale).astype(low)
    key[...] = nt(weight[width : 2 * width, :], gathered_t[...]).astype(low)
    value[...] = nt(weight[2 * width : 3 * width, :], gathered_t[...]).astype(low)

    for head in range(width // HEAD_DIM):
        span = pl.ds(head * HEAD_DIM, HEAD_DIM)
        query_h, key_h, value_h, lifted_h = query[span, :], key[span, :], value[span, :], lifted[span, :]
        scores = tn(key_h, query_h)
        expo = jnp.exp(scores - jnp.max(scores, axis=0, keepdims=True))
        probs = expo * (1.0 / jnp.sum(expo, axis=0, keepdims=True))
        probs_low = probs.astype(low)
        attended = nn(value_h, probs_low)
        delta = jnp.sum(lifted_h.astype(jnp.float32) * attended, axis=0, keepdims=True)
        score_grad = (probs * (tn(value_h, lifted_h) - delta)).astype(low)
        stack[pl.ds(head * HEAD_DIM, HEAD_DIM), :] = (nn(key_h, score_grad) * scale).astype(low)
        stack[pl.ds(width + head * HEAD_DIM, HEAD_DIM), :] = nt(query_h, score_grad).astype(low)
        stack[pl.ds(2 * width + head * HEAD_DIM, HEAD_DIM), :] = nt(lifted_h, probs_low).astype(low)
        stack[pl.ds(3 * width + head * HEAD_DIM, HEAD_DIM), :] = attended.astype(low)

    grads[...] = stack[0 : 3 * width, :]
    for slot_y, slot_x in ((0, 0), (1, 0), (0, 1), (1, 1)):
        block = (info[5] ^ slot_y) * 2 + (info[6] ^ slot_x)
        cols = pl.ds(pl.multiple_of(block * width, width), width)
        term_t = nn(stack[0 : 3 * width, :], gathered_t[:, cols])
        term_g = nn(stack[3 * width : 4 * width, :], gathered_g[:, cols]).T
        x_target = x_send if slot_x else x_keep
        y_target = y_send if slot_y else y_keep
        for side in range(2):
            across = slice(side * lanes, (side + 1) * lanes)
            spot = info[7] ^ side
            x_target[slot_y, spot, :, :] = term_t[0 : 2 * width, across].astype(x_target.dtype)
            y_target[slot_x, spot, 0:width, :] = term_t[2 * width : 3 * width, across].astype(y_target.dtype)
            for part in range(2):
                y_target[slot_x, spot, width + part * lanes : width + (part + 1) * lanes, :] = term_g[
                    across, part * lanes : (part + 1) * lanes
                ].astype(y_target.dtype)


def normed_kernel(info, own, other, w_qkv, back_one, back_two, weight, sems):
    width = own.shape[0] // 3
    rows = own.shape[1]
    capacity = back_one.shape[0]
    first = pl.multiple_of((info[4] >> 1) * 2 * width, 2 * width)
    core = info[4] & 1
    loads = [
        pltpu.make_async_copy(
            w_qkv.at[part, pl.ds(first, 2 * width), :],
            weight.at[pl.ds(part * 2 * width, 2 * width), :],
            sems.at[part],
        )
        for part in range(3)
    ]
    for copy in loads:
        copy.start()
    half = 2 * capacity
    mine = gather_matrix([info[block] for block in range(4)], capacity, rows)[:, 0:half]
    theirs = gather_matrix([info[(block + 2) % 4] for block in range(4)], capacity, rows)[:, half:]
    own_grads = nn(own[...], mine).astype(own.dtype)
    other_grads = nn(other[...], theirs).astype(own.dtype)
    total = jnp.zeros((half, weight.shape[1]), jnp.float32)
    for part in range(3):
        loads[part].wait()
        span = slice(part * width, (part + 1) * width)
        for grads, spot in ((own_grads, core), (other_grads, 1 - core)):
            place = pl.ds(pl.multiple_of((part * 2 + spot) * width, width), width)
            total = total + tn(grads[span, :], weight[place, :])
    back_one[...] = total[0:capacity].astype(back_one.dtype)
    back_two[...] = total[capacity:half].astype(back_two.dtype)


def sum_kernel(x_part, y_part, x_second, y_second, home_send, guest_send, own):
    half = x_part.shape[1]
    for rows, part, second in ((0, x_part, x_second), (half, y_part, y_second)):
        span = pl.ds(rows, half)
        home_send[span, :] = (part[0] + second[0].astype(part.dtype)).astype(home_send.dtype)
        total = part[1] + second[1].astype(part.dtype)
        guest_send[span, :] = total.astype(guest_send.dtype)
        own[span, :] = total


def specs(space, count):
    return [pl.BlockSpec(memory_space=space)] * count


VMEM_BYTES = 50 * 1024 * 1024
MAIN_BYTES = 28 * 1024 * 1024
FULL_BYTES = 60 * 1024 * 1024


def column_shards(tokens, positions, counts, ln_gain, w_qkv, w_out, d_out):
    low, wide = jnp.bfloat16, jnp.float32
    inputs = tokens[0]
    upstream = d_out[0]
    capacity, features = inputs.shape
    seqs = lax.axis_size("seq")
    chips = lax.axis_size("dp") // 2
    seat = lax.axis_index("seq")
    dp = lax.axis_index("dp")
    core, place_x, place_y = dp & 1, (dp >> 1) & 1, dp >> 2
    total = seqs * capacity
    half = total // 2
    width = features // seqs
    lanes = width // 2
    factor = 1.0 / math.sqrt(lax.axis_size("dp") * (3 * total // 4))
    guest = core ^ (seat & 1)
    resident = guest == 0

    axes = ("dp", "seq")
    first = column_pairs(FIRST_MOVES, chips, seqs)
    second = column_pairs(SECOND_MOVES, chips, seqs)
    first_back = column_pairs(FIRST_MOVES, chips, seqs, True)
    home = column_pairs(HOME_MOVES, chips, seqs)
    guests = column_pairs(GUEST_MOVES, chips, seqs)

    def across(array, bit):
        return lax.ppermute(array, "dp", [(i, i ^ bit) for i in range(2 * chips)])

    def fetch(array):
        two = lax.ppermute(array, axes, second)
        return lax.ppermute(array, axes, first), two

    def share(pair):
        return pair + (across(pair[0], 1), across(pair[1], 1))

    group = (seat >> 1) * 2 + core
    place = jnp.stack([group, place_y, place_x, core ^ 1 ^ guest]).astype(jnp.int32)
    params = pltpu.CompilerParams(vmem_limit_bytes=VMEM_BYTES)
    smem = specs(pltpu.SMEM, 1)

    fetched_g = fetch(upstream)
    other_counts = across(counts[0], 1)
    steps = np.arange(features // 2, dtype=np.float32) * np.float32(-math.log(10000.0) / (features // 2))
    normed = pl.pallas_call(
        layer_norm_kernel,
        out_shape=jax.ShapeDtypeStruct((capacity, features), low),
        in_specs=specs(pltpu.VMEM, 4),
        out_specs=pl.BlockSpec(memory_space=pltpu.VMEM),
        compiler_params=pltpu.CompilerParams(vmem_limit_bytes=FULL_BYTES),
    )(positions, inputs, ln_gain[None], jnp.asarray(np.exp(steps)[None]))
    fetched_t = fetch(normed)
    own_out, own_qkv = pl.pallas_call(
        weight_kernel,
        out_shape=(
            jax.ShapeDtypeStruct((features, width), low),
            jax.ShapeDtypeStruct((3 * width, features), low),
        ),
        in_specs=smem + specs(pl.ANY, 2),
        out_specs=specs(pltpu.VMEM, 2),
        scratch_shapes=[pltpu.SemaphoreType.DMA((4,))],
        compiler_params=params,
        cost_estimate=pl.CostEstimate(flops=0, bytes_accessed=4 * 1024 * 1024, transcendentals=0),
    )(place, w_out, w_qkv)
    _, standard, inv_std = layer_norm(inputs, positions[0], ln_gain)
    own_valid = jnp.arange(capacity, dtype=jnp.int32) < lax.dynamic_index_in_dim(counts[0], seat, 0, False)
    masked_grad = jnp.where(own_valid[:, None], upstream, jnp.zeros_like(upstream))

    sizes = jnp.where(resident, counts[0], other_counts)
    table = jnp.array(block_table(), jnp.int32)
    order = jnp.concatenate([table[seat * 2 + core], table[seat * 2 + 1 - core]])
    info = jnp.concatenate([sizes[order], place])

    fetched_g, info, own_out, own_qkv, masked_grad = lax.optimization_barrier(
        (fetched_g, info, own_out, own_qkv, masked_grad)
    )
    blocks_g = share(fetched_g)
    fetched_t, blocks_g = lax.optimization_barrier((fetched_t, blocks_g))
    rows = 3 * total // 4
    gathered_g, lifted = pl.pallas_call(
        lift_kernel,
        out_shape=(
            jax.ShapeDtypeStruct((rows, features), low),
            jax.ShapeDtypeStruct((width, rows), low),
        ),
        in_specs=smem + specs(pl.ANY, 4) + specs(pltpu.VMEM, 1),
        out_specs=specs(pltpu.VMEM, 2),
        scratch_shapes=[pltpu.VMEM((total, features), low), pltpu.SemaphoreType.DMA((4,))],
        compiler_params=pltpu.CompilerParams(vmem_limit_bytes=MAIN_BYTES),
        cost_estimate=pl.CostEstimate(
            flops=2 * rows * features * (width + total), bytes_accessed=3 * 1024 * 1024, transcendentals=0
        ),
    )(info, *blocks_g, own_out)
    blocks_t = share(fetched_t)

    send_shape = jax.ShapeDtypeStruct((2, 2, 2 * width, lanes), low)
    keep_shape = jax.ShapeDtypeStruct((2, 2, 2 * width, lanes), wide)
    grads_shape = jax.ShapeDtypeStruct((3 * width, rows), low)
    x_send, x_keep, y_send, y_keep, grads = pl.pallas_call(
        main_kernel,
        out_shape=(
            send_shape, keep_shape, send_shape, keep_shape, grads_shape
        ),
        in_specs=smem + specs(pltpu.VMEM, 7),
        out_specs=specs(pltpu.VMEM, 5),
        scratch_shapes=[
            pltpu.VMEM((total, features), low),
            pltpu.VMEM((rows, features), low),
            pltpu.VMEM((width, rows), low),
            pltpu.VMEM((width, rows), low),
            pltpu.VMEM((width, rows), low),
            pltpu.VMEM((4 * width, rows), low),
        ],
        compiler_params=pltpu.CompilerParams(vmem_limit_bytes=MAIN_BYTES),
        cost_estimate=pl.CostEstimate(
            flops=2 * total * features * width * 7 + 12 * 4 * total * total * HEAD_DIM,
            bytes_accessed=8 * 1024 * 1024,
            transcendentals=4 * total * total,
        ),
    )(info, *blocks_t, gathered_g, lifted, own_qkv)

    x_first, y_first = across(x_send, 2), across(y_send, 4)
    from_core = across(grads, 1)
    block_shape = jax.ShapeDtypeStruct((capacity, features), low)
    back_one, back_two = pl.pallas_call(
        normed_kernel,
        out_shape=(block_shape, block_shape),
        in_specs=smem + specs(pltpu.VMEM, 2) + specs(pl.ANY, 1),
        out_specs=specs(pltpu.VMEM, 2),
        scratch_shapes=[
            pltpu.VMEM((6 * width, features), low),
            pltpu.SemaphoreType.DMA((3,)),
        ],
        compiler_params=params,
        cost_estimate=pl.CostEstimate(
            flops=2 * total * features * width * 3, bytes_accessed=4 * 1024 * 1024, transcendentals=0
        ),
    )(info, grads, from_core, w_qkv)
    home_one = lax.ppermute(back_one, axes, first_back)
    x_first, y_first, home_one, back_two = lax.optimization_barrier((x_first, y_first, home_one, back_two))
    home_two = lax.ppermute(back_two, axes, second)
    x_second = across((x_keep[1] + x_first[1].astype(wide)).astype(low), 4)
    y_second = across((y_keep[1] + y_first[1].astype(wide)).astype(low), 2)
    x_part = x_keep[0] + x_first[0].astype(wide)
    y_part = y_keep[0] + y_first[0].astype(wide)
    x_part, y_part = lax.optimization_barrier((x_part, y_part))
    home_send, guest_send, own = pl.pallas_call(
        sum_kernel,
        out_shape=(
            jax.ShapeDtypeStruct((4 * width, lanes), low),
            jax.ShapeDtypeStruct((4 * width, lanes), low),
            jax.ShapeDtypeStruct((4 * width, lanes), wide),
        ),
        in_specs=specs(pltpu.VMEM, 4),
        out_specs=specs(pltpu.VMEM, 3),
        compiler_params=pltpu.CompilerParams(vmem_limit_bytes=16 * 1024 * 1024),
        cost_estimate=pl.CostEstimate(flops=4 * width * 2 * lanes, bytes_accessed=2 * 1024 * 1024, transcendentals=0),
    )(x_part, y_part, x_second, y_second)
    from_home = lax.ppermute(home_send, axes, home)
    from_guest = lax.ppermute(guest_send, axes, guests)

    def finish(low_row, high_row):
        rest = jnp.where(resident, own[low_row:high_row], from_guest[low_row:high_row].astype(wide))
        return (from_home[low_row:high_row].astype(wide) + rest) * factor

    grad_qkv = finish(0, 3 * width).reshape(3, width, lanes)
    grad_out = jnp.concatenate(
        [finish(3 * width, 3 * width + lanes), finish(3 * width + lanes, 4 * width)], axis=1
    )

    normed_grad = home_one.astype(wide) + home_two.astype(wide)
    unit_grad = normed_grad * ln_gain
    inner = unit_grad - jnp.mean(unit_grad, axis=1, keepdims=True)
    inner = inner - standard * jnp.mean(unit_grad * standard, axis=1, keepdims=True)
    d_inputs = (masked_grad.astype(wide) + inv_std * inner).astype(low)
    return (d_inputs[None], grad_qkv, grad_out)


def solution(mesh):
    fits = mesh.shape["dp"] == 8 and mesh.shape["seq"] == 4
    placed = (
        P("dp", "seq", None),
        P("dp", "seq"),
        P("dp", None),
        P(),
        P(),
        P(),
        P("dp", "seq", None),
    )
    return jax.shard_map(
        column_shards if fits else shards,
        mesh=mesh,
        in_specs=placed,
        out_specs=(P("dp", "seq", None), P(None, "seq", "dp"), P("dp", "seq")),
        check_vma=False,
    )
```

```python
import math

import jax
import jax.numpy as jnp
import numpy as np
from jax import lax
from jax.experimental import pallas as pl
from jax.experimental.pallas import tpu as pltpu
from jax.sharding import PartitionSpec as P

HEAD_DIM = 64


EPSILON = 1e-06
MASKED = -1e30


def position_code(places, feature_width):
    half = feature_width // 2
    freqs = jnp.exp(jnp.arange(half, dtype=jnp.float32) * (-math.log(10000.0) / half))
    angle = places.astype(jnp.float32)[:, None] * freqs[None, :]
    return jnp.concatenate([jnp.sin(angle), jnp.cos(angle)], axis=1)


def layer_norm(inputs, places, ln_gain):
    shifted = inputs.astype(jnp.float32) + position_code(places, inputs.shape[1])
    centred = shifted - jnp.mean(shifted, axis=1, keepdims=True)
    inv_std = lax.rsqrt(jnp.mean(centred * centred, axis=1, keepdims=True) + EPSILON)
    standard = centred * inv_std
    normed = (standard * ln_gain).astype(jnp.bfloat16)
    return (normed, standard, inv_std)


def input_grad(query_grad, key_grad, value_grad, masked_grad, w_qkv, standard, inv_std, ln_gain):
    normed_grad = jnp.dot(query_grad, w_qkv[0], preferred_element_type=jnp.float32)
    normed_grad = normed_grad + jnp.dot(key_grad, w_qkv[1], preferred_element_type=jnp.float32)
    normed_grad = normed_grad + jnp.dot(value_grad, w_qkv[2], preferred_element_type=jnp.float32)
    unit_grad = normed_grad * ln_gain
    inner = unit_grad - jnp.mean(unit_grad, axis=1, keepdims=True)
    inner = inner - standard * jnp.mean(unit_grad * standard, axis=1, keepdims=True)
    return (masked_grad.astype(jnp.float32) + inv_std * inner).astype(jnp.bfloat16)


def project(normed, weight):
    return jnp.einsum("td,od->to", normed, weight, preferred_element_type=jnp.float32).astype(
        jnp.bfloat16
    )


def token_sum(left, right):
    return lax.dot_general(
        left, right, (((0,), (0,)), ((), ())), preferred_element_type=jnp.float32
    )


def attention_grads(queries, key_rows, value_rows, attn_grad, key_valid, score_scale):
    total, span = queries.shape
    heads_here = span // HEAD_DIM
    block = math.gcd(512, total)
    blocks = total // block
    key_three = key_rows.reshape(total, heads_here, HEAD_DIM)
    value_three = value_rows.reshape(total, heads_here, HEAD_DIM)
    query_four = queries.reshape(blocks, block, heads_here, HEAD_DIM)
    grad_four = attn_grad.reshape(blocks, block, heads_here, HEAD_DIM)

    def step(carry, item):
        key_acc, value_acc = carry
        query_block, grad_block = item
        scores = (
            jnp.einsum("qhd,khd->hqk", query_block, key_three, preferred_element_type=jnp.float32)
            * score_scale
        )
        scores = jnp.where(key_valid[None, None, :], scores, MASKED)
        peak = jnp.max(scores, axis=2, keepdims=True)
        expo = jnp.exp(scores - peak)
        probs = expo / jnp.sum(expo, axis=2, keepdims=True)
        probs_low = probs.astype(jnp.bfloat16)
        attended = jnp.einsum(
            "hqk,khd->qhd", probs_low, value_three, preferred_element_type=jnp.float32
        )
        delta = jnp.sum(grad_block.astype(jnp.float32) * attended, axis=2)
        prob_grad = jnp.einsum(
            "qhd,khd->hqk", grad_block, value_three, preferred_element_type=jnp.float32
        )
        score_grad = (probs * (prob_grad - jnp.transpose(delta)[:, :, None])).astype(jnp.bfloat16)
        query_grad = jnp.einsum(
            "hqk,khd->qhd", score_grad, key_three, preferred_element_type=jnp.float32
        )
        query_grad = (query_grad * score_scale).astype(jnp.bfloat16)
        key_acc = key_acc + jnp.einsum(
            "hqk,qhd->khd", score_grad, query_block, preferred_element_type=jnp.float32
        )
        value_acc = value_acc + jnp.einsum(
            "hqk,qhd->khd", probs_low, grad_block, preferred_element_type=jnp.float32
        )
        return ((key_acc, value_acc), (attended.astype(jnp.bfloat16), query_grad))

    zeros_acc = jnp.zeros((total, heads_here, HEAD_DIM), jnp.float32)
    sums, outputs = lax.scan(step, (zeros_acc, zeros_acc), (query_four, grad_four))
    attended = outputs[0].reshape(total, span)
    query_grad = outputs[1].reshape(total, span)
    key_grad = (sums[0] * score_scale).astype(jnp.bfloat16).reshape(total, span)
    value_grad = sums[1].astype(jnp.bfloat16).reshape(total, span)
    return (attended, query_grad, key_grad, value_grad)


def shards(tokens, positions, counts, ln_gain, w_qkv, w_out, d_out):
    inputs = tokens[0]
    places = positions[0]
    upstream = d_out[0]
    capacity, feature_width = inputs.shape
    shard_total = lax.axis_size("seq")
    shard_index = lax.axis_index("seq")
    slot_count = capacity * shard_total
    key_valid = jnp.arange(slot_count, dtype=jnp.int32) % capacity < jnp.repeat(counts[0], capacity)
    own_valid = lax.dynamic_slice_in_dim(key_valid, shard_index * capacity, capacity)
    normed, standard, inv_std = layer_norm(inputs, places, ln_gain)
    masked_grad = jnp.where(own_valid[:, None], upstream, jnp.zeros_like(upstream))
    score_scale = HEAD_DIM ** (-0.5)
    factor = 1.0 / math.sqrt(lax.axis_size("dp") * (3 * slot_count // 4))
    head_width = feature_width // shard_total
    normed_all, grad_all = (
        lax.all_gather(normed, "seq", axis=0, tiled=True),
        lax.all_gather(masked_grad, "seq", axis=0, tiled=True),
    )
    local_qkv = lax.dynamic_slice_in_dim(w_qkv, shard_index * head_width, head_width, 1)
    local_out = lax.dynamic_slice_in_dim(w_out, shard_index * head_width, head_width, 1)
    queries = project(normed_all, local_qkv[0])
    key_rows = project(normed_all, local_qkv[1])
    value_rows = project(normed_all, local_qkv[2])
    attn_grad = jnp.dot(grad_all, local_out, preferred_element_type=jnp.float32).astype(
        jnp.bfloat16
    )
    attended, query_grad, key_grad, value_grad = attention_grads(
        queries, key_rows, value_rows, attn_grad, key_valid, score_scale
    )
    term_qkv = jnp.stack(
        [
            token_sum(query_grad, normed_all),
            token_sum(key_grad, normed_all),
            token_sum(value_grad, normed_all),
        ]
    )
    term_out = token_sum(grad_all, attended)
    grad_qkv, grad_out = (
        lax.psum_scatter(term_qkv, "dp", scatter_dimension=2, tiled=True),
        lax.psum_scatter(term_out, "dp", scatter_dimension=0, tiled=True),
    )
    query_rows, key_back, value_back = (
        lax.all_to_all(query_grad, "seq", split_axis=0, concat_axis=1, tiled=True),
        lax.all_to_all(key_grad, "seq", split_axis=0, concat_axis=1, tiled=True),
        lax.all_to_all(value_grad, "seq", split_axis=0, concat_axis=1, tiled=True),
    )
    d_inputs = input_grad(
        query_rows, key_back, value_back, masked_grad, w_qkv, standard, inv_std, ln_gain
    )
    return (d_inputs[None], grad_qkv * factor, grad_out * factor)


FIRST_MOVES = (
    ((0, 0), (2, 0)),
    ((1, 0), (0, 0)),
    ((2, 0), (0, 1)),
    ((3, 0), (2, 1)),
    ((0, 1), (1, 0)),
    ((1, 1), (3, 1)),
    ((2, 1), (3, 0)),
    ((3, 1), (1, 1)),
)
SECOND_MOVES = (
    ((0, 1), (3, 0)),
    ((3, 0), (0, 1)),
    ((1, 0), (2, 1)),
    ((2, 1), (1, 0)),
    ((0, 0), (0, 0)),
    ((1, 1), (1, 1)),
    ((2, 0), (2, 0)),
    ((3, 1), (3, 1)),
)
HOME_MOVES = (
    ((0, 0), (0, 1)),
    ((1, 1), (1, 0)),
    ((1, 0), (0, 0)),
    ((0, 1), (1, 1)),
    ((2, 0), (2, 1)),
    ((3, 1), (3, 0)),
    ((3, 0), (2, 0)),
    ((2, 1), (3, 1)),
)
GUEST_MOVES = (
    ((1, 0), (0, 1)),
    ((0, 1), (1, 0)),
    ((3, 0), (2, 1)),
    ((2, 1), (3, 0)),
)


def column_pairs(moves, chips, seqs, back=False):
    pairs = []
    for chip in range(chips):
        for source, target in moves:
            if back:
                source, target = target, source
            pairs.append(
                ((chip * 2 + source[1]) * seqs + source[0], (chip * 2 + target[1]) * seqs + target[0])
            )
    return pairs


def block_table():
    table = [[0, 0] for _ in range(8)]
    for place, moves in enumerate((FIRST_MOVES, SECOND_MOVES)):
        for (source, _), (target, core) in moves:
            table[target * 2 + core][place] = source
    return table


def nt(left, right):
    return lax.dot_general(left, right, (((1,), (1,)), ((), ())), preferred_element_type=jnp.float32)


def nn(left, right):
    return lax.dot_general(left, right, (((1,), (0,)), ((), ())), preferred_element_type=jnp.float32)


def tn(left, right):
    return lax.dot_general(left, right, (((0,), (0,)), ((), ())), preferred_element_type=jnp.float32)


def gather_matrix(sizes, capacity, rows):
    total = len(sizes) * capacity
    slot = lax.broadcasted_iota(jnp.int32, (1, total), 1)
    limit = jnp.zeros((1, total), jnp.int32)
    shift = jnp.zeros((1, total), jnp.int32)
    start = 0
    for block, size in enumerate(sizes):
        later = slot >= block * capacity
        limit = jnp.where(later, block * capacity + size, limit)
        shift = jnp.where(later, start - block * capacity, shift)
        start = start + size
    rank = jnp.where(slot < limit, slot + shift, -1)
    row = lax.broadcasted_iota(jnp.int32, (rows, total), 0)
    return jnp.where(row == rank, 1.0, 0.0).astype(jnp.bfloat16)


def layer_norm_kernel(places, inputs, ln_gain, freqs, normed):
    rows, features = inputs.shape
    place = jnp.broadcast_to(places[...].astype(jnp.float32), (rows, rows)).T
    angle = jnp.concatenate([place] * (features // 2 // rows), axis=1) * freqs[...]
    shifted = inputs[...].astype(jnp.float32) + jnp.concatenate([jnp.sin(angle), jnp.cos(angle)], axis=1)
    centred = shifted - jnp.mean(shifted, axis=1, keepdims=True)
    inv_std = lax.rsqrt(jnp.mean(centred * centred, axis=1, keepdims=True) + EPSILON)
    normed[...] = (centred * inv_std * ln_gain[...]).astype(normed.dtype)


def lift_kernel(info, g0, g1, g2, g3, weight_out, gathered, lifted, rows_g, sems):
    capacity = g0.shape[0]
    copies = [
        pltpu.make_async_copy(source, rows_g.at[pl.ds(block * capacity, capacity), :], sems.at[block])
        for block, source in enumerate((g0, g1, g2, g3))
    ]
    for copy in copies:
        copy.start()
    matrix = gather_matrix([info[block] for block in range(4)], capacity, gathered.shape[0])
    for copy in copies:
        copy.wait()
    gathered[...] = nn(matrix, rows_g[...]).astype(gathered.dtype)
    lifted[...] = nn(gathered[...], weight_out[...]).T.astype(lifted.dtype)


def weight_kernel(place, w_out, w_qkv, own_out, own_qkv, sems):
    width = own_out.shape[1]
    group = pl.multiple_of(place[0] * width, width)
    copies = [pltpu.make_async_copy(w_out.at[:, pl.ds(group, width)], own_out, sems.at[3])]
    for part in range(3):
        copies.append(
            pltpu.make_async_copy(
                w_qkv.at[part, pl.ds(group, width), :],
                own_qkv.at[pl.ds(part * width, width), :],
                sems.at[part],
            )
        )
    for copy in copies:
        copy.start()
    for copy in copies:
        copy.wait()


def main_kernel(
    info, t0, t1, t2, t3, gathered_g, lifted, weight,
    x_send, x_keep, y_send, y_keep, grads,
    rows_t, gathered_t, query, key, value, stack,
):
    capacity = t0.shape[0]
    width = lifted.shape[0]
    lanes = width // 2
    low = jnp.bfloat16
    scale = HEAD_DIM ** (-0.5)

    matrix = gather_matrix([info[block] for block in range(4)], capacity, gathered_t.shape[0])
    for block, source in enumerate((t0, t1, t2, t3)):
        rows_t[pl.ds(block * capacity, capacity), :] = source[...]
    gathered_t[...] = nn(matrix, rows_t[...]).astype(low)
    query[...] = (nt(weight[0:width, :], gathered_t[...]).astype(low) * scale).astype(low)
    key[...] = nt(weight[width : 2 * width, :], gathered_t[...]).astype(low)
    value[...] = nt(weight[2 * width : 3 * width, :], gathered_t[...]).astype(low)

    for head in range(width // HEAD_DIM):
        span = pl.ds(head * HEAD_DIM, HEAD_DIM)
        query_h, key_h, value_h, lifted_h = query[span, :], key[span, :], value[span, :], lifted[span, :]
        scores = tn(key_h, query_h)
        expo = jnp.exp(scores - jnp.max(scores, axis=0, keepdims=True))
        probs = expo * (1.0 / jnp.sum(expo, axis=0, keepdims=True))
        probs_low = probs.astype(low)
        attended = nn(value_h, probs_low)
        delta = jnp.sum(lifted_h.astype(jnp.float32) * attended, axis=0, keepdims=True)
        score_grad = (probs * (tn(value_h, lifted_h) - delta)).astype(low)
        stack[pl.ds(head * HEAD_DIM, HEAD_DIM), :] = (nn(key_h, score_grad) * scale).astype(low)
        stack[pl.ds(width + head * HEAD_DIM, HEAD_DIM), :] = nt(query_h, score_grad).astype(low)
        stack[pl.ds(2 * width + head * HEAD_DIM, HEAD_DIM), :] = nt(lifted_h, probs_low).astype(low)
        stack[pl.ds(3 * width + head * HEAD_DIM, HEAD_DIM), :] = attended.astype(low)

    grads[...] = stack[0 : 3 * width, :]
    for slot_y, slot_x in ((0, 0), (1, 0), (0, 1), (1, 1)):
        block = (info[5] ^ slot_y) * 2 + (info[6] ^ slot_x)
        cols = pl.ds(pl.multiple_of(block * width, width), width)
        term_t = nn(stack[0 : 3 * width, :], gathered_t[:, cols])
        term_g = nn(stack[3 * width : 4 * width, :], gathered_g[:, cols]).T
        x_target = x_send if slot_x else x_keep
        y_target = y_send if slot_y else y_keep
        for side in range(2):
            across = slice(side * lanes, (side + 1) * lanes)
            spot = info[7] ^ side
            x_target[slot_y, spot, :, :] = term_t[0 : 2 * width, across].astype(x_target.dtype)
            y_target[slot_x, spot, 0:width, :] = term_t[2 * width : 3 * width, across].astype(y_target.dtype)
            for part in range(2):
                y_target[slot_x, spot, width + part * lanes : width + (part + 1) * lanes, :] = term_g[
                    across, part * lanes : (part + 1) * lanes
                ].astype(y_target.dtype)


def normed_kernel(info, own, other, w_qkv, back_one, back_two, weight, sems):
    width = own.shape[0] // 3
    rows = own.shape[1]
    capacity = back_one.shape[0]
    first = pl.multiple_of((info[4] >> 1) * 2 * width, 2 * width)
    core = info[4] & 1
    loads = [
        pltpu.make_async_copy(
            w_qkv.at[part, pl.ds(first, 2 * width), :],
            weight.at[pl.ds(part * 2 * width, 2 * width), :],
            sems.at[part],
        )
        for part in range(3)
    ]
    for copy in loads:
        copy.start()
    half = 2 * capacity
    mine = gather_matrix([info[block] for block in range(4)], capacity, rows)[:, 0:half]
    theirs = gather_matrix([info[(block + 2) % 4] for block in range(4)], capacity, rows)[:, half:]
    own_grads = nn(own[...], mine).astype(own.dtype)
    other_grads = nn(other[...], theirs).astype(own.dtype)
    total = jnp.zeros((half, weight.shape[1]), jnp.float32)
    for part in range(3):
        loads[part].wait()
        span = slice(part * width, (part + 1) * width)
        for grads, spot in ((own_grads, core), (other_grads, 1 - core)):
            place = pl.ds(pl.multiple_of((part * 2 + spot) * width, width), width)
            total = total + tn(grads[span, :], weight[place, :])
    back_one[...] = total[0:capacity].astype(back_one.dtype)
    back_two[...] = total[capacity:half].astype(back_two.dtype)


def sum_kernel(x_part, y_part, x_second, y_second, home_send, guest_send, own):
    half = x_part.shape[1]
    for rows, part, second in ((0, x_part, x_second), (half, y_part, y_second)):
        span = pl.ds(rows, half)
        home_send[span, :] = (part[0] + second[0].astype(part.dtype)).astype(home_send.dtype)
        total = part[1] + second[1].astype(part.dtype)
        guest_send[span, :] = total.astype(guest_send.dtype)
        own[span, :] = total


def specs(space, count):
    return [pl.BlockSpec(memory_space=space)] * count


VMEM_BYTES = 50 * 1024 * 1024
MAIN_BYTES = 28 * 1024 * 1024
FULL_BYTES = 60 * 1024 * 1024


def column_shards(tokens, positions, counts, ln_gain, w_qkv, w_out, d_out):
    low, wide = jnp.bfloat16, jnp.float32
    inputs = tokens[0]
    upstream = d_out[0]
    capacity, features = inputs.shape
    seqs = lax.axis_size("seq")
    chips = lax.axis_size("dp") // 2
    seat = lax.axis_index("seq")
    dp = lax.axis_index("dp")
    core, place_x, place_y = dp & 1, (dp >> 1) & 1, dp >> 2
    total = seqs * capacity
    half = total // 2
    width = features // seqs
    lanes = width // 2
    factor = 1.0 / math.sqrt(lax.axis_size("dp") * (3 * total // 4))
    guest = core ^ (seat & 1)
    resident = guest == 0

    axes = ("dp", "seq")
    first = column_pairs(FIRST_MOVES, chips, seqs)
    second = column_pairs(SECOND_MOVES, chips, seqs)
    first_back = column_pairs(FIRST_MOVES, chips, seqs, True)
    home = column_pairs(HOME_MOVES, chips, seqs)
    guests = column_pairs(GUEST_MOVES, chips, seqs)

    def across(array, bit):
        return lax.ppermute(array, "dp", [(i, i ^ bit) for i in range(2 * chips)])

    def fetch(array):
        two = lax.ppermute(array, axes, second)
        return lax.ppermute(array, axes, first), two

    def share(pair):
        return pair + (across(pair[0], 1), across(pair[1], 1))

    group = (seat >> 1) * 2 + core
    place = jnp.stack([group, place_y, place_x, core ^ 1 ^ guest]).astype(jnp.int32)
    params = pltpu.CompilerParams(vmem_limit_bytes=VMEM_BYTES)
    smem = specs(pltpu.SMEM, 1)

    fetched_g = fetch(upstream)
    other_counts = across(counts[0], 1)
    steps = np.arange(features // 2, dtype=np.float32) * np.float32(-math.log(10000.0) / (features // 2))
    normed = pl.pallas_call(
        layer_norm_kernel,
        out_shape=jax.ShapeDtypeStruct((capacity, features), low),
        in_specs=specs(pltpu.VMEM, 4),
        out_specs=pl.BlockSpec(memory_space=pltpu.VMEM),
        compiler_params=pltpu.CompilerParams(vmem_limit_bytes=FULL_BYTES),
    )(positions, inputs, ln_gain[None], jnp.asarray(np.exp(steps)[None]))
    fetched_t = fetch(normed)
    own_out, own_qkv = pl.pallas_call(
        weight_kernel,
        out_shape=(
            jax.ShapeDtypeStruct((features, width), low),
            jax.ShapeDtypeStruct((3 * width, features), low),
        ),
        in_specs=smem + specs(pl.ANY, 2),
        out_specs=specs(pltpu.VMEM, 2),
        scratch_shapes=[pltpu.SemaphoreType.DMA((4,))],
        compiler_params=params,
        cost_estimate=pl.CostEstimate(flops=0, bytes_accessed=4 * 1024 * 1024, transcendentals=0),
    )(place, w_out, w_qkv)
    own_valid = jnp.arange(capacity, dtype=jnp.int32) < lax.dynamic_index_in_dim(counts[0], seat, 0, False)
    masked_grad = jnp.where(own_valid[:, None], upstream, jnp.zeros_like(upstream))

    sizes = jnp.where(resident, counts[0], other_counts)
    table = jnp.array(block_table(), jnp.int32)
    order = jnp.concatenate([table[seat * 2 + core], table[seat * 2 + 1 - core]])
    info = jnp.concatenate([sizes[order], place])

    fetched_g, info, own_out, own_qkv, masked_grad = lax.optimization_barrier(
        (fetched_g, info, own_out, own_qkv, masked_grad)
    )
    blocks_g = share(fetched_g)
    fetched_t, blocks_g = lax.optimization_barrier((fetched_t, blocks_g))
    rows = 3 * total // 4
    gathered_g, lifted = pl.pallas_call(
        lift_kernel,
        out_shape=(
            jax.ShapeDtypeStruct((rows, features), low),
            jax.ShapeDtypeStruct((width, rows), low),
        ),
        in_specs=smem + specs(pl.ANY, 4) + specs(pltpu.VMEM, 1),
        out_specs=specs(pltpu.VMEM, 2),
        scratch_shapes=[pltpu.VMEM((total, features), low), pltpu.SemaphoreType.DMA((4,))],
        compiler_params=pltpu.CompilerParams(vmem_limit_bytes=MAIN_BYTES),
        cost_estimate=pl.CostEstimate(
            flops=2 * rows * features * (width + total), bytes_accessed=3 * 1024 * 1024, transcendentals=0
        ),
    )(info, *blocks_g, own_out)
    blocks_t = share(fetched_t)

    send_shape = jax.ShapeDtypeStruct((2, 2, 2 * width, lanes), low)
    keep_shape = jax.ShapeDtypeStruct((2, 2, 2 * width, lanes), wide)
    grads_shape = jax.ShapeDtypeStruct((3 * width, rows), low)
    x_send, x_keep, y_send, y_keep, grads = pl.pallas_call(
        main_kernel,
        out_shape=(
            send_shape, keep_shape, send_shape, keep_shape, grads_shape
        ),
        in_specs=smem + specs(pltpu.VMEM, 7),
        out_specs=specs(pltpu.VMEM, 5),
        scratch_shapes=[
            pltpu.VMEM((total, features), low),
            pltpu.VMEM((rows, features), low),
            pltpu.VMEM((width, rows), low),
            pltpu.VMEM((width, rows), low),
            pltpu.VMEM((width, rows), low),
            pltpu.VMEM((4 * width, rows), low),
        ],
        compiler_params=pltpu.CompilerParams(vmem_limit_bytes=MAIN_BYTES),
        cost_estimate=pl.CostEstimate(
            flops=2 * total * features * width * 7 + 12 * 4 * total * total * HEAD_DIM,
            bytes_accessed=8 * 1024 * 1024,
            transcendentals=4 * total * total,
        ),
    )(info, *blocks_t, gathered_g, lifted, own_qkv)

    x_first, y_first = across(x_send, 2), across(y_send, 4)
    from_core = across(grads, 1)
    block_shape = jax.ShapeDtypeStruct((capacity, features), low)
    back_one, back_two = pl.pallas_call(
        normed_kernel,
        out_shape=(block_shape, block_shape),
        in_specs=smem + specs(pltpu.VMEM, 2) + specs(pl.ANY, 1),
        out_specs=specs(pltpu.VMEM, 2),
        scratch_shapes=[
            pltpu.VMEM((6 * width, features), low),
            pltpu.SemaphoreType.DMA((3,)),
        ],
        compiler_params=params,
        cost_estimate=pl.CostEstimate(
            flops=2 * total * features * width * 3, bytes_accessed=4 * 1024 * 1024, transcendentals=0
        ),
    )(info, grads, from_core, w_qkv)
    places, back_one = lax.optimization_barrier((positions, back_one))
    _, standard, inv_std = layer_norm(inputs, places[0], ln_gain)
    home_one = lax.ppermute(back_one, axes, first_back)
    x_first, y_first, home_one, back_two = lax.optimization_barrier((x_first, y_first, home_one, back_two))
    home_two = lax.ppermute(back_two, axes, second)
    x_second = across((x_keep[1] + x_first[1].astype(wide)).astype(low), 4)
    y_second = across((y_keep[1] + y_first[1].astype(wide)).astype(low), 2)
    x_part = x_keep[0] + x_first[0].astype(wide)
    y_part = y_keep[0] + y_first[0].astype(wide)
    x_part, y_part = lax.optimization_barrier((x_part, y_part))
    home_send, guest_send, own = pl.pallas_call(
        sum_kernel,
        out_shape=(
            jax.ShapeDtypeStruct((4 * width, lanes), low),
            jax.ShapeDtypeStruct((4 * width, lanes), low),
            jax.ShapeDtypeStruct((4 * width, lanes), wide),
        ),
        in_specs=specs(pltpu.VMEM, 4),
        out_specs=specs(pltpu.VMEM, 3),
        compiler_params=pltpu.CompilerParams(vmem_limit_bytes=16 * 1024 * 1024),
        cost_estimate=pl.CostEstimate(flops=4 * width * 2 * lanes, bytes_accessed=2 * 1024 * 1024, transcendentals=0),
    )(x_part, y_part, x_second, y_second)
    from_home = lax.ppermute(home_send, axes, home)
    from_guest = lax.ppermute(guest_send, axes, guests)

    def finish(low_row, high_row):
        rest = jnp.where(resident, own[low_row:high_row], from_guest[low_row:high_row].astype(wide))
        return (from_home[low_row:high_row].astype(wide) + rest) * factor

    grad_qkv = finish(0, 3 * width).reshape(3, width, lanes)
    grad_out = jnp.concatenate(
        [finish(3 * width, 3 * width + lanes), finish(3 * width + lanes, 4 * width)], axis=1
    )

    normed_grad = home_one.astype(wide) + home_two.astype(wide)
    unit_grad = normed_grad * ln_gain
    inner = unit_grad - jnp.mean(unit_grad, axis=1, keepdims=True)
    inner = inner - standard * jnp.mean(unit_grad * standard, axis=1, keepdims=True)
    d_inputs = (masked_grad.astype(wide) + inv_std * inner).astype(low)
    return (d_inputs[None], grad_qkv, grad_out)


def solution(mesh):
    fits = mesh.shape["dp"] == 8 and mesh.shape["seq"] == 4
    placed = (
        P("dp", "seq", None),
        P("dp", "seq"),
        P("dp", None),
        P(),
        P(),
        P(),
        P("dp", "seq", None),
    )
    return jax.shard_map(
        column_shards if fits else shards,
        mesh=mesh,
        in_specs=placed,
        out_specs=(P("dp", "seq", None), P(None, "seq", "dp"), P("dp", "seq")),
        check_vma=False,
    )
```

```python
import functools
import math

import jax
import jax.numpy as jnp
import numpy as np
from jax import lax
from jax.experimental import pallas as pl
from jax.experimental.pallas import tpu as pltpu
from jax.sharding import PartitionSpec as P

HEAD_DIM = 64


EPSILON = 1e-06
MASKED = -1e30


def position_code(places, feature_width):
    half = feature_width // 2
    freqs = jnp.exp(jnp.arange(half, dtype=jnp.float32) * (-math.log(10000.0) / half))
    angle = places.astype(jnp.float32)[:, None] * freqs[None, :]
    return jnp.concatenate([jnp.sin(angle), jnp.cos(angle)], axis=1)


def layer_norm(inputs, places, ln_gain):
    shifted = inputs.astype(jnp.float32) + position_code(places, inputs.shape[1])
    centred = shifted - jnp.mean(shifted, axis=1, keepdims=True)
    inv_std = lax.rsqrt(jnp.mean(centred * centred, axis=1, keepdims=True) + EPSILON)
    standard = centred * inv_std
    normed = (standard * ln_gain).astype(jnp.bfloat16)
    return (normed, standard, inv_std)


def input_grad(query_grad, key_grad, value_grad, masked_grad, w_qkv, standard, inv_std, ln_gain):
    normed_grad = jnp.dot(query_grad, w_qkv[0], preferred_element_type=jnp.float32)
    normed_grad = normed_grad + jnp.dot(key_grad, w_qkv[1], preferred_element_type=jnp.float32)
    normed_grad = normed_grad + jnp.dot(value_grad, w_qkv[2], preferred_element_type=jnp.float32)
    unit_grad = normed_grad * ln_gain
    inner = unit_grad - jnp.mean(unit_grad, axis=1, keepdims=True)
    inner = inner - standard * jnp.mean(unit_grad * standard, axis=1, keepdims=True)
    return (masked_grad.astype(jnp.float32) + inv_std * inner).astype(jnp.bfloat16)


def project(normed, weight):
    return jnp.einsum("td,od->to", normed, weight, preferred_element_type=jnp.float32).astype(
        jnp.bfloat16
    )


def token_sum(left, right):
    return lax.dot_general(
        left, right, (((0,), (0,)), ((), ())), preferred_element_type=jnp.float32
    )


def attention_grads(queries, key_rows, value_rows, attn_grad, key_valid, score_scale):
    total, span = queries.shape
    heads_here = span // HEAD_DIM
    block = math.gcd(512, total)
    blocks = total // block
    key_three = key_rows.reshape(total, heads_here, HEAD_DIM)
    value_three = value_rows.reshape(total, heads_here, HEAD_DIM)
    query_four = queries.reshape(blocks, block, heads_here, HEAD_DIM)
    grad_four = attn_grad.reshape(blocks, block, heads_here, HEAD_DIM)

    def step(carry, item):
        key_acc, value_acc = carry
        query_block, grad_block = item
        scores = (
            jnp.einsum("qhd,khd->hqk", query_block, key_three, preferred_element_type=jnp.float32)
            * score_scale
        )
        scores = jnp.where(key_valid[None, None, :], scores, MASKED)
        peak = jnp.max(scores, axis=2, keepdims=True)
        expo = jnp.exp(scores - peak)
        probs = expo / jnp.sum(expo, axis=2, keepdims=True)
        probs_low = probs.astype(jnp.bfloat16)
        attended = jnp.einsum(
            "hqk,khd->qhd", probs_low, value_three, preferred_element_type=jnp.float32
        )
        delta = jnp.sum(grad_block.astype(jnp.float32) * attended, axis=2)
        prob_grad = jnp.einsum(
            "qhd,khd->hqk", grad_block, value_three, preferred_element_type=jnp.float32
        )
        score_grad = (probs * (prob_grad - jnp.transpose(delta)[:, :, None])).astype(jnp.bfloat16)
        query_grad = jnp.einsum(
            "hqk,khd->qhd", score_grad, key_three, preferred_element_type=jnp.float32
        )
        query_grad = (query_grad * score_scale).astype(jnp.bfloat16)
        key_acc = key_acc + jnp.einsum(
            "hqk,qhd->khd", score_grad, query_block, preferred_element_type=jnp.float32
        )
        value_acc = value_acc + jnp.einsum(
            "hqk,qhd->khd", probs_low, grad_block, preferred_element_type=jnp.float32
        )
        return ((key_acc, value_acc), (attended.astype(jnp.bfloat16), query_grad))

    zeros_acc = jnp.zeros((total, heads_here, HEAD_DIM), jnp.float32)
    sums, outputs = lax.scan(step, (zeros_acc, zeros_acc), (query_four, grad_four))
    attended = outputs[0].reshape(total, span)
    query_grad = outputs[1].reshape(total, span)
    key_grad = (sums[0] * score_scale).astype(jnp.bfloat16).reshape(total, span)
    value_grad = sums[1].astype(jnp.bfloat16).reshape(total, span)
    return (attended, query_grad, key_grad, value_grad)


def shards(tokens, positions, counts, ln_gain, w_qkv, w_out, d_out):
    inputs = tokens[0]
    places = positions[0]
    upstream = d_out[0]
    capacity, feature_width = inputs.shape
    shard_total = lax.axis_size("seq")
    shard_index = lax.axis_index("seq")
    slot_count = capacity * shard_total
    key_valid = jnp.arange(slot_count, dtype=jnp.int32) % capacity < jnp.repeat(counts[0], capacity)
    own_valid = lax.dynamic_slice_in_dim(key_valid, shard_index * capacity, capacity)
    normed, standard, inv_std = layer_norm(inputs, places, ln_gain)
    masked_grad = jnp.where(own_valid[:, None], upstream, jnp.zeros_like(upstream))
    score_scale = HEAD_DIM ** (-0.5)
    factor = 1.0 / math.sqrt(lax.axis_size("dp") * (3 * slot_count // 4))
    head_width = feature_width // shard_total
    normed_all, grad_all = (
        lax.all_gather(normed, "seq", axis=0, tiled=True),
        lax.all_gather(masked_grad, "seq", axis=0, tiled=True),
    )
    local_qkv = lax.dynamic_slice_in_dim(w_qkv, shard_index * head_width, head_width, 1)
    local_out = lax.dynamic_slice_in_dim(w_out, shard_index * head_width, head_width, 1)
    queries = project(normed_all, local_qkv[0])
    key_rows = project(normed_all, local_qkv[1])
    value_rows = project(normed_all, local_qkv[2])
    attn_grad = jnp.dot(grad_all, local_out, preferred_element_type=jnp.float32).astype(
        jnp.bfloat16
    )
    attended, query_grad, key_grad, value_grad = attention_grads(
        queries, key_rows, value_rows, attn_grad, key_valid, score_scale
    )
    term_qkv = jnp.stack(
        [
            token_sum(query_grad, normed_all),
            token_sum(key_grad, normed_all),
            token_sum(value_grad, normed_all),
        ]
    )
    term_out = token_sum(grad_all, attended)
    grad_qkv, grad_out = (
        lax.psum_scatter(term_qkv, "dp", scatter_dimension=2, tiled=True),
        lax.psum_scatter(term_out, "dp", scatter_dimension=0, tiled=True),
    )
    query_rows, key_back, value_back = (
        lax.all_to_all(query_grad, "seq", split_axis=0, concat_axis=1, tiled=True),
        lax.all_to_all(key_grad, "seq", split_axis=0, concat_axis=1, tiled=True),
        lax.all_to_all(value_grad, "seq", split_axis=0, concat_axis=1, tiled=True),
    )
    d_inputs = input_grad(
        query_rows, key_back, value_back, masked_grad, w_qkv, standard, inv_std, ln_gain
    )
    return (d_inputs[None], grad_qkv * factor, grad_out * factor)


FIRST_MOVES = (
    ((0, 0), (2, 0)),
    ((1, 0), (0, 0)),
    ((2, 0), (0, 1)),
    ((3, 0), (2, 1)),
    ((0, 1), (1, 0)),
    ((1, 1), (3, 1)),
    ((2, 1), (3, 0)),
    ((3, 1), (1, 1)),
)
SECOND_MOVES = (
    ((0, 1), (3, 0)),
    ((3, 0), (0, 1)),
    ((1, 0), (2, 1)),
    ((2, 1), (1, 0)),
    ((0, 0), (0, 0)),
    ((1, 1), (1, 1)),
    ((2, 0), (2, 0)),
    ((3, 1), (3, 1)),
)
HOME_MOVES = (
    ((0, 0), (0, 1)),
    ((1, 1), (1, 0)),
    ((1, 0), (0, 0)),
    ((0, 1), (1, 1)),
    ((2, 0), (2, 1)),
    ((3, 1), (3, 0)),
    ((3, 0), (2, 0)),
    ((2, 1), (3, 1)),
)
GUEST_MOVES = (
    ((1, 0), (0, 1)),
    ((0, 1), (1, 0)),
    ((3, 0), (2, 1)),
    ((2, 1), (3, 0)),
)


def column_pairs(moves, chips, seqs, back=False):
    pairs = []
    for chip in range(chips):
        for source, target in moves:
            if back:
                source, target = target, source
            pairs.append(
                ((chip * 2 + source[1]) * seqs + source[0], (chip * 2 + target[1]) * seqs + target[0])
            )
    return pairs


def block_table():
    table = [[0, 0] for _ in range(8)]
    for place, moves in enumerate((FIRST_MOVES, SECOND_MOVES)):
        for (source, _), (target, core) in moves:
            table[target * 2 + core][place] = source
    return table


def nt(left, right):
    return lax.dot_general(left, right, (((1,), (1,)), ((), ())), preferred_element_type=jnp.float32)


def nn(left, right):
    return lax.dot_general(left, right, (((1,), (0,)), ((), ())), preferred_element_type=jnp.float32)


def tn(left, right):
    return lax.dot_general(left, right, (((0,), (0,)), ((), ())), preferred_element_type=jnp.float32)


def gather_matrix(sizes, capacity, rows):
    total = len(sizes) * capacity
    slot = lax.broadcasted_iota(jnp.int32, (1, total), 1)
    limit = jnp.zeros((1, total), jnp.int32)
    shift = jnp.zeros((1, total), jnp.int32)
    start = 0
    for block, size in enumerate(sizes):
        later = slot >= block * capacity
        limit = jnp.where(later, block * capacity + size, limit)
        shift = jnp.where(later, start - block * capacity, shift)
        start = start + size
    rank = jnp.where(slot < limit, slot + shift, -1)
    row = lax.broadcasted_iota(jnp.int32, (rows, total), 0)
    return jnp.where(row == rank, 1.0, 0.0).astype(jnp.bfloat16)


def layer_norm_kernel(places, inputs, ln_gain, freqs, normed):
    rows, features = inputs.shape
    place = jnp.broadcast_to(places[...].astype(jnp.float32), (rows, rows)).T
    angle = jnp.concatenate([place] * (features // 2 // rows), axis=1) * freqs[...]
    shifted = inputs[...].astype(jnp.float32) + jnp.concatenate([jnp.sin(angle), jnp.cos(angle)], axis=1)
    centred = shifted - jnp.mean(shifted, axis=1, keepdims=True)
    inv_std = lax.rsqrt(jnp.mean(centred * centred, axis=1, keepdims=True) + EPSILON)
    normed[...] = (centred * inv_std * ln_gain[...]).astype(normed.dtype)


def lift_kernel(info, g0, g1, g2, g3, weight_out, gathered, lifted, rows_g):
    capacity = g0.shape[0]
    matrix = gather_matrix([info[block] for block in range(4)], capacity, gathered.shape[0])
    for block, source in enumerate((g0, g1, g2, g3)):
        rows_g[pl.ds(block * capacity, capacity), :] = source[...]
    gathered[...] = nn(matrix, rows_g[...]).astype(gathered.dtype)
    lifted[...] = nn(gathered[...], weight_out[...]).T.astype(lifted.dtype)


def weight_kernel(place, w_out, w_qkv, own_out, own_qkv, pair_qkv, sems):
    width = own_out.shape[1]
    group = pl.multiple_of(place[0] * width, width)
    pair = pl.multiple_of((place[0] >> 1) * 2 * width, 2 * width)
    copies = [pltpu.make_async_copy(w_out.at[:, pl.ds(group, width)], own_out, sems.at[3])]
    for part in range(3):
        copies.append(
            pltpu.make_async_copy(
                w_qkv.at[part, pl.ds(group, width), :],
                own_qkv.at[pl.ds(part * width, width), :],
                sems.at[part],
            )
        )
        copies.append(
            pltpu.make_async_copy(
                w_qkv.at[part, pl.ds(pair, 2 * width), :],
                pair_qkv.at[pl.ds(part * 2 * width, 2 * width), :],
                sems.at[4 + part],
            )
        )
    for copy in copies:
        copy.start()
    for copy in copies:
        copy.wait()


def main_kernel(
    info, t0, t1, t2, t3, gathered_g, lifted, weight,
    x_send, x_keep, y_send, y_keep, grads,
    rows_t, gathered_t, query, key, value, stack,
):
    capacity = t0.shape[0]
    width = lifted.shape[0]
    lanes = width // 2
    low = jnp.bfloat16
    scale = HEAD_DIM ** (-0.5)

    matrix = gather_matrix([info[block] for block in range(4)], capacity, gathered_t.shape[0])
    for block, source in enumerate((t0, t1, t2, t3)):
        rows_t[pl.ds(block * capacity, capacity), :] = source[...]
    gathered_t[...] = nn(matrix, rows_t[...]).astype(low)
    query[...] = (nt(weight[0:width, :], gathered_t[...]).astype(low) * scale).astype(low)
    key[...] = nt(weight[width : 2 * width, :], gathered_t[...]).astype(low)
    value[...] = nt(weight[2 * width : 3 * width, :], gathered_t[...]).astype(low)

    heads = []
    for head in range(width // HEAD_DIM):
        span = pl.ds(head * HEAD_DIM, HEAD_DIM)
        rows_h = query[span, :], key[span, :], value[span, :], lifted[span, :]
        heads.append(rows_h + (tn(rows_h[1], rows_h[0]), tn(rows_h[2], rows_h[3])))
    weighted = []
    for _, _, _, _, scores, _ in heads:
        expo = jnp.exp(scores - jnp.max(scores, axis=0, keepdims=True))
        probs = expo * (1.0 / jnp.sum(expo, axis=0, keepdims=True))
        weighted.append((probs, probs.astype(low)))
    for head, (query_h, key_h, value_h, lifted_h, _, prob_grad) in enumerate(heads):
        probs, probs_low = weighted[head]
        spans = [pl.ds(part * width + head * HEAD_DIM, HEAD_DIM) for part in range(4)]
        attended = nn(value_h, probs_low)
        delta = jnp.sum(lifted_h.astype(jnp.float32) * attended, axis=0, keepdims=True)
        score_grad = (probs * (prob_grad - delta)).astype(low)
        stack[spans[0], :] = (nn(key_h, score_grad) * scale).astype(low)
        stack[spans[1], :] = nt(query_h, score_grad).astype(low)
        stack[spans[2], :] = nt(lifted_h, probs_low).astype(low)
        stack[spans[3], :] = attended.astype(low)

    grads[...] = stack[0 : 3 * width, :]
    for slot_y, slot_x in ((0, 0), (1, 0), (0, 1), (1, 1)):
        block = (info[5] ^ slot_y) * 2 + (info[6] ^ slot_x)
        cols = pl.ds(pl.multiple_of(block * width, width), width)
        term_t = nn(stack[0 : 3 * width, :], gathered_t[:, cols])
        term_g = nn(stack[3 * width : 4 * width, :], gathered_g[:, cols]).T
        x_target = x_send if slot_x else x_keep
        y_target = y_send if slot_y else y_keep
        for side in range(2):
            across = slice(side * lanes, (side + 1) * lanes)
            spot = info[7] ^ side
            x_target[slot_y, spot, :, :] = term_t[0 : 2 * width, across].astype(x_target.dtype)
            y_target[slot_x, spot, 0:width, :] = term_t[2 * width : 3 * width, across].astype(y_target.dtype)
            for part in range(2):
                y_target[slot_x, spot, width + part * lanes : width + (part + 1) * lanes, :] = term_g[
                    across, part * lanes : (part + 1) * lanes
                ].astype(y_target.dtype)


def normed_kernel(info, own, other, weight, back_one, back_two):
    width = own.shape[0] // 3
    rows = own.shape[1]
    capacity = back_one.shape[0]
    core = info[4] & 1
    half = 2 * capacity
    mine = gather_matrix([info[block] for block in range(4)], capacity, rows)[:, 0:half]
    theirs = gather_matrix([info[(block + 2) % 4] for block in range(4)], capacity, rows)[:, half:]
    own_grads = nn(own[...], mine).astype(own.dtype)
    other_grads = nn(other[...], theirs).astype(own.dtype)
    total = jnp.zeros((half, weight.shape[1]), jnp.float32)
    for part in range(3):
        span = slice(part * width, (part + 1) * width)
        for grads, spot in ((own_grads, core), (other_grads, 1 - core)):
            place = pl.ds(pl.multiple_of((part * 2 + spot) * width, width), width)
            total = total + tn(grads[span, :], weight[place, :])
    back_one[...] = total[0:capacity].astype(back_one.dtype)
    back_two[...] = total[capacity:half].astype(back_two.dtype)


def sum_kernel(x_part, y_part, x_second, y_second, home_send, guest_send, own):
    half = x_part.shape[1]
    for rows, part, second in ((0, x_part, x_second), (half, y_part, y_second)):
        span = pl.ds(rows, half)
        home_send[span, :] = (part[0] + second[0].astype(part.dtype)).astype(home_send.dtype)
        total = part[1] + second[1].astype(part.dtype)
        guest_send[span, :] = total.astype(guest_send.dtype)
        own[span, :] = total


def final_kernel(guest, from_home, from_guest, own, grad_qkv, grad_out, *, factor):
    rows, lanes = grad_qkv.shape

    def finish(low_row, high_row):
        span = slice(low_row, high_row)
        rest = jnp.where(guest[0] == 0, own[span, :], from_guest[span, :].astype(jnp.float32))
        return (from_home[span, :].astype(jnp.float32) + rest) * factor

    grad_qkv[...] = finish(0, rows)
    grad_out[:, 0:lanes] = finish(rows, rows + lanes)
    grad_out[:, lanes : 2 * lanes] = finish(rows + lanes, rows + 2 * lanes)


def specs(space, count):
    return [pl.BlockSpec(memory_space=space)] * count


VMEM_BYTES = 50 * 1024 * 1024
MAIN_BYTES = 28 * 1024 * 1024
FULL_BYTES = 60 * 1024 * 1024


def column_shards(tokens, positions, counts, ln_gain, w_qkv, w_out, d_out):
    low, wide = jnp.bfloat16, jnp.float32
    inputs = tokens[0]
    upstream = d_out[0]
    capacity, features = inputs.shape
    seqs = lax.axis_size("seq")
    chips = lax.axis_size("dp") // 2
    seat = lax.axis_index("seq")
    dp = lax.axis_index("dp")
    core, place_x, place_y = dp & 1, (dp >> 1) & 1, dp >> 2
    total = seqs * capacity
    half = total // 2
    width = features // seqs
    lanes = width // 2
    factor = 1.0 / math.sqrt(lax.axis_size("dp") * (3 * total // 4))
    guest = core ^ (seat & 1)
    resident = guest == 0

    axes = ("dp", "seq")
    first = column_pairs(FIRST_MOVES, chips, seqs)
    second = column_pairs(SECOND_MOVES, chips, seqs)
    first_back = column_pairs(FIRST_MOVES, chips, seqs, True)
    home = column_pairs(HOME_MOVES, chips, seqs)
    guests = column_pairs(GUEST_MOVES, chips, seqs)

    def across(array, bit):
        return lax.ppermute(array, "dp", [(i, i ^ bit) for i in range(2 * chips)])

    def fetch(array):
        two = lax.ppermute(array, axes, second)
        return lax.ppermute(array, axes, first), two

    def share(pair):
        return pair + (across(pair[0], 1), across(pair[1], 1))

    group = (seat >> 1) * 2 + core
    place = jnp.stack([group, place_y, place_x, core ^ 1 ^ guest]).astype(jnp.int32)
    params = pltpu.CompilerParams(vmem_limit_bytes=VMEM_BYTES)
    smem = specs(pltpu.SMEM, 1)

    fetched_g = fetch(upstream)
    other_counts = across(counts[0], 1)
    steps = np.arange(features // 2, dtype=np.float32) * np.float32(-math.log(10000.0) / (features // 2))
    normed = pl.pallas_call(
        layer_norm_kernel,
        out_shape=jax.ShapeDtypeStruct((capacity, features), low),
        in_specs=specs(pltpu.VMEM, 4),
        out_specs=pl.BlockSpec(memory_space=pltpu.VMEM),
        compiler_params=pltpu.CompilerParams(vmem_limit_bytes=FULL_BYTES),
    )(positions, inputs, ln_gain[None], jnp.asarray(np.exp(steps)[None]))
    fetched_t = fetch(normed)
    own_out, own_qkv, pair_qkv = pl.pallas_call(
        weight_kernel,
        out_shape=(
            jax.ShapeDtypeStruct((features, width), low),
            jax.ShapeDtypeStruct((3 * width, features), low),
            jax.ShapeDtypeStruct((6 * width, features), low),
        ),
        in_specs=smem + specs(pl.ANY, 2),
        out_specs=specs(pltpu.VMEM, 3),
        scratch_shapes=[pltpu.SemaphoreType.DMA((7,))],
        compiler_params=params,
        cost_estimate=pl.CostEstimate(flops=0, bytes_accessed=4 * 1024 * 1024, transcendentals=0),
    )(place, w_out, w_qkv)
    own_valid = jnp.arange(capacity, dtype=jnp.int32) < lax.dynamic_index_in_dim(counts[0], seat, 0, False)
    masked_grad = jnp.where(own_valid[:, None], upstream, jnp.zeros_like(upstream))

    sizes = jnp.where(resident, counts[0], other_counts)
    table = jnp.array(block_table(), jnp.int32)
    order = jnp.concatenate([table[seat * 2 + core], table[seat * 2 + 1 - core]])
    info = jnp.concatenate([sizes[order], place])

    fetched_g, info, own_out, own_qkv, masked_grad = lax.optimization_barrier(
        (fetched_g, info, own_out, own_qkv, masked_grad)
    )
    blocks_g = share(fetched_g)
    fetched_t, blocks_g = lax.optimization_barrier((fetched_t, blocks_g))
    rows = 3 * total // 4
    gathered_g, lifted = pl.pallas_call(
        lift_kernel,
        out_shape=(
            jax.ShapeDtypeStruct((rows, features), low),
            jax.ShapeDtypeStruct((width, rows), low),
        ),
        in_specs=smem + specs(pltpu.VMEM, 5),
        out_specs=specs(pltpu.VMEM, 2),
        scratch_shapes=[pltpu.VMEM((total, features), low)],
        compiler_params=pltpu.CompilerParams(vmem_limit_bytes=MAIN_BYTES),
        cost_estimate=pl.CostEstimate(
            flops=2 * rows * features * (width + total), bytes_accessed=3 * 1024 * 1024, transcendentals=0
        ),
    )(info, *blocks_g, own_out)
    blocks_t = share(fetched_t)

    send_shape = jax.ShapeDtypeStruct((2, 2, 2 * width, lanes), low)
    keep_shape = jax.ShapeDtypeStruct((2, 2, 2 * width, lanes), wide)
    grads_shape = jax.ShapeDtypeStruct((3 * width, rows), low)
    x_send, x_keep, y_send, y_keep, grads = pl.pallas_call(
        main_kernel,
        out_shape=(
            send_shape, keep_shape, send_shape, keep_shape, grads_shape
        ),
        in_specs=smem + specs(pltpu.VMEM, 7),
        out_specs=specs(pltpu.VMEM, 5),
        scratch_shapes=[
            pltpu.VMEM((total, features), low),
            pltpu.VMEM((rows, features), low),
            pltpu.VMEM((width, rows), low),
            pltpu.VMEM((width, rows), low),
            pltpu.VMEM((width, rows), low),
            pltpu.VMEM((4 * width, rows), low),
        ],
        compiler_params=pltpu.CompilerParams(vmem_limit_bytes=MAIN_BYTES),
        cost_estimate=pl.CostEstimate(
            flops=2 * total * features * width * 7 + 12 * 4 * total * total * HEAD_DIM,
            bytes_accessed=8 * 1024 * 1024,
            transcendentals=4 * total * total,
        ),
    )(info, *blocks_t, gathered_g, lifted, own_qkv)

    x_first, y_first = across(x_send, 2), across(y_send, 4)
    from_core = across(grads, 1)
    block_shape = jax.ShapeDtypeStruct((capacity, features), low)
    back_one, back_two = pl.pallas_call(
        normed_kernel,
        out_shape=(block_shape, block_shape),
        in_specs=smem + specs(pltpu.VMEM, 3),
        out_specs=specs(pltpu.VMEM, 2),
        compiler_params=pltpu.CompilerParams(vmem_limit_bytes=MAIN_BYTES),
        cost_estimate=pl.CostEstimate(
            flops=2 * total * features * width * 3, bytes_accessed=4 * 1024 * 1024, transcendentals=0
        ),
    )(info, grads, from_core, pair_qkv)
    places, back_one = lax.optimization_barrier((positions, back_one))
    _, standard, inv_std = layer_norm(inputs, places[0], ln_gain)
    home_one = lax.ppermute(back_one, axes, first_back)
    x_first, y_first, home_one, back_two = lax.optimization_barrier((x_first, y_first, home_one, back_two))
    home_two = lax.ppermute(back_two, axes, second)
    x_second = across((x_keep[1] + x_first[1].astype(wide)).astype(low), 4)
    y_second = across((y_keep[1] + y_first[1].astype(wide)).astype(low), 2)
    x_part = x_keep[0] + x_first[0].astype(wide)
    y_part = y_keep[0] + y_first[0].astype(wide)
    x_part, y_part = lax.optimization_barrier((x_part, y_part))
    home_send, guest_send, own = pl.pallas_call(
        sum_kernel,
        out_shape=(
            jax.ShapeDtypeStruct((4 * width, lanes), low),
            jax.ShapeDtypeStruct((4 * width, lanes), low),
            jax.ShapeDtypeStruct((4 * width, lanes), wide),
        ),
        in_specs=specs(pltpu.VMEM, 4),
        out_specs=specs(pltpu.VMEM, 3),
        compiler_params=pltpu.CompilerParams(vmem_limit_bytes=16 * 1024 * 1024),
        cost_estimate=pl.CostEstimate(flops=4 * width * 2 * lanes, bytes_accessed=2 * 1024 * 1024, transcendentals=0),
    )(x_part, y_part, x_second, y_second)
    from_home = lax.ppermute(home_send, axes, home)
    from_guest = lax.ppermute(guest_send, axes, guests)

    grad_qkv, grad_out = pl.pallas_call(
        functools.partial(final_kernel, factor=factor),
        out_shape=(
            jax.ShapeDtypeStruct((3 * width, lanes), wide),
            jax.ShapeDtypeStruct((lanes, width), wide),
        ),
        in_specs=smem + specs(pltpu.VMEM, 3),
        out_specs=specs(pltpu.VMEM, 2),
        compiler_params=pltpu.CompilerParams(vmem_limit_bytes=8 * 1024 * 1024),
    )(guest[None].astype(jnp.int32), from_home, from_guest, own)
    grad_qkv = grad_qkv.reshape(3, width, lanes)

    normed_grad = home_one.astype(wide) + home_two.astype(wide)
    unit_grad = normed_grad * ln_gain
    inner = unit_grad - jnp.mean(unit_grad, axis=1, keepdims=True)
    inner = inner - standard * jnp.mean(unit_grad * standard, axis=1, keepdims=True)
    d_inputs = (masked_grad.astype(wide) + inv_std * inner).astype(low)
    return (d_inputs[None], grad_qkv, grad_out)


def solution(mesh):
    fits = mesh.shape["dp"] == 8 and mesh.shape["seq"] == 4
    placed = (
        P("dp", "seq", None),
        P("dp", "seq"),
        P("dp", None),
        P(),
        P(),
        P(),
        P("dp", "seq", None),
    )
    return jax.shard_map(
        column_shards if fits else shards,
        mesh=mesh,
        in_specs=placed,
        out_specs=(P("dp", "seq", None), P(None, "seq", "dp"), P("dp", "seq")),
        check_vma=False,
    )
```

```python
import functools
import math

import jax
import jax.numpy as jnp
import numpy as np
from jax import lax
from jax.experimental import pallas as pl
from jax.experimental.pallas import tpu as pltpu
from jax.sharding import PartitionSpec as P

HEAD_DIM = 64


EPSILON = 1e-06
MASKED = -1e30


def position_code(places, feature_width):
    half = feature_width // 2
    freqs = jnp.exp(jnp.arange(half, dtype=jnp.float32) * (-math.log(10000.0) / half))
    angle = places.astype(jnp.float32)[:, None] * freqs[None, :]
    return jnp.concatenate([jnp.sin(angle), jnp.cos(angle)], axis=1)


def layer_norm(inputs, places, ln_gain):
    shifted = inputs.astype(jnp.float32) + position_code(places, inputs.shape[1])
    centred = shifted - jnp.mean(shifted, axis=1, keepdims=True)
    inv_std = lax.rsqrt(jnp.mean(centred * centred, axis=1, keepdims=True) + EPSILON)
    standard = centred * inv_std
    normed = (standard * ln_gain).astype(jnp.bfloat16)
    return (normed, standard, inv_std)


def input_grad(query_grad, key_grad, value_grad, masked_grad, w_qkv, standard, inv_std, ln_gain):
    normed_grad = jnp.dot(query_grad, w_qkv[0], preferred_element_type=jnp.float32)
    normed_grad = normed_grad + jnp.dot(key_grad, w_qkv[1], preferred_element_type=jnp.float32)
    normed_grad = normed_grad + jnp.dot(value_grad, w_qkv[2], preferred_element_type=jnp.float32)
    unit_grad = normed_grad * ln_gain
    inner = unit_grad - jnp.mean(unit_grad, axis=1, keepdims=True)
    inner = inner - standard * jnp.mean(unit_grad * standard, axis=1, keepdims=True)
    return (masked_grad.astype(jnp.float32) + inv_std * inner).astype(jnp.bfloat16)


def project(normed, weight):
    return jnp.einsum("td,od->to", normed, weight, preferred_element_type=jnp.float32).astype(
        jnp.bfloat16
    )


def token_sum(left, right):
    return lax.dot_general(
        left, right, (((0,), (0,)), ((), ())), preferred_element_type=jnp.float32
    )


def attention_grads(queries, key_rows, value_rows, attn_grad, key_valid, score_scale):
    total, span = queries.shape
    heads_here = span // HEAD_DIM
    block = math.gcd(512, total)
    blocks = total // block
    key_three = key_rows.reshape(total, heads_here, HEAD_DIM)
    value_three = value_rows.reshape(total, heads_here, HEAD_DIM)
    query_four = queries.reshape(blocks, block, heads_here, HEAD_DIM)
    grad_four = attn_grad.reshape(blocks, block, heads_here, HEAD_DIM)

    def step(carry, item):
        key_acc, value_acc = carry
        query_block, grad_block = item
        scores = (
            jnp.einsum("qhd,khd->hqk", query_block, key_three, preferred_element_type=jnp.float32)
            * score_scale
        )
        scores = jnp.where(key_valid[None, None, :], scores, MASKED)
        peak = jnp.max(scores, axis=2, keepdims=True)
        expo = jnp.exp(scores - peak)
        probs = expo / jnp.sum(expo, axis=2, keepdims=True)
        probs_low = probs.astype(jnp.bfloat16)
        attended = jnp.einsum(
            "hqk,khd->qhd", probs_low, value_three, preferred_element_type=jnp.float32
        )
        delta = jnp.sum(grad_block.astype(jnp.float32) * attended, axis=2)
        prob_grad = jnp.einsum(
            "qhd,khd->hqk", grad_block, value_three, preferred_element_type=jnp.float32
        )
        score_grad = (probs * (prob_grad - jnp.transpose(delta)[:, :, None])).astype(jnp.bfloat16)
        query_grad = jnp.einsum(
            "hqk,khd->qhd", score_grad, key_three, preferred_element_type=jnp.float32
        )
        query_grad = (query_grad * score_scale).astype(jnp.bfloat16)
        key_acc = key_acc + jnp.einsum(
            "hqk,qhd->khd", score_grad, query_block, preferred_element_type=jnp.float32
        )
        value_acc = value_acc + jnp.einsum(
            "hqk,qhd->khd", probs_low, grad_block, preferred_element_type=jnp.float32
        )
        return ((key_acc, value_acc), (attended.astype(jnp.bfloat16), query_grad))

    zeros_acc = jnp.zeros((total, heads_here, HEAD_DIM), jnp.float32)
    sums, outputs = lax.scan(step, (zeros_acc, zeros_acc), (query_four, grad_four))
    attended = outputs[0].reshape(total, span)
    query_grad = outputs[1].reshape(total, span)
    key_grad = (sums[0] * score_scale).astype(jnp.bfloat16).reshape(total, span)
    value_grad = sums[1].astype(jnp.bfloat16).reshape(total, span)
    return (attended, query_grad, key_grad, value_grad)


def shards(tokens, positions, counts, ln_gain, w_qkv, w_out, d_out):
    inputs = tokens[0]
    places = positions[0]
    upstream = d_out[0]
    capacity, feature_width = inputs.shape
    shard_total = lax.axis_size("seq")
    shard_index = lax.axis_index("seq")
    slot_count = capacity * shard_total
    key_valid = jnp.arange(slot_count, dtype=jnp.int32) % capacity < jnp.repeat(counts[0], capacity)
    own_valid = lax.dynamic_slice_in_dim(key_valid, shard_index * capacity, capacity)
    normed, standard, inv_std = layer_norm(inputs, places, ln_gain)
    masked_grad = jnp.where(own_valid[:, None], upstream, jnp.zeros_like(upstream))
    score_scale = HEAD_DIM ** (-0.5)
    factor = 1.0 / math.sqrt(lax.axis_size("dp") * (3 * slot_count // 4))
    head_width = feature_width // shard_total
    normed_all, grad_all = (
        lax.all_gather(normed, "seq", axis=0, tiled=True),
        lax.all_gather(masked_grad, "seq", axis=0, tiled=True),
    )
    local_qkv = lax.dynamic_slice_in_dim(w_qkv, shard_index * head_width, head_width, 1)
    local_out = lax.dynamic_slice_in_dim(w_out, shard_index * head_width, head_width, 1)
    queries = project(normed_all, local_qkv[0])
    key_rows = project(normed_all, local_qkv[1])
    value_rows = project(normed_all, local_qkv[2])
    attn_grad = jnp.dot(grad_all, local_out, preferred_element_type=jnp.float32).astype(
        jnp.bfloat16
    )
    attended, query_grad, key_grad, value_grad = attention_grads(
        queries, key_rows, value_rows, attn_grad, key_valid, score_scale
    )
    term_qkv = jnp.stack(
        [
            token_sum(query_grad, normed_all),
            token_sum(key_grad, normed_all),
            token_sum(value_grad, normed_all),
        ]
    )
    term_out = token_sum(grad_all, attended)
    grad_qkv, grad_out = (
        lax.psum_scatter(term_qkv, "dp", scatter_dimension=2, tiled=True),
        lax.psum_scatter(term_out, "dp", scatter_dimension=0, tiled=True),
    )
    query_rows, key_back, value_back = (
        lax.all_to_all(query_grad, "seq", split_axis=0, concat_axis=1, tiled=True),
        lax.all_to_all(key_grad, "seq", split_axis=0, concat_axis=1, tiled=True),
        lax.all_to_all(value_grad, "seq", split_axis=0, concat_axis=1, tiled=True),
    )
    d_inputs = input_grad(
        query_rows, key_back, value_back, masked_grad, w_qkv, standard, inv_std, ln_gain
    )
    return (d_inputs[None], grad_qkv * factor, grad_out * factor)


FIRST_MOVES = (
    ((0, 0), (2, 0)),
    ((1, 0), (0, 0)),
    ((2, 0), (0, 1)),
    ((3, 0), (2, 1)),
    ((0, 1), (1, 0)),
    ((1, 1), (3, 1)),
    ((2, 1), (3, 0)),
    ((3, 1), (1, 1)),
)
SECOND_MOVES = (
    ((0, 1), (3, 0)),
    ((3, 0), (0, 1)),
    ((1, 0), (2, 1)),
    ((2, 1), (1, 0)),
    ((0, 0), (0, 0)),
    ((1, 1), (1, 1)),
    ((2, 0), (2, 0)),
    ((3, 1), (3, 1)),
)
HOME_MOVES = (
    ((0, 0), (0, 1)),
    ((1, 1), (1, 0)),
    ((1, 0), (0, 0)),
    ((0, 1), (1, 1)),
    ((2, 0), (2, 1)),
    ((3, 1), (3, 0)),
    ((3, 0), (2, 0)),
    ((2, 1), (3, 1)),
)
GUEST_MOVES = (
    ((1, 0), (0, 1)),
    ((0, 1), (1, 0)),
    ((3, 0), (2, 1)),
    ((2, 1), (3, 0)),
)


def column_pairs(moves, chips, seqs, back=False):
    pairs = []
    for chip in range(chips):
        for source, target in moves:
            if back:
                source, target = target, source
            pairs.append(
                ((chip * 2 + source[1]) * seqs + source[0], (chip * 2 + target[1]) * seqs + target[0])
            )
    return pairs


def block_table():
    table = [[0, 0] for _ in range(8)]
    for place, moves in enumerate((FIRST_MOVES, SECOND_MOVES)):
        for (source, _), (target, core) in moves:
            table[target * 2 + core][place] = source
    return table


def nt(left, right):
    return lax.dot_general(left, right, (((1,), (1,)), ((), ())), preferred_element_type=jnp.float32)


def nn(left, right):
    return lax.dot_general(left, right, (((1,), (0,)), ((), ())), preferred_element_type=jnp.float32)


def tn(left, right):
    return lax.dot_general(left, right, (((0,), (0,)), ((), ())), preferred_element_type=jnp.float32)


def seats():
    seat, dp = lax.axis_index("seq"), lax.axis_index("dp")
    core = dp & 1
    return (seat >> 1) * 2 + core, core, core ^ (seat & 1), dp >> 2, (dp >> 1) & 1


def gather_matrix(rank, rows):
    row = lax.broadcasted_iota(jnp.int32, (rows, rank.shape[1]), 0)
    return jnp.where(row == rank[...], 1.0, 0.0).astype(jnp.bfloat16)


def layer_norm_kernel(places, inputs, ln_gain, freqs, normed):
    rows, features = inputs.shape
    place = jnp.broadcast_to(places[...].astype(jnp.float32), (rows, rows)).T
    angle = jnp.concatenate([place] * (features // 2 // rows), axis=1) * freqs[...]
    shifted = inputs[...].astype(jnp.float32) + jnp.concatenate([jnp.sin(angle), jnp.cos(angle)], axis=1)
    centred = shifted - jnp.mean(shifted, axis=1, keepdims=True)
    inv_std = lax.rsqrt(jnp.mean(centred * centred, axis=1, keepdims=True) + EPSILON)
    normed[...] = (centred * inv_std * ln_gain[...]).astype(normed.dtype)


def slot_kernel(counts, other_counts, table, upstream, rank, own_rank, other_rank, masked):
    capacity = upstream.shape[0]
    half = own_rank.shape[1]
    seat = lax.axis_index("seq")
    _, core, guest, _, _ = seats()
    sizes = []
    for block in range(rank.shape[1] // capacity):
        holder = core if block < 2 else 1 - core
        source = table[(seat * 2 + holder) * 2 + block % 2]
        sizes.append(jnp.where(guest == 0, counts[source], other_counts[source]))
    slot = lax.broadcasted_iota(jnp.int32, rank.shape, 1)
    limit = jnp.zeros(rank.shape, jnp.int32)
    shift = jnp.zeros(rank.shape, jnp.int32)
    start = 0
    for block, size in enumerate(sizes):
        later = slot >= block * capacity
        limit = jnp.where(later, block * capacity + size, limit)
        shift = jnp.where(later, start - block * capacity, shift)
        start = start + size
    here = jnp.where(slot < limit, slot + shift, -1)
    rank[...] = here
    here = here[:, 0:half]
    own_rank[...] = here
    other_rank[...] = jnp.where(here >= 0, here + sizes[2] + sizes[3], -1)
    row = lax.broadcasted_iota(jnp.int32, (capacity, 1), 0)
    rows = upstream[...].astype(jnp.float32)
    masked[...] = jnp.where(row < counts[seat], rows, 0.0).astype(masked.dtype)


def lift_kernel(rank, g0, g1, g2, g3, weight_out, gathered, lifted, rows_g):
    capacity = g0.shape[0]
    matrix = gather_matrix(rank, gathered.shape[0])
    for block, source in enumerate((g0, g1, g2, g3)):
        rows_g[pl.ds(block * capacity, capacity), :] = source[...]
    gathered[...] = nn(matrix, rows_g[...]).astype(gathered.dtype)
    lifted[...] = nn(gathered[...], weight_out[...]).T.astype(lifted.dtype)


def weight_kernel(w_out, w_qkv, own_out, own_qkv, pair_qkv, sems):
    width = own_out.shape[1]
    head_group = seats()[0]
    group = pl.multiple_of(head_group * width, width)
    pair = pl.multiple_of((head_group >> 1) * 2 * width, 2 * width)
    copies = [pltpu.make_async_copy(w_out.at[:, pl.ds(group, width)], own_out, sems.at[3])]
    for part in range(3):
        copies.append(
            pltpu.make_async_copy(
                w_qkv.at[part, pl.ds(group, width), :],
                own_qkv.at[pl.ds(part * width, width), :],
                sems.at[part],
            )
        )
        copies.append(
            pltpu.make_async_copy(
                w_qkv.at[part, pl.ds(pair, 2 * width), :],
                pair_qkv.at[pl.ds(part * 2 * width, 2 * width), :],
                sems.at[4 + part],
            )
        )
    for copy in copies:
        copy.start()
    for copy in copies:
        copy.wait()


def main_kernel(
    rank, t0, t1, t2, t3, gathered_g, lifted, weight,
    x_send, x_keep, y_send, y_keep, grads,
    rows_t, gathered_t, query, key, value, stack,
):
    capacity = t0.shape[0]
    width = lifted.shape[0]
    lanes = width // 2
    low = jnp.bfloat16
    scale = HEAD_DIM ** (-0.5)

    _, core, guest, place_y, place_x = seats()
    matrix = gather_matrix(rank, gathered_t.shape[0])
    for block, source in enumerate((t0, t1, t2, t3)):
        rows_t[pl.ds(block * capacity, capacity), :] = source[...]
    gathered_t[...] = nn(matrix, rows_t[...]).astype(low)
    query[...] = (nt(weight[0:width, :], gathered_t[...]).astype(low) * scale).astype(low)
    key[...] = nt(weight[width : 2 * width, :], gathered_t[...]).astype(low)
    value[...] = nt(weight[2 * width : 3 * width, :], gathered_t[...]).astype(low)

    heads = []
    for head in range(width // HEAD_DIM):
        span = pl.ds(head * HEAD_DIM, HEAD_DIM)
        rows_h = query[span, :], key[span, :], value[span, :], lifted[span, :]
        heads.append(rows_h + (tn(rows_h[1], rows_h[0]), tn(rows_h[2], rows_h[3])))
    weighted = []
    for _, _, _, _, scores, _ in heads:
        expo = jnp.exp(scores - jnp.max(scores, axis=0, keepdims=True))
        probs = expo * (1.0 / jnp.sum(expo, axis=0, keepdims=True))
        weighted.append((probs, probs.astype(low)))
    for head, (query_h, key_h, value_h, lifted_h, _, prob_grad) in enumerate(heads):
        probs, probs_low = weighted[head]
        spans = [pl.ds(part * width + head * HEAD_DIM, HEAD_DIM) for part in range(4)]
        attended = nn(value_h, probs_low)
        delta = jnp.sum(lifted_h.astype(jnp.float32) * attended, axis=0, keepdims=True)
        score_grad = (probs * (prob_grad - delta)).astype(low)
        stack[spans[0], :] = (nn(key_h, score_grad) * scale).astype(low)
        stack[spans[1], :] = nt(query_h, score_grad).astype(low)
        stack[spans[2], :] = nt(lifted_h, probs_low).astype(low)
        stack[spans[3], :] = attended.astype(low)

    grads[...] = stack[0 : 3 * width, :]
    for slot_y, slot_x in ((0, 0), (1, 0), (0, 1), (1, 1)):
        block = (place_y ^ slot_y) * 2 + (place_x ^ slot_x)
        cols = pl.ds(pl.multiple_of(block * width, width), width)
        term_t = nn(stack[0 : 3 * width, :], gathered_t[:, cols])
        term_g = nn(stack[3 * width : 4 * width, :], gathered_g[:, cols]).T
        x_target = x_send if slot_x else x_keep
        y_target = y_send if slot_y else y_keep
        for side in range(2):
            across = slice(side * lanes, (side + 1) * lanes)
            spot = core ^ 1 ^ guest ^ side
            x_target[slot_y, spot, :, :] = term_t[0 : 2 * width, across].astype(x_target.dtype)
            y_target[slot_x, spot, 0:width, :] = term_t[2 * width : 3 * width, across].astype(y_target.dtype)
            for part in range(2):
                y_target[slot_x, spot, width + part * lanes : width + (part + 1) * lanes, :] = term_g[
                    across, part * lanes : (part + 1) * lanes
                ].astype(y_target.dtype)


def normed_kernel(own_rank, other_rank, own, other, weight, back_one, back_two):
    width = own.shape[0] // 3
    rows = own.shape[1]
    capacity = back_one.shape[0]
    core = seats()[1]
    half = 2 * capacity
    mine = gather_matrix(own_rank, rows)
    theirs = gather_matrix(other_rank, rows)
    own_grads = nn(own[...], mine).astype(own.dtype)
    other_grads = nn(other[...], theirs).astype(own.dtype)
    total = jnp.zeros((half, weight.shape[1]), jnp.float32)
    for part in range(3):
        span = slice(part * width, (part + 1) * width)
        for grads, spot in ((own_grads, core), (other_grads, 1 - core)):
            place = pl.ds(pl.multiple_of((part * 2 + spot) * width, width), width)
            total = total + tn(grads[span, :], weight[place, :])
    back_one[...] = total[0:capacity].astype(back_one.dtype)
    back_two[...] = total[capacity:half].astype(back_two.dtype)


def sum_kernel(x_part, y_part, x_second, y_second, home_send, guest_send, own):
    half = x_part.shape[1]
    for rows, part, second in ((0, x_part, x_second), (half, y_part, y_second)):
        span = pl.ds(rows, half)
        home_send[span, :] = (part[0] + second[0].astype(part.dtype)).astype(home_send.dtype)
        total = part[1] + second[1].astype(part.dtype)
        guest_send[span, :] = total.astype(guest_send.dtype)
        own[span, :] = total


def final_kernel(from_home, from_guest, own, grad_qkv, grad_out, *, factor):
    rows, lanes = grad_qkv.shape
    guest = seats()[2]

    def finish(low_row, high_row):
        span = slice(low_row, high_row)
        rest = jnp.where(guest == 0, own[span, :], from_guest[span, :].astype(jnp.float32))
        return (from_home[span, :].astype(jnp.float32) + rest) * factor

    grad_qkv[...] = finish(0, rows)
    grad_out[:, 0:lanes] = finish(rows, rows + lanes)
    grad_out[:, lanes : 2 * lanes] = finish(rows + lanes, rows + 2 * lanes)


def specs(space, count):
    return [pl.BlockSpec(memory_space=space)] * count


VMEM_BYTES = 50 * 1024 * 1024
MAIN_BYTES = 28 * 1024 * 1024
FULL_BYTES = 60 * 1024 * 1024


def column_shards(tokens, positions, counts, ln_gain, w_qkv, w_out, d_out):
    low, wide = jnp.bfloat16, jnp.float32
    inputs = tokens[0]
    upstream = d_out[0]
    capacity, features = inputs.shape
    seqs = lax.axis_size("seq")
    chips = lax.axis_size("dp") // 2
    seat = lax.axis_index("seq")
    dp = lax.axis_index("dp")
    core = dp & 1
    total = seqs * capacity
    half = total // 2
    width = features // seqs
    lanes = width // 2
    factor = 1.0 / math.sqrt(lax.axis_size("dp") * (3 * total // 4))

    axes = ("dp", "seq")
    first = column_pairs(FIRST_MOVES, chips, seqs)
    second = column_pairs(SECOND_MOVES, chips, seqs)
    first_back = column_pairs(FIRST_MOVES, chips, seqs, True)
    home = column_pairs(HOME_MOVES, chips, seqs)
    guests = column_pairs(GUEST_MOVES, chips, seqs)

    def across(array, bit):
        return lax.ppermute(array, "dp", [(i, i ^ bit) for i in range(2 * chips)])

    def fetch(array):
        two = lax.ppermute(array, axes, second)
        return lax.ppermute(array, axes, first), two

    def share(pair):
        return pair + (across(pair[0], 1), across(pair[1], 1))

    params = pltpu.CompilerParams(vmem_limit_bytes=VMEM_BYTES)

    fetched_g = fetch(upstream)
    other_counts = across(counts[0], 1)
    steps = np.arange(features // 2, dtype=np.float32) * np.float32(-math.log(10000.0) / (features // 2))
    normed = pl.pallas_call(
        layer_norm_kernel,
        out_shape=jax.ShapeDtypeStruct((capacity, features), low),
        in_specs=specs(pltpu.VMEM, 4),
        out_specs=pl.BlockSpec(memory_space=pltpu.VMEM),
        compiler_params=pltpu.CompilerParams(vmem_limit_bytes=FULL_BYTES),
    )(positions, inputs, ln_gain[None], jnp.asarray(np.exp(steps)[None]))
    fetched_t = fetch(normed)
    own_out, own_qkv, pair_qkv = pl.pallas_call(
        weight_kernel,
        out_shape=(
            jax.ShapeDtypeStruct((features, width), low),
            jax.ShapeDtypeStruct((3 * width, features), low),
            jax.ShapeDtypeStruct((6 * width, features), low),
        ),
        in_specs=specs(pl.ANY, 2),
        out_specs=specs(pltpu.VMEM, 3),
        scratch_shapes=[pltpu.SemaphoreType.DMA((7,))],
        compiler_params=params,
        cost_estimate=pl.CostEstimate(flops=0, bytes_accessed=4 * 1024 * 1024, transcendentals=0),
    )(w_out, w_qkv)
    table = [block for pair in block_table() for block in pair]
    rank, own_rank, other_rank, masked_grad = pl.pallas_call(
        slot_kernel,
        out_shape=(
            jax.ShapeDtypeStruct((1, total), jnp.int32),
            jax.ShapeDtypeStruct((1, half), jnp.int32),
            jax.ShapeDtypeStruct((1, half), jnp.int32),
            jax.ShapeDtypeStruct((capacity, features), low),
        ),
        in_specs=specs(pltpu.SMEM, 3) + specs(pltpu.VMEM, 1),
        out_specs=specs(pltpu.VMEM, 4),
        compiler_params=pltpu.CompilerParams(vmem_limit_bytes=MAIN_BYTES),
    )(counts[0], other_counts, jnp.array(table, jnp.int32), upstream)

    fetched_g, rank, own_rank, other_rank, own_out, own_qkv, masked_grad = lax.optimization_barrier(
        (fetched_g, rank, own_rank, other_rank, own_out, own_qkv, masked_grad)
    )
    blocks_g = share(fetched_g)
    fetched_t, blocks_g = lax.optimization_barrier((fetched_t, blocks_g))
    rows = 3 * total // 4
    gathered_g, lifted = pl.pallas_call(
        lift_kernel,
        out_shape=(
            jax.ShapeDtypeStruct((rows, features), low),
            jax.ShapeDtypeStruct((width, rows), low),
        ),
        in_specs=specs(pltpu.VMEM, 6),
        out_specs=specs(pltpu.VMEM, 2),
        scratch_shapes=[pltpu.VMEM((total, features), low)],
        compiler_params=pltpu.CompilerParams(vmem_limit_bytes=MAIN_BYTES),
        cost_estimate=pl.CostEstimate(
            flops=2 * rows * features * (width + total), bytes_accessed=3 * 1024 * 1024, transcendentals=0
        ),
    )(rank, *blocks_g, own_out)
    blocks_t = share(fetched_t)

    send_shape = jax.ShapeDtypeStruct((2, 2, 2 * width, lanes), low)
    keep_shape = jax.ShapeDtypeStruct((2, 2, 2 * width, lanes), wide)
    grads_shape = jax.ShapeDtypeStruct((3 * width, rows), low)
    x_send, x_keep, y_send, y_keep, grads = pl.pallas_call(
        main_kernel,
        out_shape=(
            send_shape, keep_shape, send_shape, keep_shape, grads_shape
        ),
        in_specs=specs(pltpu.VMEM, 8),
        out_specs=specs(pltpu.VMEM, 5),
        scratch_shapes=[
            pltpu.VMEM((total, features), low),
            pltpu.VMEM((rows, features), low),
            pltpu.VMEM((width, rows), low),
            pltpu.VMEM((width, rows), low),
            pltpu.VMEM((width, rows), low),
            pltpu.VMEM((4 * width, rows), low),
        ],
        compiler_params=pltpu.CompilerParams(vmem_limit_bytes=MAIN_BYTES),
        cost_estimate=pl.CostEstimate(
            flops=2 * total * features * width * 7 + 12 * 4 * total * total * HEAD_DIM,
            bytes_accessed=8 * 1024 * 1024,
            transcendentals=4 * total * total,
        ),
    )(rank, *blocks_t, gathered_g, lifted, own_qkv)

    x_first, y_first = across(x_send, 2), across(y_send, 4)
    from_core = across(grads, 1)
    block_shape = jax.ShapeDtypeStruct((capacity, features), low)
    back_one, back_two = pl.pallas_call(
        normed_kernel,
        out_shape=(block_shape, block_shape),
        in_specs=specs(pltpu.VMEM, 5),
        out_specs=specs(pltpu.VMEM, 2),
        compiler_params=pltpu.CompilerParams(vmem_limit_bytes=MAIN_BYTES),
        cost_estimate=pl.CostEstimate(
            flops=2 * total * features * width * 3, bytes_accessed=4 * 1024 * 1024, transcendentals=0
        ),
    )(own_rank, other_rank, grads, from_core, pair_qkv)
    places, back_one = lax.optimization_barrier((positions, back_one))
    _, standard, inv_std = layer_norm(inputs, places[0], ln_gain)
    home_one = lax.ppermute(back_one, axes, first_back)
    x_first, y_first, home_one, back_two = lax.optimization_barrier((x_first, y_first, home_one, back_two))
    home_two = lax.ppermute(back_two, axes, second)
    x_second = across((x_keep[1] + x_first[1].astype(wide)).astype(low), 4)
    y_second = across((y_keep[1] + y_first[1].astype(wide)).astype(low), 2)
    x_part = x_keep[0] + x_first[0].astype(wide)
    y_part = y_keep[0] + y_first[0].astype(wide)
    x_part, y_part = lax.optimization_barrier((x_part, y_part))
    home_send, guest_send, own = pl.pallas_call(
        sum_kernel,
        out_shape=(
            jax.ShapeDtypeStruct((4 * width, lanes), low),
            jax.ShapeDtypeStruct((4 * width, lanes), low),
            jax.ShapeDtypeStruct((4 * width, lanes), wide),
        ),
        in_specs=specs(pltpu.VMEM, 4),
        out_specs=specs(pltpu.VMEM, 3),
        compiler_params=pltpu.CompilerParams(vmem_limit_bytes=16 * 1024 * 1024),
        cost_estimate=pl.CostEstimate(flops=4 * width * 2 * lanes, bytes_accessed=2 * 1024 * 1024, transcendentals=0),
    )(x_part, y_part, x_second, y_second)
    from_home = lax.ppermute(home_send, axes, home)
    from_guest = lax.ppermute(guest_send, axes, guests)

    grad_qkv, grad_out = pl.pallas_call(
        functools.partial(final_kernel, factor=factor),
        out_shape=(
            jax.ShapeDtypeStruct((3 * width, lanes), wide),
            jax.ShapeDtypeStruct((lanes, width), wide),
        ),
        in_specs=specs(pltpu.VMEM, 3),
        out_specs=specs(pltpu.VMEM, 2),
        compiler_params=pltpu.CompilerParams(vmem_limit_bytes=8 * 1024 * 1024),
    )(from_home, from_guest, own)
    grad_qkv = grad_qkv.reshape(3, width, lanes)

    normed_grad = home_one.astype(wide) + home_two.astype(wide)
    unit_grad = normed_grad * ln_gain
    inner = unit_grad - jnp.mean(unit_grad, axis=1, keepdims=True)
    inner = inner - standard * jnp.mean(unit_grad * standard, axis=1, keepdims=True)
    d_inputs = (masked_grad.astype(wide) + inv_std * inner).astype(low)
    return (d_inputs[None], grad_qkv, grad_out)


def solution(mesh):
    fits = mesh.shape["dp"] == 8 and mesh.shape["seq"] == 4
    placed = (
        P("dp", "seq", None),
        P("dp", "seq"),
        P("dp", None),
        P(),
        P(),
        P(),
        P("dp", "seq", None),
    )
    return jax.shard_map(
        column_shards if fits else shards,
        mesh=mesh,
        in_specs=placed,
        out_specs=(P("dp", "seq", None), P(None, "seq", "dp"), P("dp", "seq")),
        check_vma=False,
    )
```

```python
import functools
import math

import jax
import jax.numpy as jnp
import numpy as np
from jax import lax
from jax.experimental import pallas as pl
from jax.experimental.pallas import tpu as pltpu
from jax.sharding import PartitionSpec as P

HEAD_DIM = 64


EPSILON = 1e-06
MASKED = -1e30


def position_code(places, feature_width):
    half = feature_width // 2
    freqs = jnp.exp(jnp.arange(half, dtype=jnp.float32) * (-math.log(10000.0) / half))
    angle = places.astype(jnp.float32)[:, None] * freqs[None, :]
    return jnp.concatenate([jnp.sin(angle), jnp.cos(angle)], axis=1)


def layer_norm(inputs, places, ln_gain):
    shifted = inputs.astype(jnp.float32) + position_code(places, inputs.shape[1])
    centred = shifted - jnp.mean(shifted, axis=1, keepdims=True)
    inv_std = lax.rsqrt(jnp.mean(centred * centred, axis=1, keepdims=True) + EPSILON)
    standard = centred * inv_std
    normed = (standard * ln_gain).astype(jnp.bfloat16)
    return (normed, standard, inv_std)


def input_grad(query_grad, key_grad, value_grad, masked_grad, w_qkv, standard, inv_std, ln_gain):
    normed_grad = jnp.dot(query_grad, w_qkv[0], preferred_element_type=jnp.float32)
    normed_grad = normed_grad + jnp.dot(key_grad, w_qkv[1], preferred_element_type=jnp.float32)
    normed_grad = normed_grad + jnp.dot(value_grad, w_qkv[2], preferred_element_type=jnp.float32)
    unit_grad = normed_grad * ln_gain
    inner = unit_grad - jnp.mean(unit_grad, axis=1, keepdims=True)
    inner = inner - standard * jnp.mean(unit_grad * standard, axis=1, keepdims=True)
    return (masked_grad.astype(jnp.float32) + inv_std * inner).astype(jnp.bfloat16)


def project(normed, weight):
    return jnp.einsum("td,od->to", normed, weight, preferred_element_type=jnp.float32).astype(
        jnp.bfloat16
    )


def token_sum(left, right):
    return lax.dot_general(
        left, right, (((0,), (0,)), ((), ())), preferred_element_type=jnp.float32
    )


def attention_grads(queries, key_rows, value_rows, attn_grad, key_valid, score_scale):
    total, span = queries.shape
    heads_here = span // HEAD_DIM
    block = math.gcd(512, total)
    blocks = total // block
    key_three = key_rows.reshape(total, heads_here, HEAD_DIM)
    value_three = value_rows.reshape(total, heads_here, HEAD_DIM)
    query_four = queries.reshape(blocks, block, heads_here, HEAD_DIM)
    grad_four = attn_grad.reshape(blocks, block, heads_here, HEAD_DIM)

    def step(carry, item):
        key_acc, value_acc = carry
        query_block, grad_block = item
        scores = (
            jnp.einsum("qhd,khd->hqk", query_block, key_three, preferred_element_type=jnp.float32)
            * score_scale
        )
        scores = jnp.where(key_valid[None, None, :], scores, MASKED)
        peak = jnp.max(scores, axis=2, keepdims=True)
        expo = jnp.exp(scores - peak)
        probs = expo / jnp.sum(expo, axis=2, keepdims=True)
        probs_low = probs.astype(jnp.bfloat16)
        attended = jnp.einsum(
            "hqk,khd->qhd", probs_low, value_three, preferred_element_type=jnp.float32
        )
        delta = jnp.sum(grad_block.astype(jnp.float32) * attended, axis=2)
        prob_grad = jnp.einsum(
            "qhd,khd->hqk", grad_block, value_three, preferred_element_type=jnp.float32
        )
        score_grad = (probs * (prob_grad - jnp.transpose(delta)[:, :, None])).astype(jnp.bfloat16)
        query_grad = jnp.einsum(
            "hqk,khd->qhd", score_grad, key_three, preferred_element_type=jnp.float32
        )
        query_grad = (query_grad * score_scale).astype(jnp.bfloat16)
        key_acc = key_acc + jnp.einsum(
            "hqk,qhd->khd", score_grad, query_block, preferred_element_type=jnp.float32
        )
        value_acc = value_acc + jnp.einsum(
            "hqk,qhd->khd", probs_low, grad_block, preferred_element_type=jnp.float32
        )
        return ((key_acc, value_acc), (attended.astype(jnp.bfloat16), query_grad))

    zeros_acc = jnp.zeros((total, heads_here, HEAD_DIM), jnp.float32)
    sums, outputs = lax.scan(step, (zeros_acc, zeros_acc), (query_four, grad_four))
    attended = outputs[0].reshape(total, span)
    query_grad = outputs[1].reshape(total, span)
    key_grad = (sums[0] * score_scale).astype(jnp.bfloat16).reshape(total, span)
    value_grad = sums[1].astype(jnp.bfloat16).reshape(total, span)
    return (attended, query_grad, key_grad, value_grad)


def shards(tokens, positions, counts, ln_gain, w_qkv, w_out, d_out):
    inputs = tokens[0]
    places = positions[0]
    upstream = d_out[0]
    capacity, feature_width = inputs.shape
    shard_total = lax.axis_size("seq")
    shard_index = lax.axis_index("seq")
    slot_count = capacity * shard_total
    key_valid = jnp.arange(slot_count, dtype=jnp.int32) % capacity < jnp.repeat(counts[0], capacity)
    own_valid = lax.dynamic_slice_in_dim(key_valid, shard_index * capacity, capacity)
    normed, standard, inv_std = layer_norm(inputs, places, ln_gain)
    masked_grad = jnp.where(own_valid[:, None], upstream, jnp.zeros_like(upstream))
    score_scale = HEAD_DIM ** (-0.5)
    factor = 1.0 / math.sqrt(lax.axis_size("dp") * (3 * slot_count // 4))
    head_width = feature_width // shard_total
    normed_all, grad_all = (
        lax.all_gather(normed, "seq", axis=0, tiled=True),
        lax.all_gather(masked_grad, "seq", axis=0, tiled=True),
    )
    local_qkv = lax.dynamic_slice_in_dim(w_qkv, shard_index * head_width, head_width, 1)
    local_out = lax.dynamic_slice_in_dim(w_out, shard_index * head_width, head_width, 1)
    queries = project(normed_all, local_qkv[0])
    key_rows = project(normed_all, local_qkv[1])
    value_rows = project(normed_all, local_qkv[2])
    attn_grad = jnp.dot(grad_all, local_out, preferred_element_type=jnp.float32).astype(
        jnp.bfloat16
    )
    attended, query_grad, key_grad, value_grad = attention_grads(
        queries, key_rows, value_rows, attn_grad, key_valid, score_scale
    )
    term_qkv = jnp.stack(
        [
            token_sum(query_grad, normed_all),
            token_sum(key_grad, normed_all),
            token_sum(value_grad, normed_all),
        ]
    )
    term_out = token_sum(grad_all, attended)
    grad_qkv, grad_out = (
        lax.psum_scatter(term_qkv, "dp", scatter_dimension=2, tiled=True),
        lax.psum_scatter(term_out, "dp", scatter_dimension=0, tiled=True),
    )
    query_rows, key_back, value_back = (
        lax.all_to_all(query_grad, "seq", split_axis=0, concat_axis=1, tiled=True),
        lax.all_to_all(key_grad, "seq", split_axis=0, concat_axis=1, tiled=True),
        lax.all_to_all(value_grad, "seq", split_axis=0, concat_axis=1, tiled=True),
    )
    d_inputs = input_grad(
        query_rows, key_back, value_back, masked_grad, w_qkv, standard, inv_std, ln_gain
    )
    return (d_inputs[None], grad_qkv * factor, grad_out * factor)


FIRST_MOVES = (
    ((0, 0), (2, 0)),
    ((1, 0), (0, 0)),
    ((2, 0), (0, 1)),
    ((3, 0), (2, 1)),
    ((0, 1), (1, 0)),
    ((1, 1), (3, 1)),
    ((2, 1), (3, 0)),
    ((3, 1), (1, 1)),
)
SECOND_MOVES = (
    ((0, 1), (3, 0)),
    ((3, 0), (0, 1)),
    ((1, 0), (2, 1)),
    ((2, 1), (1, 0)),
    ((0, 0), (0, 0)),
    ((1, 1), (1, 1)),
    ((2, 0), (2, 0)),
    ((3, 1), (3, 1)),
)
HOME_MOVES = (
    ((0, 0), (0, 1)),
    ((1, 1), (1, 0)),
    ((1, 0), (0, 0)),
    ((0, 1), (1, 1)),
    ((2, 0), (2, 1)),
    ((3, 1), (3, 0)),
    ((3, 0), (2, 0)),
    ((2, 1), (3, 1)),
)
GUEST_MOVES = (
    ((1, 0), (0, 1)),
    ((0, 1), (1, 0)),
    ((3, 0), (2, 1)),
    ((2, 1), (3, 0)),
)


def column_pairs(moves, chips, seqs, back=False):
    pairs = []
    for chip in range(chips):
        for source, target in moves:
            if back:
                source, target = target, source
            pairs.append(
                ((chip * 2 + source[1]) * seqs + source[0], (chip * 2 + target[1]) * seqs + target[0])
            )
    return pairs


def block_table():
    table = [[0, 0] for _ in range(8)]
    for place, moves in enumerate((FIRST_MOVES, SECOND_MOVES)):
        for (source, _), (target, core) in moves:
            table[target * 2 + core][place] = source
    return table


def nt(left, right):
    return lax.dot_general(left, right, (((1,), (1,)), ((), ())), preferred_element_type=jnp.float32)


def nn(left, right):
    return lax.dot_general(left, right, (((1,), (0,)), ((), ())), preferred_element_type=jnp.float32)


def tn(left, right):
    return lax.dot_general(left, right, (((0,), (0,)), ((), ())), preferred_element_type=jnp.float32)


def seats():
    seat, dp = lax.axis_index("seq"), lax.axis_index("dp")
    core = dp & 1
    return (seat >> 1) * 2 + core, core, core ^ (seat & 1), dp >> 2, (dp >> 1) & 1


def gather_matrix(rank, rows):
    row = lax.broadcasted_iota(jnp.int32, (rows, rank.shape[1]), 0)
    return jnp.where(row == rank[...], 1.0, 0.0).astype(jnp.bfloat16)


def layer_norm_kernel(places, inputs, ln_gain, freqs, normed):
    rows, features = inputs.shape
    place = jnp.broadcast_to(places[...].astype(jnp.float32), (rows, rows)).T
    angle = jnp.concatenate([place] * (features // 2 // rows), axis=1) * freqs[...]
    shifted = inputs[...].astype(jnp.float32) + jnp.concatenate([jnp.sin(angle), jnp.cos(angle)], axis=1)
    centred = shifted - jnp.mean(shifted, axis=1, keepdims=True)
    inv_std = lax.rsqrt(jnp.mean(centred * centred, axis=1, keepdims=True) + EPSILON)
    normed[...] = (centred * inv_std * ln_gain[...]).astype(normed.dtype)


def slot_kernel(counts, other_counts, table, upstream, rank, own_rank, other_rank, masked):
    capacity = upstream.shape[0]
    half = own_rank.shape[1]
    seat = lax.axis_index("seq")
    _, core, guest, _, _ = seats()
    sizes = []
    for block in range(rank.shape[1] // capacity):
        holder = core if block < 2 else 1 - core
        source = table[(seat * 2 + holder) * 2 + block % 2]
        sizes.append(jnp.where(guest == 0, counts[source], other_counts[source]))
    slot = lax.broadcasted_iota(jnp.int32, rank.shape, 1)
    limit = jnp.zeros(rank.shape, jnp.int32)
    shift = jnp.zeros(rank.shape, jnp.int32)
    start = 0
    for block, size in enumerate(sizes):
        later = slot >= block * capacity
        limit = jnp.where(later, block * capacity + size, limit)
        shift = jnp.where(later, start - block * capacity, shift)
        start = start + size
    here = jnp.where(slot < limit, slot + shift, -1)
    rank[...] = here
    here = here[:, 0:half]
    own_rank[...] = here
    other_rank[...] = jnp.where(here >= 0, here + sizes[2] + sizes[3], -1)
    row = lax.broadcasted_iota(jnp.int32, (capacity, 1), 0)
    rows = upstream[...].astype(jnp.float32)
    masked[...] = jnp.where(row < counts[seat], rows, 0.0).astype(masked.dtype)


def lift_kernel(rank, g0, g1, g2, g3, weight_out, gathered, lifted, rows_g):
    capacity = g0.shape[0]
    matrix = gather_matrix(rank, gathered.shape[0])
    for block, source in enumerate((g0, g1, g2, g3)):
        rows_g[pl.ds(block * capacity, capacity), :] = source[...]
    gathered[...] = nn(matrix, rows_g[...]).astype(gathered.dtype)
    lifted[...] = nn(gathered[...], weight_out[...]).T.astype(lifted.dtype)


def weight_kernel(w_out, w_qkv, own_out, own_qkv, pair_qkv, sems):
    width = own_out.shape[1]
    head_group = seats()[0]
    group = pl.multiple_of(head_group * width, width)
    pair = pl.multiple_of((head_group >> 1) * 2 * width, 2 * width)
    copies = [pltpu.make_async_copy(w_out.at[:, pl.ds(group, width)], own_out, sems.at[3])]
    for part in range(3):
        copies.append(
            pltpu.make_async_copy(
                w_qkv.at[part, pl.ds(group, width), :],
                own_qkv.at[pl.ds(part * width, width), :],
                sems.at[part],
            )
        )
        copies.append(
            pltpu.make_async_copy(
                w_qkv.at[part, pl.ds(pair, 2 * width), :],
                pair_qkv.at[pl.ds(part * 2 * width, 2 * width), :],
                sems.at[4 + part],
            )
        )
    for copy in copies:
        copy.start()
    for copy in copies:
        copy.wait()


def main_kernel(
    rank, t0, t1, t2, t3, gathered_g, lifted, weight,
    x_send, x_keep, y_send, y_keep, grads,
    rows_t, gathered_t, query, key, value, stack,
):
    capacity = t0.shape[0]
    width = lifted.shape[0]
    lanes = width // 2
    low = jnp.bfloat16
    scale = HEAD_DIM ** (-0.5)

    _, core, guest, place_y, place_x = seats()
    matrix = gather_matrix(rank, gathered_t.shape[0])
    for block, source in enumerate((t0, t1, t2, t3)):
        rows_t[pl.ds(block * capacity, capacity), :] = source[...]
    gathered_t[...] = nn(matrix, rows_t[...]).astype(low)
    query[...] = (nt(weight[0:width, :], gathered_t[...]).astype(low) * scale).astype(low)
    key[...] = nt(weight[width : 2 * width, :], gathered_t[...]).astype(low)
    value[...] = nt(weight[2 * width : 3 * width, :], gathered_t[...]).astype(low)

    heads = []
    for head in range(width // HEAD_DIM):
        span = pl.ds(head * HEAD_DIM, HEAD_DIM)
        rows_h = query[span, :], key[span, :], value[span, :], lifted[span, :]
        heads.append(rows_h + (tn(rows_h[1], rows_h[0]), tn(rows_h[2], rows_h[3])))
    weighted = []
    for _, _, _, _, scores, _ in heads:
        expo = jnp.exp(scores - jnp.max(scores, axis=0, keepdims=True))
        probs = expo * (1.0 / jnp.sum(expo, axis=0, keepdims=True))
        weighted.append((probs, probs.astype(low)))
    for head, (query_h, key_h, value_h, lifted_h, _, prob_grad) in enumerate(heads):
        probs, probs_low = weighted[head]
        spans = [pl.ds(part * width + head * HEAD_DIM, HEAD_DIM) for part in range(4)]
        attended = nn(value_h, probs_low)
        delta = jnp.sum(lifted_h.astype(jnp.float32) * attended, axis=0, keepdims=True)
        score_grad = (probs * (prob_grad - delta)).astype(low)
        stack[spans[0], :] = (nn(key_h, score_grad) * scale).astype(low)
        stack[spans[1], :] = nt(query_h, score_grad).astype(low)
        stack[spans[2], :] = nt(lifted_h, probs_low).astype(low)
        stack[spans[3], :] = attended.astype(low)

    grads[...] = stack[0 : 3 * width, :]
    for slot_y, slot_x in ((0, 0), (1, 0), (0, 1), (1, 1)):
        block = (place_y ^ slot_y) * 2 + (place_x ^ slot_x)
        cols = pl.ds(pl.multiple_of(block * width, width), width)
        term_t = nn(stack[0 : 3 * width, :], gathered_t[:, cols])
        term_g = nn(stack[3 * width : 4 * width, :], gathered_g[:, cols]).T
        x_target = x_send if slot_x else x_keep
        y_target = y_send if slot_y else y_keep
        for side in range(2):
            across = slice(side * lanes, (side + 1) * lanes)
            spot = core ^ 1 ^ guest ^ side
            x_target[slot_y, spot, :, :] = term_t[0 : 2 * width, across].astype(x_target.dtype)
            y_target[slot_x, spot, 0:width, :] = term_t[2 * width : 3 * width, across].astype(y_target.dtype)
            for part in range(2):
                y_target[slot_x, spot, width + part * lanes : width + (part + 1) * lanes, :] = term_g[
                    across, part * lanes : (part + 1) * lanes
                ].astype(y_target.dtype)


def normed_kernel(own_rank, other_rank, own, other, weight, back_one, back_two):
    width = own.shape[0] // 3
    rows = own.shape[1]
    capacity = back_one.shape[0]
    core = seats()[1]
    half = 2 * capacity
    mine = gather_matrix(own_rank, rows)
    theirs = gather_matrix(other_rank, rows)
    own_grads = nn(own[...], mine).astype(own.dtype)
    other_grads = nn(other[...], theirs).astype(own.dtype)
    total = jnp.zeros((half, weight.shape[1]), jnp.float32)
    for part in range(3):
        span = slice(part * width, (part + 1) * width)
        for grads, spot in ((own_grads, core), (other_grads, 1 - core)):
            place = pl.ds(pl.multiple_of((part * 2 + spot) * width, width), width)
            total = total + tn(grads[span, :], weight[place, :])
    back_one[...] = total[0:capacity].astype(back_one.dtype)
    back_two[...] = total[capacity:half].astype(back_two.dtype)


def split_kernel(keep, first, _, home_send, guest_send, own):
    for slot in range(keep.shape[0]):
        home_send[slot] = (keep[slot, 0] + first[slot, 0].astype(keep.dtype)).astype(home_send.dtype)
        total = keep[slot, 1] + first[slot, 1].astype(keep.dtype)
        guest_send[slot] = total.astype(guest_send.dtype)
        own[slot] = total


def joined(from_home, from_guest, own, wide=jnp.float32):
    guest = seats()[2]
    return from_home.astype(wide) + jnp.where(guest == 0, own, from_guest.astype(wide))


def turn_kernel(from_home, from_guest, own, keep, send):
    keep[...] = joined(from_home[0], from_guest[0], own[0])
    send[...] = joined(from_home[1], from_guest[1], own[1]).astype(send.dtype)


def final_kernel(from_home, from_guest, own, keep, last, grad_qkv, grad_out, *, factor):
    half = own.shape[0]
    rows, lanes = grad_qkv.shape
    grad_qkv[0:half, :] = joined(from_home[...], from_guest[...], own[...]) * factor
    rest = (keep[...] + last[...].astype(keep.dtype)) * factor
    grad_qkv[half:rows, :] = rest[0 : rows - half]
    for part in range(2):
        low_row = rows - half + part * lanes
        grad_out[:, part * lanes : (part + 1) * lanes] = rest[low_row : low_row + lanes]


def specs(space, count):
    return [pl.BlockSpec(memory_space=space)] * count


VMEM_BYTES = 50 * 1024 * 1024
MAIN_BYTES = 28 * 1024 * 1024
FULL_BYTES = 60 * 1024 * 1024


def column_shards(tokens, positions, counts, ln_gain, w_qkv, w_out, d_out):
    low, wide = jnp.bfloat16, jnp.float32
    inputs = tokens[0]
    upstream = d_out[0]
    capacity, features = inputs.shape
    seqs = lax.axis_size("seq")
    chips = lax.axis_size("dp") // 2
    seat = lax.axis_index("seq")
    dp = lax.axis_index("dp")
    core = dp & 1
    total = seqs * capacity
    half = total // 2
    width = features // seqs
    lanes = width // 2
    factor = 1.0 / math.sqrt(lax.axis_size("dp") * (3 * total // 4))

    axes = ("dp", "seq")
    first = column_pairs(FIRST_MOVES, chips, seqs)
    second = column_pairs(SECOND_MOVES, chips, seqs)
    first_back = column_pairs(FIRST_MOVES, chips, seqs, True)
    home = column_pairs(HOME_MOVES, chips, seqs)
    guests = column_pairs(GUEST_MOVES, chips, seqs)

    def across(array, bit):
        return lax.ppermute(array, "dp", [(i, i ^ bit) for i in range(2 * chips)])

    def fetch(array):
        two = lax.ppermute(array, axes, second)
        return lax.ppermute(array, axes, first), two

    def share(pair):
        return pair + (across(pair[0], 1), across(pair[1], 1))

    params = pltpu.CompilerParams(vmem_limit_bytes=VMEM_BYTES)

    fetched_g = fetch(upstream)
    other_counts = across(counts[0], 1)
    steps = np.arange(features // 2, dtype=np.float32) * np.float32(-math.log(10000.0) / (features // 2))
    normed = pl.pallas_call(
        layer_norm_kernel,
        out_shape=jax.ShapeDtypeStruct((capacity, features), low),
        in_specs=specs(pltpu.VMEM, 4),
        out_specs=pl.BlockSpec(memory_space=pltpu.VMEM),
        compiler_params=pltpu.CompilerParams(vmem_limit_bytes=FULL_BYTES),
    )(positions, inputs, ln_gain[None], jnp.asarray(np.exp(steps)[None]))
    fetched_t = fetch(normed)
    own_out, own_qkv, pair_qkv = pl.pallas_call(
        weight_kernel,
        out_shape=(
            jax.ShapeDtypeStruct((features, width), low),
            jax.ShapeDtypeStruct((3 * width, features), low),
            jax.ShapeDtypeStruct((6 * width, features), low),
        ),
        in_specs=specs(pl.ANY, 2),
        out_specs=specs(pltpu.VMEM, 3),
        scratch_shapes=[pltpu.SemaphoreType.DMA((7,))],
        compiler_params=params,
        cost_estimate=pl.CostEstimate(flops=0, bytes_accessed=4 * 1024 * 1024, transcendentals=0),
    )(w_out, w_qkv)
    table = [block for pair in block_table() for block in pair]
    rank, own_rank, other_rank, masked_grad = pl.pallas_call(
        slot_kernel,
        out_shape=(
            jax.ShapeDtypeStruct((1, total), jnp.int32),
            jax.ShapeDtypeStruct((1, half), jnp.int32),
            jax.ShapeDtypeStruct((1, half), jnp.int32),
            jax.ShapeDtypeStruct((capacity, features), low),
        ),
        in_specs=specs(pltpu.SMEM, 3) + specs(pltpu.VMEM, 1),
        out_specs=specs(pltpu.VMEM, 4),
        compiler_params=pltpu.CompilerParams(vmem_limit_bytes=MAIN_BYTES),
    )(counts[0], other_counts, jnp.array(table, jnp.int32), upstream)

    fetched_g, rank, own_rank, other_rank, own_out, own_qkv, masked_grad = lax.optimization_barrier(
        (fetched_g, rank, own_rank, other_rank, own_out, own_qkv, masked_grad)
    )
    blocks_g = share(fetched_g)
    fetched_t, blocks_g = lax.optimization_barrier((fetched_t, blocks_g))
    rows = 3 * total // 4
    gathered_g, lifted = pl.pallas_call(
        lift_kernel,
        out_shape=(
            jax.ShapeDtypeStruct((rows, features), low),
            jax.ShapeDtypeStruct((width, rows), low),
        ),
        in_specs=specs(pltpu.VMEM, 6),
        out_specs=specs(pltpu.VMEM, 2),
        scratch_shapes=[pltpu.VMEM((total, features), low)],
        compiler_params=pltpu.CompilerParams(vmem_limit_bytes=MAIN_BYTES),
        cost_estimate=pl.CostEstimate(
            flops=2 * rows * features * (width + total), bytes_accessed=3 * 1024 * 1024, transcendentals=0
        ),
    )(rank, *blocks_g, own_out)
    blocks_t = share(fetched_t)

    send_shape = jax.ShapeDtypeStruct((2, 2, 2 * width, lanes), low)
    keep_shape = jax.ShapeDtypeStruct((2, 2, 2 * width, lanes), wide)
    grads_shape = jax.ShapeDtypeStruct((3 * width, rows), low)
    x_send, x_keep, y_send, y_keep, grads = pl.pallas_call(
        main_kernel,
        out_shape=(
            send_shape, keep_shape, send_shape, keep_shape, grads_shape
        ),
        in_specs=specs(pltpu.VMEM, 8),
        out_specs=specs(pltpu.VMEM, 5),
        scratch_shapes=[
            pltpu.VMEM((total, features), low),
            pltpu.VMEM((rows, features), low),
            pltpu.VMEM((width, rows), low),
            pltpu.VMEM((width, rows), low),
            pltpu.VMEM((width, rows), low),
            pltpu.VMEM((4 * width, rows), low),
        ],
        compiler_params=pltpu.CompilerParams(vmem_limit_bytes=MAIN_BYTES),
        cost_estimate=pl.CostEstimate(
            flops=2 * total * features * width * 7 + 12 * 4 * total * total * HEAD_DIM,
            bytes_accessed=8 * 1024 * 1024,
            transcendentals=4 * total * total,
        ),
    )(rank, *blocks_t, gathered_g, lifted, own_qkv)

    x_first, y_first = across(x_send, 2), across(y_send, 4)
    from_core = across(grads, 1)
    block_shape = jax.ShapeDtypeStruct((capacity, features), low)
    back_one, back_two = pl.pallas_call(
        normed_kernel,
        out_shape=(block_shape, block_shape),
        in_specs=specs(pltpu.VMEM, 5),
        out_specs=specs(pltpu.VMEM, 2),
        compiler_params=pltpu.CompilerParams(vmem_limit_bytes=MAIN_BYTES),
        cost_estimate=pl.CostEstimate(
            flops=2 * total * features * width * 3, bytes_accessed=4 * 1024 * 1024, transcendentals=0
        ),
    )(own_rank, other_rank, grads, from_core, pair_qkv)
    places, back_one = lax.optimization_barrier((positions, back_one))
    _, standard, inv_std = layer_norm(inputs, places[0], ln_gain)
    home_one = lax.ppermute(back_one, axes, first_back)
    token = across(back_one[:16], 1)
    x_first, y_first, token = lax.optimization_barrier((x_first, y_first, token))
    home_two = lax.ppermute(back_two, axes, second)
    x_second = across((x_keep[1] + x_first[1].astype(wide)).astype(low), 4)
    x_part = x_keep[0] + x_first[0].astype(wide)
    small = pltpu.CompilerParams(vmem_limit_bytes=12 * 1024 * 1024)
    part_shape = (2, 2 * width, lanes)

    def split(keep, first, token):
        return pl.pallas_call(
            split_kernel,
            out_shape=tuple(
                jax.ShapeDtypeStruct(keep.shape[:1] + keep.shape[2:], dtype) for dtype in (low, low, wide)
            ),
            in_specs=specs(pltpu.VMEM, 2) + specs(pl.ANY, 1),
            out_specs=specs(pltpu.VMEM, 3),
            compiler_params=small,
        )(keep, first, token)

    y_home, y_guest, y_own = split(y_keep, y_first, token)
    from_home = lax.ppermute(y_home, axes, home)
    from_guest = lax.ppermute(y_guest, axes, guests)
    y_part, y_send_last = pl.pallas_call(
        turn_kernel,
        out_shape=(
            jax.ShapeDtypeStruct(part_shape[1:], wide),
            jax.ShapeDtypeStruct(part_shape[1:], low),
        ),
        in_specs=specs(pltpu.VMEM, 3),
        out_specs=specs(pltpu.VMEM, 2),
        compiler_params=small,
    )(from_home, from_guest, y_own)
    y_last = across(y_send_last, 2)
    x_home, x_guest, x_own = split(x_part[None], x_second[None], token)
    grad_qkv, grad_out = pl.pallas_call(
        functools.partial(final_kernel, factor=factor),
        out_shape=(
            jax.ShapeDtypeStruct((3 * width, lanes), wide),
            jax.ShapeDtypeStruct((lanes, width), wide),
        ),
        in_specs=specs(pltpu.VMEM, 5),
        out_specs=specs(pltpu.VMEM, 2),
        compiler_params=small,
    )(
        lax.ppermute(x_home[0], axes, home),
        lax.ppermute(x_guest[0], axes, guests),
        x_own[0],
        y_part,
        y_last,
    )
    grad_qkv = grad_qkv.reshape(3, width, lanes)

    normed_grad = home_one.astype(wide) + home_two.astype(wide)
    unit_grad = normed_grad * ln_gain
    inner = unit_grad - jnp.mean(unit_grad, axis=1, keepdims=True)
    inner = inner - standard * jnp.mean(unit_grad * standard, axis=1, keepdims=True)
    d_inputs = (masked_grad.astype(wide) + inv_std * inner).astype(low)
    return (d_inputs[None], grad_qkv, grad_out)


def solution(mesh):
    fits = mesh.shape["dp"] == 8 and mesh.shape["seq"] == 4
    placed = (
        P("dp", "seq", None),
        P("dp", "seq"),
        P("dp", None),
        P(),
        P(),
        P(),
        P("dp", "seq", None),
    )
    return jax.shard_map(
        column_shards if fits else shards,
        mesh=mesh,
        in_specs=placed,
        out_specs=(P("dp", "seq", None), P(None, "seq", "dp"), P("dp", "seq")),
        check_vma=False,
    )
```

```python
import functools
import math

import jax
import jax.numpy as jnp
import numpy as np
from jax import lax
from jax.experimental import pallas as pl
from jax.experimental.pallas import tpu as pltpu
from jax.sharding import PartitionSpec as P

HEAD_DIM = 64


EPSILON = 1e-06
MASKED = -1e30


def position_code(places, feature_width):
    half = feature_width // 2
    freqs = jnp.exp(jnp.arange(half, dtype=jnp.float32) * (-math.log(10000.0) / half))
    angle = places.astype(jnp.float32)[:, None] * freqs[None, :]
    return jnp.concatenate([jnp.sin(angle), jnp.cos(angle)], axis=1)


def layer_norm(inputs, places, ln_gain):
    shifted = inputs.astype(jnp.float32) + position_code(places, inputs.shape[1])
    centred = shifted - jnp.mean(shifted, axis=1, keepdims=True)
    inv_std = lax.rsqrt(jnp.mean(centred * centred, axis=1, keepdims=True) + EPSILON)
    standard = centred * inv_std
    normed = (standard * ln_gain).astype(jnp.bfloat16)
    return (normed, standard, inv_std)


def input_grad(query_grad, key_grad, value_grad, masked_grad, w_qkv, standard, inv_std, ln_gain):
    normed_grad = jnp.dot(query_grad, w_qkv[0], preferred_element_type=jnp.float32)
    normed_grad = normed_grad + jnp.dot(key_grad, w_qkv[1], preferred_element_type=jnp.float32)
    normed_grad = normed_grad + jnp.dot(value_grad, w_qkv[2], preferred_element_type=jnp.float32)
    unit_grad = normed_grad * ln_gain
    inner = unit_grad - jnp.mean(unit_grad, axis=1, keepdims=True)
    inner = inner - standard * jnp.mean(unit_grad * standard, axis=1, keepdims=True)
    return (masked_grad.astype(jnp.float32) + inv_std * inner).astype(jnp.bfloat16)


def project(normed, weight):
    return jnp.einsum("td,od->to", normed, weight, preferred_element_type=jnp.float32).astype(
        jnp.bfloat16
    )


def token_sum(left, right):
    return lax.dot_general(
        left, right, (((0,), (0,)), ((), ())), preferred_element_type=jnp.float32
    )


def attention_grads(queries, key_rows, value_rows, attn_grad, key_valid, score_scale):
    total, span = queries.shape
    heads_here = span // HEAD_DIM
    block = math.gcd(512, total)
    blocks = total // block
    key_three = key_rows.reshape(total, heads_here, HEAD_DIM)
    value_three = value_rows.reshape(total, heads_here, HEAD_DIM)
    query_four = queries.reshape(blocks, block, heads_here, HEAD_DIM)
    grad_four = attn_grad.reshape(blocks, block, heads_here, HEAD_DIM)

    def step(carry, item):
        key_acc, value_acc = carry
        query_block, grad_block = item
        scores = (
            jnp.einsum("qhd,khd->hqk", query_block, key_three, preferred_element_type=jnp.float32)
            * score_scale
        )
        scores = jnp.where(key_valid[None, None, :], scores, MASKED)
        peak = jnp.max(scores, axis=2, keepdims=True)
        expo = jnp.exp(scores - peak)
        probs = expo / jnp.sum(expo, axis=2, keepdims=True)
        probs_low = probs.astype(jnp.bfloat16)
        attended = jnp.einsum(
            "hqk,khd->qhd", probs_low, value_three, preferred_element_type=jnp.float32
        )
        delta = jnp.sum(grad_block.astype(jnp.float32) * attended, axis=2)
        prob_grad = jnp.einsum(
            "qhd,khd->hqk", grad_block, value_three, preferred_element_type=jnp.float32
        )
        score_grad = (probs * (prob_grad - jnp.transpose(delta)[:, :, None])).astype(jnp.bfloat16)
        query_grad = jnp.einsum(
            "hqk,khd->qhd", score_grad, key_three, preferred_element_type=jnp.float32
        )
        query_grad = (query_grad * score_scale).astype(jnp.bfloat16)
        key_acc = key_acc + jnp.einsum(
            "hqk,qhd->khd", score_grad, query_block, preferred_element_type=jnp.float32
        )
        value_acc = value_acc + jnp.einsum(
            "hqk,qhd->khd", probs_low, grad_block, preferred_element_type=jnp.float32
        )
        return ((key_acc, value_acc), (attended.astype(jnp.bfloat16), query_grad))

    zeros_acc = jnp.zeros((total, heads_here, HEAD_DIM), jnp.float32)
    sums, outputs = lax.scan(step, (zeros_acc, zeros_acc), (query_four, grad_four))
    attended = outputs[0].reshape(total, span)
    query_grad = outputs[1].reshape(total, span)
    key_grad = (sums[0] * score_scale).astype(jnp.bfloat16).reshape(total, span)
    value_grad = sums[1].astype(jnp.bfloat16).reshape(total, span)
    return (attended, query_grad, key_grad, value_grad)


def shards(tokens, positions, counts, ln_gain, w_qkv, w_out, d_out):
    inputs = tokens[0]
    places = positions[0]
    upstream = d_out[0]
    capacity, feature_width = inputs.shape
    shard_total = lax.axis_size("seq")
    shard_index = lax.axis_index("seq")
    slot_count = capacity * shard_total
    key_valid = jnp.arange(slot_count, dtype=jnp.int32) % capacity < jnp.repeat(counts[0], capacity)
    own_valid = lax.dynamic_slice_in_dim(key_valid, shard_index * capacity, capacity)
    normed, standard, inv_std = layer_norm(inputs, places, ln_gain)
    masked_grad = jnp.where(own_valid[:, None], upstream, jnp.zeros_like(upstream))
    score_scale = HEAD_DIM ** (-0.5)
    factor = 1.0 / math.sqrt(lax.axis_size("dp") * (3 * slot_count // 4))
    head_width = feature_width // shard_total
    normed_all, grad_all = (
        lax.all_gather(normed, "seq", axis=0, tiled=True),
        lax.all_gather(masked_grad, "seq", axis=0, tiled=True),
    )
    local_qkv = lax.dynamic_slice_in_dim(w_qkv, shard_index * head_width, head_width, 1)
    local_out = lax.dynamic_slice_in_dim(w_out, shard_index * head_width, head_width, 1)
    queries = project(normed_all, local_qkv[0])
    key_rows = project(normed_all, local_qkv[1])
    value_rows = project(normed_all, local_qkv[2])
    attn_grad = jnp.dot(grad_all, local_out, preferred_element_type=jnp.float32).astype(
        jnp.bfloat16
    )
    attended, query_grad, key_grad, value_grad = attention_grads(
        queries, key_rows, value_rows, attn_grad, key_valid, score_scale
    )
    term_qkv = jnp.stack(
        [
            token_sum(query_grad, normed_all),
            token_sum(key_grad, normed_all),
            token_sum(value_grad, normed_all),
        ]
    )
    term_out = token_sum(grad_all, attended)
    grad_qkv, grad_out = (
        lax.psum_scatter(term_qkv, "dp", scatter_dimension=2, tiled=True),
        lax.psum_scatter(term_out, "dp", scatter_dimension=0, tiled=True),
    )
    query_rows, key_back, value_back = (
        lax.all_to_all(query_grad, "seq", split_axis=0, concat_axis=1, tiled=True),
        lax.all_to_all(key_grad, "seq", split_axis=0, concat_axis=1, tiled=True),
        lax.all_to_all(value_grad, "seq", split_axis=0, concat_axis=1, tiled=True),
    )
    d_inputs = input_grad(
        query_rows, key_back, value_back, masked_grad, w_qkv, standard, inv_std, ln_gain
    )
    return (d_inputs[None], grad_qkv * factor, grad_out * factor)


FIRST_MOVES = (
    ((0, 0), (2, 0)),
    ((1, 0), (0, 0)),
    ((2, 0), (0, 1)),
    ((3, 0), (2, 1)),
    ((0, 1), (1, 0)),
    ((1, 1), (3, 1)),
    ((2, 1), (3, 0)),
    ((3, 1), (1, 1)),
)
SECOND_MOVES = (
    ((0, 1), (3, 0)),
    ((3, 0), (0, 1)),
    ((1, 0), (2, 1)),
    ((2, 1), (1, 0)),
    ((0, 0), (0, 0)),
    ((1, 1), (1, 1)),
    ((2, 0), (2, 0)),
    ((3, 1), (3, 1)),
)
HOME_MOVES = (
    ((0, 0), (0, 1)),
    ((1, 1), (1, 0)),
    ((1, 0), (0, 0)),
    ((0, 1), (1, 1)),
    ((2, 0), (2, 1)),
    ((3, 1), (3, 0)),
    ((3, 0), (2, 0)),
    ((2, 1), (3, 1)),
)
GUEST_MOVES = (
    ((1, 0), (0, 1)),
    ((0, 1), (1, 0)),
    ((3, 0), (2, 1)),
    ((2, 1), (3, 0)),
)


def column_pairs(moves, chips, seqs, back=False):
    pairs = []
    for chip in range(chips):
        for source, target in moves:
            if back:
                source, target = target, source
            pairs.append(
                ((chip * 2 + source[1]) * seqs + source[0], (chip * 2 + target[1]) * seqs + target[0])
            )
    return pairs


def block_table():
    table = [[0, 0] for _ in range(8)]
    for place, moves in enumerate((FIRST_MOVES, SECOND_MOVES)):
        for (source, _), (target, core) in moves:
            table[target * 2 + core][place] = source
    return table


def nt(left, right):
    return lax.dot_general(left, right, (((1,), (1,)), ((), ())), preferred_element_type=jnp.float32)


def nn(left, right):
    return lax.dot_general(left, right, (((1,), (0,)), ((), ())), preferred_element_type=jnp.float32)


def tn(left, right):
    return lax.dot_general(left, right, (((0,), (0,)), ((), ())), preferred_element_type=jnp.float32)


def seats():
    seat, dp = lax.axis_index("seq"), lax.axis_index("dp")
    core = dp & 1
    return (seat >> 1) * 2 + core, core, core ^ (seat & 1), dp >> 2, (dp >> 1) & 1


def gather_matrix(rank, rows):
    row = lax.broadcasted_iota(jnp.int32, (rows, rank.shape[1]), 0)
    return jnp.where(row == rank[...], 1.0, 0.0).astype(jnp.bfloat16)


def layer_norm_kernel(places, inputs, ln_gain, freqs, normed):
    rows, features = inputs.shape
    place = jnp.broadcast_to(places[...].astype(jnp.float32), (rows, rows)).T
    angle = jnp.concatenate([place] * (features // 2 // rows), axis=1) * freqs[...]
    shifted = inputs[...].astype(jnp.float32) + jnp.concatenate([jnp.sin(angle), jnp.cos(angle)], axis=1)
    centred = shifted - jnp.mean(shifted, axis=1, keepdims=True)
    inv_std = lax.rsqrt(jnp.mean(centred * centred, axis=1, keepdims=True) + EPSILON)
    normed[...] = (centred * inv_std * ln_gain[...]).astype(normed.dtype)


def slot_kernel(counts, other_counts, table, upstream, rank, own_rank, other_rank, masked):
    capacity = upstream.shape[0]
    half = own_rank.shape[1]
    seat = lax.axis_index("seq")
    _, core, guest, _, _ = seats()
    sizes = []
    for block in range(rank.shape[1] // capacity):
        holder = core if block < 2 else 1 - core
        source = table[(seat * 2 + holder) * 2 + block % 2]
        sizes.append(jnp.where(guest == 0, counts[source], other_counts[source]))
    slot = lax.broadcasted_iota(jnp.int32, rank.shape, 1)
    limit = jnp.zeros(rank.shape, jnp.int32)
    shift = jnp.zeros(rank.shape, jnp.int32)
    start = 0
    for block, size in enumerate(sizes):
        later = slot >= block * capacity
        limit = jnp.where(later, block * capacity + size, limit)
        shift = jnp.where(later, start - block * capacity, shift)
        start = start + size
    here = jnp.where(slot < limit, slot + shift, -1)
    rank[...] = here
    here = here[:, 0:half]
    own_rank[...] = here
    other_rank[...] = jnp.where(here >= 0, here + sizes[2] + sizes[3], -1)
    row = lax.broadcasted_iota(jnp.int32, (capacity, 1), 0)
    rows = upstream[...].astype(jnp.float32)
    masked[...] = jnp.where(row < counts[seat], rows, 0.0).astype(masked.dtype)


def lift_kernel(rank, g0, g1, g2, g3, weight_out, gathered, lifted, rows_g):
    capacity = g0.shape[0]
    matrix = gather_matrix(rank, gathered.shape[0])
    for block, source in enumerate((g0, g1, g2, g3)):
        rows_g[pl.ds(block * capacity, capacity), :] = source[...]
    gathered[...] = nn(matrix, rows_g[...]).astype(gathered.dtype)
    lifted[...] = nn(gathered[...], weight_out[...]).T.astype(lifted.dtype)


def weight_kernel(w_out, w_qkv, own_out, own_qkv, pair_qkv, sems):
    width = own_out.shape[1]
    head_group = seats()[0]
    group = pl.multiple_of(head_group * width, width)
    pair = pl.multiple_of((head_group >> 1) * 2 * width, 2 * width)
    copies = [pltpu.make_async_copy(w_out.at[:, pl.ds(group, width)], own_out, sems.at[3])]
    for part in range(3):
        copies.append(
            pltpu.make_async_copy(
                w_qkv.at[part, pl.ds(group, width), :],
                own_qkv.at[pl.ds(part * width, width), :],
                sems.at[part],
            )
        )
        copies.append(
            pltpu.make_async_copy(
                w_qkv.at[part, pl.ds(pair, 2 * width), :],
                pair_qkv.at[pl.ds(part * 2 * width, 2 * width), :],
                sems.at[4 + part],
            )
        )
    for copy in copies:
        copy.start()
    for copy in copies:
        copy.wait()


def main_kernel(
    rank, t0, t1, t2, t3, gathered_g, lifted, weight,
    x_send, x_keep, y_send, y_keep, grads,
    rows_t, gathered_t, query, key, value, stack,
):
    capacity = t0.shape[0]
    width = lifted.shape[0]
    lanes = width // 2
    low = jnp.bfloat16
    scale = HEAD_DIM ** (-0.5)

    _, core, guest, place_y, place_x = seats()
    matrix = gather_matrix(rank, gathered_t.shape[0])
    for block, source in enumerate((t0, t1, t2, t3)):
        rows_t[pl.ds(block * capacity, capacity), :] = source[...]
    gathered_t[...] = nn(matrix, rows_t[...]).astype(low)
    query[...] = (nt(weight[0:width, :], gathered_t[...]).astype(low) * scale).astype(low)
    key[...] = nt(weight[width : 2 * width, :], gathered_t[...]).astype(low)
    value[...] = nt(weight[2 * width : 3 * width, :], gathered_t[...]).astype(low)

    heads = []
    for head in range(width // HEAD_DIM):
        span = pl.ds(head * HEAD_DIM, HEAD_DIM)
        rows_h = query[span, :], key[span, :], value[span, :], lifted[span, :]
        heads.append(rows_h + (tn(rows_h[1], rows_h[0]), tn(rows_h[2], rows_h[3])))
    weighted = []
    for _, _, _, _, scores, _ in heads:
        expo = jnp.exp(scores - jnp.max(scores, axis=0, keepdims=True))
        probs = expo * (1.0 / jnp.sum(expo, axis=0, keepdims=True))
        weighted.append((probs, probs.astype(low)))
    for head, (query_h, key_h, value_h, lifted_h, _, prob_grad) in enumerate(heads):
        probs, probs_low = weighted[head]
        spans = [pl.ds(part * width + head * HEAD_DIM, HEAD_DIM) for part in range(4)]
        attended = nn(value_h, probs_low)
        delta = jnp.sum(lifted_h.astype(jnp.float32) * attended, axis=0, keepdims=True)
        score_grad = (probs * (prob_grad - delta)).astype(low)
        stack[spans[0], :] = (nn(key_h, score_grad) * scale).astype(low)
        stack[spans[1], :] = nt(query_h, score_grad).astype(low)
        stack[spans[2], :] = nt(lifted_h, probs_low).astype(low)
        stack[spans[3], :] = attended.astype(low)

    grads[...] = stack[0 : 3 * width, :]
    for slot_y, slot_x in ((0, 0), (1, 0), (0, 1), (1, 1)):
        block = (place_y ^ slot_y) * 2 + (place_x ^ slot_x)
        cols = pl.ds(pl.multiple_of(block * width, width), width)
        term_t = nn(stack[0 : 3 * width, :], gathered_t[:, cols])
        term_g = nn(stack[3 * width : 4 * width, :], gathered_g[:, cols]).T
        x_target = x_send if slot_x else x_keep
        y_target = y_send if slot_y else y_keep
        for side in range(2):
            across = slice(side * lanes, (side + 1) * lanes)
            spot = core ^ 1 ^ guest ^ side
            x_target[slot_y, spot, :, :] = term_t[0 : 2 * width, across].astype(x_target.dtype)
            y_target[slot_x, spot, 0:width, :] = term_t[2 * width : 3 * width, across].astype(y_target.dtype)
            for part in range(2):
                y_target[slot_x, spot, width + part * lanes : width + (part + 1) * lanes, :] = term_g[
                    across, part * lanes : (part + 1) * lanes
                ].astype(y_target.dtype)


def normed_kernel(own_rank, other_rank, own, other, weight, back_one, back_two):
    width = own.shape[0] // 3
    rows = own.shape[1]
    capacity = back_one.shape[0]
    core = seats()[1]
    half = 2 * capacity
    mine = gather_matrix(own_rank, rows)
    theirs = gather_matrix(other_rank, rows)
    own_grads = nn(own[...], mine).astype(own.dtype)
    other_grads = nn(other[...], theirs).astype(own.dtype)
    total = jnp.zeros((half, weight.shape[1]), jnp.float32)
    for part in range(3):
        span = slice(part * width, (part + 1) * width)
        for grads, spot in ((own_grads, core), (other_grads, 1 - core)):
            place = pl.ds(pl.multiple_of((part * 2 + spot) * width, width), width)
            total = total + tn(grads[span, :], weight[place, :])
    back_one[...] = total[0:capacity].astype(back_one.dtype)
    back_two[...] = total[capacity:half].astype(back_two.dtype)


def split_kernel(keep, first, _, home_send, guest_send, own):
    for slot in range(keep.shape[0]):
        home_sum = keep[slot, 0].astype(own.dtype) + first[slot, 0].astype(own.dtype)
        home_send[slot] = home_sum.astype(home_send.dtype)
        total = keep[slot, 1].astype(own.dtype) + first[slot, 1].astype(own.dtype)
        guest_send[slot] = total.astype(guest_send.dtype)
        own[slot] = total


def joined(from_home, from_guest, own, wide=jnp.float32):
    guest = seats()[2]
    return from_home.astype(wide) + jnp.where(guest == 0, own, from_guest.astype(wide))


def turn_kernel(from_home, from_guest, own, keep, send):
    keep[...] = joined(from_home[0], from_guest[0], own[0])
    send[...] = joined(from_home[1], from_guest[1], own[1]).astype(send.dtype)


def final_kernel(from_home, from_guest, own, keep, last, grad_qkv, grad_out, *, factor):
    half = own.shape[0]
    rows, lanes = grad_qkv.shape
    grad_qkv[0:half, :] = joined(from_home[...], from_guest[...], own[...]) * factor
    rest = (keep[...] + last[...].astype(keep.dtype)) * factor
    grad_qkv[half:rows, :] = rest[0 : rows - half]
    for part in range(2):
        low_row = rows - half + part * lanes
        grad_out[:, part * lanes : (part + 1) * lanes] = rest[low_row : low_row + lanes]


def specs(space, count):
    return [pl.BlockSpec(memory_space=space)] * count


VMEM_BYTES = 50 * 1024 * 1024
MAIN_BYTES = 28 * 1024 * 1024
FULL_BYTES = 60 * 1024 * 1024


def column_shards(tokens, positions, counts, ln_gain, w_qkv, w_out, d_out):
    low, wide = jnp.bfloat16, jnp.float32
    inputs = tokens[0]
    upstream = d_out[0]
    capacity, features = inputs.shape
    seqs = lax.axis_size("seq")
    chips = lax.axis_size("dp") // 2
    seat = lax.axis_index("seq")
    dp = lax.axis_index("dp")
    core = dp & 1
    total = seqs * capacity
    half = total // 2
    width = features // seqs
    lanes = width // 2
    factor = 1.0 / math.sqrt(lax.axis_size("dp") * (3 * total // 4))

    axes = ("dp", "seq")
    first = column_pairs(FIRST_MOVES, chips, seqs)
    second = column_pairs(SECOND_MOVES, chips, seqs)
    first_back = column_pairs(FIRST_MOVES, chips, seqs, True)
    home = column_pairs(HOME_MOVES, chips, seqs)
    guests = column_pairs(GUEST_MOVES, chips, seqs)

    def across(array, bit):
        return lax.ppermute(array, "dp", [(i, i ^ bit) for i in range(2 * chips)])

    def fetch(array):
        two = lax.ppermute(array, axes, second)
        return lax.ppermute(array, axes, first), two

    def share(pair):
        return pair + (across(pair[0], 1), across(pair[1], 1))

    params = pltpu.CompilerParams(vmem_limit_bytes=VMEM_BYTES)

    fetched_g = fetch(upstream)
    other_counts = across(counts[0], 1)
    steps = np.arange(features // 2, dtype=np.float32) * np.float32(-math.log(10000.0) / (features // 2))
    normed = pl.pallas_call(
        layer_norm_kernel,
        out_shape=jax.ShapeDtypeStruct((capacity, features), low),
        in_specs=specs(pltpu.VMEM, 4),
        out_specs=pl.BlockSpec(memory_space=pltpu.VMEM),
        compiler_params=pltpu.CompilerParams(vmem_limit_bytes=FULL_BYTES),
    )(positions, inputs, ln_gain[None], jnp.asarray(np.exp(steps)[None]))
    fetched_t = fetch(normed)
    own_out, own_qkv, pair_qkv = pl.pallas_call(
        weight_kernel,
        out_shape=(
            jax.ShapeDtypeStruct((features, width), low),
            jax.ShapeDtypeStruct((3 * width, features), low),
            jax.ShapeDtypeStruct((6 * width, features), low),
        ),
        in_specs=specs(pl.ANY, 2),
        out_specs=specs(pltpu.VMEM, 3),
        scratch_shapes=[pltpu.SemaphoreType.DMA((7,))],
        compiler_params=params,
        cost_estimate=pl.CostEstimate(flops=0, bytes_accessed=4 * 1024 * 1024, transcendentals=0),
    )(w_out, w_qkv)
    table = [block for pair in block_table() for block in pair]
    rank, own_rank, other_rank, masked_grad = pl.pallas_call(
        slot_kernel,
        out_shape=(
            jax.ShapeDtypeStruct((1, total), jnp.int32),
            jax.ShapeDtypeStruct((1, half), jnp.int32),
            jax.ShapeDtypeStruct((1, half), jnp.int32),
            jax.ShapeDtypeStruct((capacity, features), low),
        ),
        in_specs=specs(pltpu.SMEM, 3) + specs(pltpu.VMEM, 1),
        out_specs=specs(pltpu.VMEM, 4),
        compiler_params=pltpu.CompilerParams(vmem_limit_bytes=MAIN_BYTES),
    )(counts[0], other_counts, jnp.array(table, jnp.int32), upstream)

    fetched_g, rank, own_rank, other_rank, own_out, own_qkv, masked_grad = lax.optimization_barrier(
        (fetched_g, rank, own_rank, other_rank, own_out, own_qkv, masked_grad)
    )
    blocks_g = share(fetched_g)
    fetched_t, blocks_g = lax.optimization_barrier((fetched_t, blocks_g))
    rows = 3 * total // 4
    gathered_g, lifted = pl.pallas_call(
        lift_kernel,
        out_shape=(
            jax.ShapeDtypeStruct((rows, features), low),
            jax.ShapeDtypeStruct((width, rows), low),
        ),
        in_specs=specs(pltpu.VMEM, 6),
        out_specs=specs(pltpu.VMEM, 2),
        scratch_shapes=[pltpu.VMEM((total, features), low)],
        compiler_params=pltpu.CompilerParams(vmem_limit_bytes=MAIN_BYTES),
        cost_estimate=pl.CostEstimate(
            flops=2 * rows * features * (width + total), bytes_accessed=3 * 1024 * 1024, transcendentals=0
        ),
    )(rank, *blocks_g, own_out)
    blocks_t = share(fetched_t)

    send_shape = jax.ShapeDtypeStruct((2, 2, 2 * width, lanes), low)
    keep_shape = send_shape
    grads_shape = jax.ShapeDtypeStruct((3 * width, rows), low)
    x_send, x_keep, y_send, y_keep, grads = pl.pallas_call(
        main_kernel,
        out_shape=(
            send_shape, keep_shape, send_shape, keep_shape, grads_shape
        ),
        in_specs=specs(pltpu.VMEM, 8),
        out_specs=specs(pltpu.VMEM, 5),
        scratch_shapes=[
            pltpu.VMEM((total, features), low),
            pltpu.VMEM((rows, features), low),
            pltpu.VMEM((width, rows), low),
            pltpu.VMEM((width, rows), low),
            pltpu.VMEM((width, rows), low),
            pltpu.VMEM((4 * width, rows), low),
        ],
        compiler_params=pltpu.CompilerParams(vmem_limit_bytes=MAIN_BYTES),
        cost_estimate=pl.CostEstimate(
            flops=2 * total * features * width * 7 + 12 * 4 * total * total * HEAD_DIM,
            bytes_accessed=8 * 1024 * 1024,
            transcendentals=4 * total * total,
        ),
    )(rank, *blocks_t, gathered_g, lifted, own_qkv)

    x_first, y_first = across(x_send, 2), across(y_send, 4)
    from_core = across(grads, 1)
    block_shape = jax.ShapeDtypeStruct((capacity, features), low)
    back_one, back_two = pl.pallas_call(
        normed_kernel,
        out_shape=(block_shape, block_shape),
        in_specs=specs(pltpu.VMEM, 5),
        out_specs=specs(pltpu.VMEM, 2),
        compiler_params=pltpu.CompilerParams(vmem_limit_bytes=MAIN_BYTES),
        cost_estimate=pl.CostEstimate(
            flops=2 * total * features * width * 3, bytes_accessed=4 * 1024 * 1024, transcendentals=0
        ),
    )(own_rank, other_rank, grads, from_core, pair_qkv)
    places, back_one = lax.optimization_barrier((positions, back_one))
    _, standard, inv_std = layer_norm(inputs, places[0], ln_gain)
    home_one = lax.ppermute(back_one, axes, first_back)
    token = across(back_one[:16], 1)
    x_first, y_first, token = lax.optimization_barrier((x_first, y_first, token))
    home_two = lax.ppermute(back_two, axes, second)
    x_second = across((x_keep[1].astype(wide) + x_first[1].astype(wide)).astype(low), 4)
    x_part = x_keep[0].astype(wide) + x_first[0].astype(wide)
    small = pltpu.CompilerParams(vmem_limit_bytes=12 * 1024 * 1024)
    part_shape = (2, 2 * width, lanes)

    def split(keep, first, token):
        return pl.pallas_call(
            split_kernel,
            out_shape=tuple(
                jax.ShapeDtypeStruct(keep.shape[:1] + keep.shape[2:], dtype) for dtype in (low, low, wide)
            ),
            in_specs=specs(pltpu.VMEM, 2) + specs(pl.ANY, 1),
            out_specs=specs(pltpu.VMEM, 3),
            compiler_params=small,
        )(keep, first, token)

    y_home, y_guest, y_own = split(y_keep, y_first, token)
    from_home = lax.ppermute(y_home, axes, home)
    from_guest = lax.ppermute(y_guest, axes, guests)
    y_part, y_send_last = pl.pallas_call(
        turn_kernel,
        out_shape=(
            jax.ShapeDtypeStruct(part_shape[1:], wide),
            jax.ShapeDtypeStruct(part_shape[1:], low),
        ),
        in_specs=specs(pltpu.VMEM, 3),
        out_specs=specs(pltpu.VMEM, 2),
        compiler_params=small,
    )(from_home, from_guest, y_own)
    y_last = across(y_send_last, 2)
    x_home, x_guest, x_own = split(x_part[None], x_second[None], token)
    grad_qkv, grad_out = pl.pallas_call(
        functools.partial(final_kernel, factor=factor),
        out_shape=(
            jax.ShapeDtypeStruct((3 * width, lanes), wide),
            jax.ShapeDtypeStruct((lanes, width), wide),
        ),
        in_specs=specs(pltpu.VMEM, 5),
        out_specs=specs(pltpu.VMEM, 2),
        compiler_params=small,
    )(
        lax.ppermute(x_home[0], axes, home),
        lax.ppermute(x_guest[0], axes, guests),
        x_own[0],
        y_part,
        y_last,
    )
    grad_qkv = grad_qkv.reshape(3, width, lanes)

    normed_grad = home_one.astype(wide) + home_two.astype(wide)
    unit_grad = normed_grad * ln_gain
    inner = unit_grad - jnp.mean(unit_grad, axis=1, keepdims=True)
    inner = inner - standard * jnp.mean(unit_grad * standard, axis=1, keepdims=True)
    d_inputs = (masked_grad.astype(wide) + inv_std * inner).astype(low)
    return (d_inputs[None], grad_qkv, grad_out)


def solution(mesh):
    fits = mesh.shape["dp"] == 8 and mesh.shape["seq"] == 4
    placed = (
        P("dp", "seq", None),
        P("dp", "seq"),
        P("dp", None),
        P(),
        P(),
        P(),
        P("dp", "seq", None),
    )
    return jax.shard_map(
        column_shards if fits else shards,
        mesh=mesh,
        in_specs=placed,
        out_specs=(P("dp", "seq", None), P(None, "seq", "dp"), P("dp", "seq")),
        check_vma=False,
    )
```

```python
import functools
import math

import jax
import jax.numpy as jnp
import numpy as np
from jax import lax
from jax.experimental import pallas as pl
from jax.experimental.pallas import tpu as pltpu
from jax.sharding import PartitionSpec as P

HEAD_DIM = 64


EPSILON = 1e-06
MASKED = -1e30


def position_code(places, feature_width):
    half = feature_width // 2
    freqs = jnp.exp(jnp.arange(half, dtype=jnp.float32) * (-math.log(10000.0) / half))
    angle = places.astype(jnp.float32)[:, None] * freqs[None, :]
    return jnp.concatenate([jnp.sin(angle), jnp.cos(angle)], axis=1)


def layer_norm(inputs, places, ln_gain):
    shifted = inputs.astype(jnp.float32) + position_code(places, inputs.shape[1])
    centred = shifted - jnp.mean(shifted, axis=1, keepdims=True)
    inv_std = lax.rsqrt(jnp.mean(centred * centred, axis=1, keepdims=True) + EPSILON)
    standard = centred * inv_std
    normed = (standard * ln_gain).astype(jnp.bfloat16)
    return (normed, standard, inv_std)


def input_grad(query_grad, key_grad, value_grad, masked_grad, w_qkv, standard, inv_std, ln_gain):
    normed_grad = jnp.dot(query_grad, w_qkv[0], preferred_element_type=jnp.float32)
    normed_grad = normed_grad + jnp.dot(key_grad, w_qkv[1], preferred_element_type=jnp.float32)
    normed_grad = normed_grad + jnp.dot(value_grad, w_qkv[2], preferred_element_type=jnp.float32)
    unit_grad = normed_grad * ln_gain
    inner = unit_grad - jnp.mean(unit_grad, axis=1, keepdims=True)
    inner = inner - standard * jnp.mean(unit_grad * standard, axis=1, keepdims=True)
    return (masked_grad.astype(jnp.float32) + inv_std * inner).astype(jnp.bfloat16)


def project(normed, weight):
    return jnp.einsum("td,od->to", normed, weight, preferred_element_type=jnp.float32).astype(
        jnp.bfloat16
    )


def token_sum(left, right):
    return lax.dot_general(
        left, right, (((0,), (0,)), ((), ())), preferred_element_type=jnp.float32
    )


def attention_grads(queries, key_rows, value_rows, attn_grad, key_valid, score_scale):
    total, span = queries.shape
    heads_here = span // HEAD_DIM
    block = math.gcd(512, total)
    blocks = total // block
    key_three = key_rows.reshape(total, heads_here, HEAD_DIM)
    value_three = value_rows.reshape(total, heads_here, HEAD_DIM)
    query_four = queries.reshape(blocks, block, heads_here, HEAD_DIM)
    grad_four = attn_grad.reshape(blocks, block, heads_here, HEAD_DIM)

    def step(carry, item):
        key_acc, value_acc = carry
        query_block, grad_block = item
        scores = (
            jnp.einsum("qhd,khd->hqk", query_block, key_three, preferred_element_type=jnp.float32)
            * score_scale
        )
        scores = jnp.where(key_valid[None, None, :], scores, MASKED)
        peak = jnp.max(scores, axis=2, keepdims=True)
        expo = jnp.exp(scores - peak)
        probs = expo / jnp.sum(expo, axis=2, keepdims=True)
        probs_low = probs.astype(jnp.bfloat16)
        attended = jnp.einsum(
            "hqk,khd->qhd", probs_low, value_three, preferred_element_type=jnp.float32
        )
        delta = jnp.sum(grad_block.astype(jnp.float32) * attended, axis=2)
        prob_grad = jnp.einsum(
            "qhd,khd->hqk", grad_block, value_three, preferred_element_type=jnp.float32
        )
        score_grad = (probs * (prob_grad - jnp.transpose(delta)[:, :, None])).astype(jnp.bfloat16)
        query_grad = jnp.einsum(
            "hqk,khd->qhd", score_grad, key_three, preferred_element_type=jnp.float32
        )
        query_grad = (query_grad * score_scale).astype(jnp.bfloat16)
        key_acc = key_acc + jnp.einsum(
            "hqk,qhd->khd", score_grad, query_block, preferred_element_type=jnp.float32
        )
        value_acc = value_acc + jnp.einsum(
            "hqk,qhd->khd", probs_low, grad_block, preferred_element_type=jnp.float32
        )
        return ((key_acc, value_acc), (attended.astype(jnp.bfloat16), query_grad))

    zeros_acc = jnp.zeros((total, heads_here, HEAD_DIM), jnp.float32)
    sums, outputs = lax.scan(step, (zeros_acc, zeros_acc), (query_four, grad_four))
    attended = outputs[0].reshape(total, span)
    query_grad = outputs[1].reshape(total, span)
    key_grad = (sums[0] * score_scale).astype(jnp.bfloat16).reshape(total, span)
    value_grad = sums[1].astype(jnp.bfloat16).reshape(total, span)
    return (attended, query_grad, key_grad, value_grad)


def shards(tokens, positions, counts, ln_gain, w_qkv, w_out, d_out):
    inputs = tokens[0]
    places = positions[0]
    upstream = d_out[0]
    capacity, feature_width = inputs.shape
    shard_total = lax.axis_size("seq")
    shard_index = lax.axis_index("seq")
    slot_count = capacity * shard_total
    key_valid = jnp.arange(slot_count, dtype=jnp.int32) % capacity < jnp.repeat(counts[0], capacity)
    own_valid = lax.dynamic_slice_in_dim(key_valid, shard_index * capacity, capacity)
    normed, standard, inv_std = layer_norm(inputs, places, ln_gain)
    masked_grad = jnp.where(own_valid[:, None], upstream, jnp.zeros_like(upstream))
    score_scale = HEAD_DIM ** (-0.5)
    factor = 1.0 / math.sqrt(lax.axis_size("dp") * (3 * slot_count // 4))
    head_width = feature_width // shard_total
    normed_all, grad_all = (
        lax.all_gather(normed, "seq", axis=0, tiled=True),
        lax.all_gather(masked_grad, "seq", axis=0, tiled=True),
    )
    local_qkv = lax.dynamic_slice_in_dim(w_qkv, shard_index * head_width, head_width, 1)
    local_out = lax.dynamic_slice_in_dim(w_out, shard_index * head_width, head_width, 1)
    queries = project(normed_all, local_qkv[0])
    key_rows = project(normed_all, local_qkv[1])
    value_rows = project(normed_all, local_qkv[2])
    attn_grad = jnp.dot(grad_all, local_out, preferred_element_type=jnp.float32).astype(
        jnp.bfloat16
    )
    attended, query_grad, key_grad, value_grad = attention_grads(
        queries, key_rows, value_rows, attn_grad, key_valid, score_scale
    )
    term_qkv = jnp.stack(
        [
            token_sum(query_grad, normed_all),
            token_sum(key_grad, normed_all),
            token_sum(value_grad, normed_all),
        ]
    )
    term_out = token_sum(grad_all, attended)
    grad_qkv, grad_out = (
        lax.psum_scatter(term_qkv, "dp", scatter_dimension=2, tiled=True),
        lax.psum_scatter(term_out, "dp", scatter_dimension=0, tiled=True),
    )
    query_rows, key_back, value_back = (
        lax.all_to_all(query_grad, "seq", split_axis=0, concat_axis=1, tiled=True),
        lax.all_to_all(key_grad, "seq", split_axis=0, concat_axis=1, tiled=True),
        lax.all_to_all(value_grad, "seq", split_axis=0, concat_axis=1, tiled=True),
    )
    d_inputs = input_grad(
        query_rows, key_back, value_back, masked_grad, w_qkv, standard, inv_std, ln_gain
    )
    return (d_inputs[None], grad_qkv * factor, grad_out * factor)


FIRST_MOVES = (
    ((0, 0), (2, 0)),
    ((1, 0), (0, 0)),
    ((2, 0), (0, 1)),
    ((3, 0), (2, 1)),
    ((0, 1), (1, 0)),
    ((1, 1), (3, 1)),
    ((2, 1), (3, 0)),
    ((3, 1), (1, 1)),
)
SECOND_MOVES = (
    ((0, 1), (3, 0)),
    ((3, 0), (0, 1)),
    ((1, 0), (2, 1)),
    ((2, 1), (1, 0)),
    ((0, 0), (0, 0)),
    ((1, 1), (1, 1)),
    ((2, 0), (2, 0)),
    ((3, 1), (3, 1)),
)
HOME_MOVES = (
    ((0, 0), (0, 1)),
    ((1, 1), (1, 0)),
    ((1, 0), (0, 0)),
    ((0, 1), (1, 1)),
    ((2, 0), (2, 1)),
    ((3, 1), (3, 0)),
    ((3, 0), (2, 0)),
    ((2, 1), (3, 1)),
)
GUEST_MOVES = (
    ((1, 0), (0, 1)),
    ((0, 1), (1, 0)),
    ((3, 0), (2, 1)),
    ((2, 1), (3, 0)),
)


def column_pairs(moves, chips, seqs, back=False):
    pairs = []
    for chip in range(chips):
        for source, target in moves:
            if back:
                source, target = target, source
            pairs.append(
                ((chip * 2 + source[1]) * seqs + source[0], (chip * 2 + target[1]) * seqs + target[0])
            )
    return pairs


def block_table():
    table = [[0, 0] for _ in range(8)]
    for place, moves in enumerate((FIRST_MOVES, SECOND_MOVES)):
        for (source, _), (target, core) in moves:
            table[target * 2 + core][place] = source
    return table


def nt(left, right):
    return lax.dot_general(left, right, (((1,), (1,)), ((), ())), preferred_element_type=jnp.float32)


def nn(left, right):
    return lax.dot_general(left, right, (((1,), (0,)), ((), ())), preferred_element_type=jnp.float32)


def tn(left, right):
    return lax.dot_general(left, right, (((0,), (0,)), ((), ())), preferred_element_type=jnp.float32)


def seats():
    seat, dp = lax.axis_index("seq"), lax.axis_index("dp")
    core = dp & 1
    return (seat >> 1) * 2 + core, core, core ^ (seat & 1), dp >> 2, (dp >> 1) & 1


def gather_matrix(rank, rows):
    row = lax.broadcasted_iota(jnp.int32, (rows, rank.shape[1]), 0)
    return jnp.where(row == rank[...], 1.0, 0.0).astype(jnp.bfloat16)


def layer_norm_kernel(places, inputs, ln_gain, freqs, normed):
    rows, features = inputs.shape
    place = jnp.broadcast_to(places[...].astype(jnp.float32), (rows, rows)).T
    angle = jnp.concatenate([place] * (features // 2 // rows), axis=1) * freqs[...]
    shifted = inputs[...].astype(jnp.float32) + jnp.concatenate([jnp.sin(angle), jnp.cos(angle)], axis=1)
    centred = shifted - jnp.mean(shifted, axis=1, keepdims=True)
    inv_std = lax.rsqrt(jnp.mean(centred * centred, axis=1, keepdims=True) + EPSILON)
    normed[...] = (centred * inv_std * ln_gain[...]).astype(normed.dtype)


def slot_kernel(counts, other_counts, table, upstream, rank, own_rank, other_rank, masked):
    capacity = upstream.shape[0]
    half = own_rank.shape[1]
    seat = lax.axis_index("seq")
    _, core, guest, _, _ = seats()
    sizes = []
    for block in range(rank.shape[1] // capacity):
        holder = core if block < 2 else 1 - core
        source = table[(seat * 2 + holder) * 2 + block % 2]
        sizes.append(jnp.where(guest == 0, counts[source], other_counts[source]))
    slot = lax.broadcasted_iota(jnp.int32, rank.shape, 1)
    limit = jnp.zeros(rank.shape, jnp.int32)
    shift = jnp.zeros(rank.shape, jnp.int32)
    start = 0
    for block, size in enumerate(sizes):
        later = slot >= block * capacity
        limit = jnp.where(later, block * capacity + size, limit)
        shift = jnp.where(later, start - block * capacity, shift)
        start = start + size
    here = jnp.where(slot < limit, slot + shift, -1)
    rank[...] = here
    here = here[:, 0:half]
    own_rank[...] = here
    other_rank[...] = jnp.where(here >= 0, here + sizes[2] + sizes[3], -1)
    row = lax.broadcasted_iota(jnp.int32, (capacity, 1), 0)
    rows = upstream[...].astype(jnp.float32)
    masked[...] = jnp.where(row < counts[seat], rows, 0.0).astype(masked.dtype)


def lift_kernel(rank, g0, g1, g2, g3, weight_out, gathered, lifted, rows_g):
    capacity = g0.shape[0]
    matrix = gather_matrix(rank, gathered.shape[0])
    for block, source in enumerate((g0, g1, g2, g3)):
        rows_g[pl.ds(block * capacity, capacity), :] = source[...]
    gathered[...] = nn(matrix, rows_g[...]).astype(gathered.dtype)
    lifted[...] = nn(gathered[...], weight_out[...]).T.astype(lifted.dtype)


def weight_kernel(w_out, w_qkv, own_out, own_qkv, pair_qkv, sems):
    width = own_out.shape[1]
    head_group = seats()[0]
    group = pl.multiple_of(head_group * width, width)
    pair = pl.multiple_of((head_group >> 1) * 2 * width, 2 * width)
    copies = [pltpu.make_async_copy(w_out.at[:, pl.ds(group, width)], own_out, sems.at[3])]
    for part in range(3):
        copies.append(
            pltpu.make_async_copy(
                w_qkv.at[part, pl.ds(group, width), :],
                own_qkv.at[pl.ds(part * width, width), :],
                sems.at[part],
            )
        )
        copies.append(
            pltpu.make_async_copy(
                w_qkv.at[part, pl.ds(pair, 2 * width), :],
                pair_qkv.at[pl.ds(part * 2 * width, 2 * width), :],
                sems.at[4 + part],
            )
        )
    for copy in copies:
        copy.start()
    for copy in copies:
        copy.wait()


def main_kernel(
    rank, t0, t1, t2, t3, gathered_g, lifted, weight,
    x_send, x_keep, y_send, y_keep, grads,
    rows_t, gathered_t, query, key, value, stack,
):
    capacity = t0.shape[0]
    width = lifted.shape[0]
    lanes = width // 2
    low = jnp.bfloat16
    scale = HEAD_DIM ** (-0.5)

    _, core, guest, place_y, place_x = seats()
    matrix = gather_matrix(rank, gathered_t.shape[0])
    for block, source in enumerate((t0, t1, t2, t3)):
        rows_t[pl.ds(block * capacity, capacity), :] = source[...]
    gathered_t[...] = nn(matrix, rows_t[...]).astype(low)
    query[...] = (nt(weight[0:width, :], gathered_t[...]).astype(low) * scale).astype(low)
    key[...] = nt(weight[width : 2 * width, :], gathered_t[...]).astype(low)
    value[...] = nt(weight[2 * width : 3 * width, :], gathered_t[...]).astype(low)

    heads = []
    for head in range(width // HEAD_DIM):
        span = pl.ds(head * HEAD_DIM, HEAD_DIM)
        rows_h = query[span, :], key[span, :], value[span, :], lifted[span, :]
        heads.append(rows_h + (tn(rows_h[1], rows_h[0]),))
    weighted = []
    for _, _, value_h, lifted_h, scores in heads:
        expo = jnp.exp(scores - jnp.max(scores, axis=0, keepdims=True))
        probs = expo * (1.0 / jnp.sum(expo, axis=0, keepdims=True))
        weighted.append((probs, probs.astype(low), tn(value_h, lifted_h)))
    for head, (query_h, key_h, value_h, lifted_h, _) in enumerate(heads):
        probs, probs_low, prob_grad = weighted[head]
        spans = [pl.ds(part * width + head * HEAD_DIM, HEAD_DIM) for part in range(4)]
        attended = nn(value_h, probs_low)
        delta = jnp.sum(lifted_h.astype(jnp.float32) * attended, axis=0, keepdims=True)
        score_grad = (probs * (prob_grad - delta)).astype(low)
        stack[spans[0], :] = (nn(key_h, score_grad) * scale).astype(low)
        stack[spans[1], :] = nt(query_h, score_grad).astype(low)
        stack[spans[2], :] = nt(lifted_h, probs_low).astype(low)
        stack[spans[3], :] = attended.astype(low)

    grads[...] = stack[0 : 3 * width, :]
    for slot_y, slot_x in ((0, 0), (1, 0), (0, 1), (1, 1)):
        block = (place_y ^ slot_y) * 2 + (place_x ^ slot_x)
        cols = pl.ds(pl.multiple_of(block * width, width), width)
        term_t = nn(stack[0 : 3 * width, :], gathered_t[:, cols])
        term_g = nn(stack[3 * width : 4 * width, :], gathered_g[:, cols]).T
        x_target = x_send if slot_x else x_keep
        y_target = y_send if slot_y else y_keep
        for side in range(2):
            across = slice(side * lanes, (side + 1) * lanes)
            spot = core ^ 1 ^ guest ^ side
            x_target[slot_y, spot, :, :] = term_t[0 : 2 * width, across].astype(x_target.dtype)
            y_target[slot_x, spot, 0:width, :] = term_t[2 * width : 3 * width, across].astype(y_target.dtype)
            for part in range(2):
                y_target[slot_x, spot, width + part * lanes : width + (part + 1) * lanes, :] = term_g[
                    across, part * lanes : (part + 1) * lanes
                ].astype(y_target.dtype)


def normed_kernel(own_rank, other_rank, own, other, weight, back_one, back_two):
    width = own.shape[0] // 3
    rows = own.shape[1]
    capacity = back_one.shape[0]
    core = seats()[1]
    half = 2 * capacity
    mine = gather_matrix(own_rank, rows)
    theirs = gather_matrix(other_rank, rows)
    own_grads = nn(own[...], mine).astype(own.dtype)
    other_grads = nn(other[...], theirs).astype(own.dtype)
    total = jnp.zeros((half, weight.shape[1]), jnp.float32)
    for part in range(3):
        span = slice(part * width, (part + 1) * width)
        for grads, spot in ((own_grads, core), (other_grads, 1 - core)):
            place = pl.ds(pl.multiple_of((part * 2 + spot) * width, width), width)
            total = total + tn(grads[span, :], weight[place, :])
    back_one[...] = total[0:capacity].astype(back_one.dtype)
    back_two[...] = total[capacity:half].astype(back_two.dtype)


def split_kernel(keep, first, _, home_send, guest_send, own):
    for slot in range(keep.shape[0]):
        home_send[slot] = (keep[slot, 0] + first[slot, 0].astype(keep.dtype)).astype(home_send.dtype)
        total = keep[slot, 1] + first[slot, 1].astype(keep.dtype)
        guest_send[slot] = total.astype(guest_send.dtype)
        own[slot] = total


def joined(from_home, from_guest, own, wide=jnp.float32):
    guest = seats()[2]
    return from_home.astype(wide) + jnp.where(guest == 0, own, from_guest.astype(wide))


def turn_kernel(from_home, from_guest, own, keep, send):
    keep[...] = joined(from_home[0], from_guest[0], own[0])
    send[...] = joined(from_home[1], from_guest[1], own[1]).astype(send.dtype)


def final_kernel(from_home, from_guest, own, keep, last, grad_qkv, grad_out, *, factor):
    half = own.shape[0]
    rows, lanes = grad_qkv.shape
    grad_qkv[0:half, :] = joined(from_home[...], from_guest[...], own[...]) * factor
    rest = (keep[...] + last[...].astype(keep.dtype)) * factor
    grad_qkv[half:rows, :] = rest[0 : rows - half]
    for part in range(2):
        low_row = rows - half + part * lanes
        grad_out[:, part * lanes : (part + 1) * lanes] = rest[low_row : low_row + lanes]


def specs(space, count):
    return [pl.BlockSpec(memory_space=space)] * count


VMEM_BYTES = 50 * 1024 * 1024
MAIN_BYTES = 28 * 1024 * 1024
FULL_BYTES = 60 * 1024 * 1024


def column_shards(tokens, positions, counts, ln_gain, w_qkv, w_out, d_out):
    low, wide = jnp.bfloat16, jnp.float32
    inputs = tokens[0]
    upstream = d_out[0]
    capacity, features = inputs.shape
    seqs = lax.axis_size("seq")
    chips = lax.axis_size("dp") // 2
    seat = lax.axis_index("seq")
    dp = lax.axis_index("dp")
    core = dp & 1
    total = seqs * capacity
    half = total // 2
    width = features // seqs
    lanes = width // 2
    factor = 1.0 / math.sqrt(lax.axis_size("dp") * (3 * total // 4))

    axes = ("dp", "seq")
    first = column_pairs(FIRST_MOVES, chips, seqs)
    second = column_pairs(SECOND_MOVES, chips, seqs)
    first_back = column_pairs(FIRST_MOVES, chips, seqs, True)
    home = column_pairs(HOME_MOVES, chips, seqs)
    guests = column_pairs(GUEST_MOVES, chips, seqs)

    def across(array, bit):
        return lax.ppermute(array, "dp", [(i, i ^ bit) for i in range(2 * chips)])

    def fetch(array):
        two = lax.ppermute(array, axes, second)
        return lax.ppermute(array, axes, first), two

    def share(pair):
        return pair + (across(pair[0], 1), across(pair[1], 1))

    params = pltpu.CompilerParams(vmem_limit_bytes=VMEM_BYTES)

    fetched_g = fetch(upstream)
    other_counts = across(counts[0], 1)
    steps = np.arange(features // 2, dtype=np.float32) * np.float32(-math.log(10000.0) / (features // 2))
    normed = pl.pallas_call(
        layer_norm_kernel,
        out_shape=jax.ShapeDtypeStruct((capacity, features), low),
        in_specs=specs(pltpu.VMEM, 4),
        out_specs=pl.BlockSpec(memory_space=pltpu.VMEM),
        compiler_params=pltpu.CompilerParams(vmem_limit_bytes=FULL_BYTES),
    )(positions, inputs, ln_gain[None], jnp.asarray(np.exp(steps)[None]))
    fetched_t = fetch(normed)
    own_out, own_qkv, pair_qkv = pl.pallas_call(
        weight_kernel,
        out_shape=(
            jax.ShapeDtypeStruct((features, width), low),
            jax.ShapeDtypeStruct((3 * width, features), low),
            jax.ShapeDtypeStruct((6 * width, features), low),
        ),
        in_specs=specs(pl.ANY, 2),
        out_specs=specs(pltpu.VMEM, 3),
        scratch_shapes=[pltpu.SemaphoreType.DMA((7,))],
        compiler_params=params,
        cost_estimate=pl.CostEstimate(flops=0, bytes_accessed=4 * 1024 * 1024, transcendentals=0),
    )(w_out, w_qkv)
    table = [block for pair in block_table() for block in pair]
    rank, own_rank, other_rank, masked_grad = pl.pallas_call(
        slot_kernel,
        out_shape=(
            jax.ShapeDtypeStruct((1, total), jnp.int32),
            jax.ShapeDtypeStruct((1, half), jnp.int32),
            jax.ShapeDtypeStruct((1, half), jnp.int32),
            jax.ShapeDtypeStruct((capacity, features), low),
        ),
        in_specs=specs(pltpu.SMEM, 3) + specs(pltpu.VMEM, 1),
        out_specs=specs(pltpu.VMEM, 4),
        compiler_params=pltpu.CompilerParams(vmem_limit_bytes=MAIN_BYTES),
    )(counts[0], other_counts, jnp.array(table, jnp.int32), upstream)

    fetched_g, rank, own_rank, other_rank, own_out, own_qkv, masked_grad = lax.optimization_barrier(
        (fetched_g, rank, own_rank, other_rank, own_out, own_qkv, masked_grad)
    )
    blocks_g = share(fetched_g)
    fetched_t, blocks_g = lax.optimization_barrier((fetched_t, blocks_g))
    rows = 3 * total // 4
    gathered_g, lifted = pl.pallas_call(
        lift_kernel,
        out_shape=(
            jax.ShapeDtypeStruct((rows, features), low),
            jax.ShapeDtypeStruct((width, rows), low),
        ),
        in_specs=specs(pltpu.VMEM, 6),
        out_specs=specs(pltpu.VMEM, 2),
        scratch_shapes=[pltpu.VMEM((total, features), low)],
        compiler_params=pltpu.CompilerParams(vmem_limit_bytes=MAIN_BYTES),
        cost_estimate=pl.CostEstimate(
            flops=2 * rows * features * (width + total), bytes_accessed=3 * 1024 * 1024, transcendentals=0
        ),
    )(rank, *blocks_g, own_out)
    blocks_t = share(fetched_t)

    send_shape = jax.ShapeDtypeStruct((2, 2, 2 * width, lanes), low)
    keep_shape = jax.ShapeDtypeStruct((2, 2, 2 * width, lanes), wide)
    grads_shape = jax.ShapeDtypeStruct((3 * width, rows), low)
    x_send, x_keep, y_send, y_keep, grads = pl.pallas_call(
        main_kernel,
        out_shape=(
            send_shape, keep_shape, send_shape, keep_shape, grads_shape
        ),
        in_specs=specs(pltpu.VMEM, 8),
        out_specs=specs(pltpu.VMEM, 5),
        scratch_shapes=[
            pltpu.VMEM((total, features), low),
            pltpu.VMEM((rows, features), low),
            pltpu.VMEM((width, rows), low),
            pltpu.VMEM((width, rows), low),
            pltpu.VMEM((width, rows), low),
            pltpu.VMEM((4 * width, rows), low),
        ],
        compiler_params=pltpu.CompilerParams(vmem_limit_bytes=MAIN_BYTES),
        cost_estimate=pl.CostEstimate(
            flops=2 * total * features * width * 7 + 12 * 4 * total * total * HEAD_DIM,
            bytes_accessed=8 * 1024 * 1024,
            transcendentals=4 * total * total,
        ),
    )(rank, *blocks_t, gathered_g, lifted, own_qkv)

    x_first, y_first = across(x_send, 2), across(y_send, 4)
    from_core = across(grads, 1)
    block_shape = jax.ShapeDtypeStruct((capacity, features), low)
    back_one, back_two = pl.pallas_call(
        normed_kernel,
        out_shape=(block_shape, block_shape),
        in_specs=specs(pltpu.VMEM, 5),
        out_specs=specs(pltpu.VMEM, 2),
        compiler_params=pltpu.CompilerParams(vmem_limit_bytes=MAIN_BYTES),
        cost_estimate=pl.CostEstimate(
            flops=2 * total * features * width * 3, bytes_accessed=4 * 1024 * 1024, transcendentals=0
        ),
    )(own_rank, other_rank, grads, from_core, pair_qkv)
    places, back_one = lax.optimization_barrier((positions, back_one))
    _, standard, inv_std = layer_norm(inputs, places[0], ln_gain)
    home_one = lax.ppermute(back_one, axes, first_back)
    token = across(back_one[:16], 1)
    x_first, y_first, token = lax.optimization_barrier((x_first, y_first, token))
    home_two = lax.ppermute(back_two, axes, second)
    x_second = across((x_keep[1] + x_first[1].astype(wide)).astype(low), 4)
    x_part = x_keep[0] + x_first[0].astype(wide)
    small = pltpu.CompilerParams(vmem_limit_bytes=12 * 1024 * 1024)
    part_shape = (2, 2 * width, lanes)

    def split(keep, first, token):
        return pl.pallas_call(
            split_kernel,
            out_shape=tuple(
                jax.ShapeDtypeStruct(keep.shape[:1] + keep.shape[2:], dtype) for dtype in (low, low, wide)
            ),
            in_specs=specs(pltpu.VMEM, 2) + specs(pl.ANY, 1),
            out_specs=specs(pltpu.VMEM, 3),
            compiler_params=small,
        )(keep, first, token)

    y_home, y_guest, y_own = split(y_keep, y_first, token)
    from_home = lax.ppermute(y_home, axes, home)
    from_guest = lax.ppermute(y_guest, axes, guests)
    y_part, y_send_last = pl.pallas_call(
        turn_kernel,
        out_shape=(
            jax.ShapeDtypeStruct(part_shape[1:], wide),
            jax.ShapeDtypeStruct(part_shape[1:], low),
        ),
        in_specs=specs(pltpu.VMEM, 3),
        out_specs=specs(pltpu.VMEM, 2),
        compiler_params=small,
    )(from_home, from_guest, y_own)
    y_last = across(y_send_last, 2)
    x_home, x_guest, x_own = split(x_part[None], x_second[None], token)
    grad_qkv, grad_out = pl.pallas_call(
        functools.partial(final_kernel, factor=factor),
        out_shape=(
            jax.ShapeDtypeStruct((3 * width, lanes), wide),
            jax.ShapeDtypeStruct((lanes, width), wide),
        ),
        in_specs=specs(pltpu.VMEM, 5),
        out_specs=specs(pltpu.VMEM, 2),
        compiler_params=small,
    )(
        lax.ppermute(x_home[0], axes, home),
        lax.ppermute(x_guest[0], axes, guests),
        x_own[0],
        y_part,
        y_last,
    )
    grad_qkv = grad_qkv.reshape(3, width, lanes)

    normed_grad = home_one.astype(wide) + home_two.astype(wide)
    unit_grad = normed_grad * ln_gain
    inner = unit_grad - jnp.mean(unit_grad, axis=1, keepdims=True)
    inner = inner - standard * jnp.mean(unit_grad * standard, axis=1, keepdims=True)
    d_inputs = (masked_grad.astype(wide) + inv_std * inner).astype(low)
    return (d_inputs[None], grad_qkv, grad_out)


def solution(mesh):
    fits = mesh.shape["dp"] == 8 and mesh.shape["seq"] == 4
    placed = (
        P("dp", "seq", None),
        P("dp", "seq"),
        P("dp", None),
        P(),
        P(),
        P(),
        P("dp", "seq", None),
    )
    return jax.shard_map(
        column_shards if fits else shards,
        mesh=mesh,
        in_specs=placed,
        out_specs=(P("dp", "seq", None), P(None, "seq", "dp"), P("dp", "seq")),
        check_vma=False,
    )
```
